32 devices in a mesh: dp: 8 (over y, x, core), mp: 4 (over z).
Axes of the slice: x: 2, y: 2, z: 4, core: 2. Of those that a mesh axis runs over, the one named last changes fastest.
Arguments:
- tokens: bfloat16 [24576, 768], P(('dp', 'mp'))
- out_cotangent: bfloat16 [24576, 768], P(('dp', 'mp')), may hold values from -6 to 6
- lengths: int32 [24], P('dp'), may hold values from 256 to 1024, as said below
- starts: int32 [24], P('dp'), may hold values from 0 to 1023, as said below
- ends: int32 [24], P('dp'), may hold values from 0 to 1023, as said below
- flags: int32 [24], P('dp'), may hold values 0 or 1
- qkv_master: float32 [3, 768, 768], P(None, 'dp', 'mp')
- proj_master: float32 [768, 768], P('mp', 'dp')
- up_master: float32 [768, 3072], P('dp', 'mp')
- down_master: float32 [3072, 768], P('mp', 'dp')
- vectors: float32 [12, 768], replicated
- qkv_first: float32 [3, 768, 768], P(None, 'dp', 'mp'), may hold values from -0.00024414062 to 0.00024414062
- proj_first: float32 [768, 768], P('mp', 'dp'), may hold values from -0.00024414062 to 0.00024414062
- up_first: float32 [768, 3072], P('dp', 'mp'), may hold values from -0.00024414062 to 0.00024414062
- down_first: float32 [3072, 768], P('mp', 'dp'), may hold values from -0.00024414062 to 0.00024414062
- qkv_second: float32 [3, 768, 768], P(None, 'dp', 'mp'), may hold values from 1.4128508e-10 to 5.651403e-10
- proj_second: float32 [768, 768], P('mp', 'dp'), may hold values from 1.4128508e-10 to 5.651403e-10
- up_second: float32 [768, 3072], P('dp', 'mp'), may hold values from 1.4128508e-10 to 5.651403e-10
- down_second: float32 [3072, 768], P('mp', 'dp'), may hold values from 1.4128508e-10 to 5.651403e-10
- vector_first: float32 [12, 768], P(None, ('dp', 'mp')), may hold values from -0.0008544922 to 0.0008544922
- vector_second: float32 [12, 768], P(None, ('dp', 'mp')), may hold values from 1.4128508e-09 to 5.6514033e-09
Outputs:
- block_out: bfloat16 [24576, 768], P(('dp', 'mp'))
- input_grad: float32 [24576, 768], P(('dp', 'mp'))
- grad_norm: float32 [], replicated
- qkv_grad: float32 [3, 768, 768], P(None, 'dp', 'mp')
- qkv_first_new: float32 [3, 768, 768], P(None, 'dp', 'mp')
- qkv_second_new: float32 [3, 768, 768], P(None, 'dp', 'mp')
- qkv_new: float32 [3, 768, 768], P(None, 'dp', 'mp')
- proj_grad: float32 [768, 768], P('mp', 'dp')
- proj_first_new: float32 [768, 768], P('mp', 'dp')
- proj_second_new: float32 [768, 768], P('mp', 'dp')
- proj_new: float32 [768, 768], P('mp', 'dp')
- up_grad: float32 [768, 3072], P('dp', 'mp')
- up_first_new: float32 [768, 3072], P('dp', 'mp')
- up_second_new: float32 [768, 3072], P('dp', 'mp')
- up_new: float32 [768, 3072], P('dp', 'mp')
- down_grad: float32 [3072, 768], P('mp', 'dp')
- down_first_new: float32 [3072, 768], P('mp', 'dp')
- down_second_new: float32 [3072, 768], P('mp', 'dp')
- down_new: float32 [3072, 768], P('mp', 'dp')
- vector_grad: float32 [12, 768], P(None, ('dp', 'mp'))
- vector_first_new: float32 [12, 768], P(None, ('dp', 'mp'))
- vector_second_new: float32 [12, 768], P(None, ('dp', 'mp'))
- vector_new: float32 [12, 768], P(None, ('dp', 'mp'))
The draws below stay inside these ranges and needn't reach their ends.
Inputs may be any that keep to these rules, and one draw needn't show every extreme that they name: `lengths`: each length is at least 256; in every aligned block of 3 sequences one sequence is longer than 768; one sequence of all has length exactly 1024, and its start and end are both 1024 - 1. Each start lies below its sequence's length; the sequence of length exactly 1024 starts at 1023. Each end is at least its start, fewer than 32 positions after it, and below its sequence's length; the sequence of length exactly 1024 ends at 1023.
All inputs are finite; a program needn't handle non-finite values. No bound on the sum of `flags` on one device may be relied on, other than what follows from the above.
Results may differ from the reference program's by a relative error of at most 0.025.
Values may be sent and summed in bfloat16 or wider, within the bound.
No kernel may reach another device: no remote copies, remote signals or barrier semaphores. Data moves between devices by JAX's collectives and lax.ppermute only.
A program may use at most 192 MiB of HBM per device.

```python
import math
import jax
import jax.numpy as jnp
from jax import lax

D = 768
HEADS = 12
HDIM = 64
FF = 3072
LEN = 1024
SEQ_DEV = 3
STEP = 10
SEQS = 24
TOKENS = 24576
NVEC = 12


def ramp(count, lowest, ratio):
    along = jnp.arange(count, dtype=jnp.float32) / max(count - 1, 1)
    return lowest * ratio ** along


def sequence_spans(key):
    lower = max(LEN // 4, 1)
    upper_low = LEN - LEN // 4 + 1
    drawn = jax.random.randint(key, (SEQS,), lower, LEN + 1)
    long_draw = jax.random.randint(jax.random.fold_in(key, 14), (SEQS,), upper_low, LEN + 1)
    chosen = jax.random.randint(jax.random.fold_in(key, 11), (SEQS // SEQ_DEV, 1), 0, SEQ_DEV)
    picked = (jnp.arange(SEQ_DEV, dtype=jnp.int32)[None, :] == chosen).reshape(SEQS)
    full_index = jax.random.randint(jax.random.fold_in(key, 15), (), 0, SEQS)
    is_full = jnp.arange(SEQS, dtype=jnp.int32) == full_index
    seq_lengths = jnp.where(picked, long_draw, drawn)
    seq_lengths = jnp.where(is_full, LEN, seq_lengths).astype(jnp.int32)
    offset_draw = jax.random.randint(jax.random.fold_in(key, 12), (SEQS,), 0, 1 << 20)
    start_pos = offset_draw % seq_lengths
    reach = jnp.minimum(32, seq_lengths - start_pos)
    span_draw = jax.random.randint(jax.random.fold_in(key, 13), (SEQS,), 0, 1 << 20)
    end_pos = start_pos + span_draw % reach
    start_pos = jnp.where(is_full, LEN - 1, start_pos)
    end_pos = jnp.where(is_full, LEN - 1, end_pos)
    return (seq_lengths, start_pos.astype(jnp.int32), end_pos.astype(jnp.int32))


def draw_lengths(key, part):
    shared = sequence_spans(key)
    return shared[0]


def draw_starts(key, part):
    shared = sequence_spans(key)
    return shared[1]


def draw_ends(key, part):
    shared = sequence_spans(key)
    return shared[2]


def draw_tokens(key, part):
    key = jax.random.fold_in(key, 4)
    noise = jax.random.normal(key, (TOKENS, D), jnp.float32)
    rising = ramp(D, 0.6, 3.0)
    return (noise * rising[None, :]).astype(jnp.bfloat16)


def draw_qkv_master(key, part):
    key = jax.random.fold_in(key, 5)
    noise = jax.random.normal(key, (3, D, D), jnp.float32)
    rising = ramp(D, 0.7, 1.9)
    return noise * rising[None, None, :] * D ** (-0.5)


def draw_proj_master(key, part):
    key = jax.random.fold_in(key, 6)
    noise = jax.random.normal(key, (D, D), jnp.float32)
    rising = ramp(D, 0.7, 1.9)
    return noise * rising[:, None] * 4.0 * D ** (-0.5)


def draw_up_master(key, part):
    key = jax.random.fold_in(key, 7)
    noise = jax.random.normal(key, (D, FF), jnp.float32)
    rising = ramp(FF, 0.7, 1.9)
    return noise * rising[None, :] * D ** (-0.5)


def draw_down_master(key, part):
    key = jax.random.fold_in(key, 8)
    noise = jax.random.normal(key, (FF, D), jnp.float32)
    rising = ramp(FF, 0.7, 1.9)
    return noise * rising[:, None] * FF ** (-0.5)


def draw_vectors(key, part):
    key = jax.random.fold_in(key, 9)
    noise = jax.random.normal(key, (NVEC, D), jnp.float32)
    rising = ramp(D, 0.6, 3.0)
    gain_rows = rising[None, :] * (1.0 + 0.1 * noise)
    row_ids = jnp.arange(NVEC, dtype=jnp.int32)
    is_gain = (row_ids == 3) | (row_ids == 6)
    return jnp.where(is_gain[:, None], gain_rows, 0.2 * noise)


def plant(values, own_key, smallest, high):
    longest = values.shape.index(max(values.shape))
    spots = []
    for shift in (0, 1):
        where = [jax.random.randint(jax.random.fold_in(own_key, axis), (), 0, length) for axis, length in enumerate(values.shape)]
        where[longest] = (where[longest] + shift) % values.shape[longest]
        spots.append(tuple(where))
    return values.at[spots[0]].set(smallest).at[spots[1]].set(high)


def steps_of(stream_key, dims, shards, smallest, top_value):
    gain, own = 1.0, jax.random.fold_in(stream_key, 6)
    for position, shards_of in shards:
        heights = jnp.exp(jax.random.uniform(jax.random.fold_in(own, position), (shards_of,), jnp.float32, smallest / len(shards), top_value / len(shards)))
        gain = gain * jnp.repeat(heights, dims[position] // shards_of).reshape([-1 if axis == position else 1 for axis in range(len(dims))])
    return gain


def centred(own_key, dims, scale, most, pieces=(), kind=jnp.bfloat16):
    values = scale * jax.random.normal(own_key, dims, jnp.float32)
    if pieces:
        values = values * steps_of(own_key, dims, pieces, -0.22, 0.18)
    return jnp.clip(values, -most, most).astype(kind)


def setup_inputs(seed: int = 0) -> dict:
    keys = jax.random.split(jax.random.key(seed), 22)
    return {
        "tokens": draw_tokens(jax.random.fold_in(keys[21], 71), 0),
        "out_cotangent": centred(keys[1], (TOKENS, D), 1.0, 6.0, ((0, 32),)),
        "lengths": draw_lengths(jax.random.fold_in(keys[21], 71), 0),
        "starts": draw_starts(jax.random.fold_in(keys[21], 71), 0),
        "ends": draw_ends(jax.random.fold_in(keys[21], 71), 0),
        "flags": plant((jax.random.randint(keys[5], (SEQS,), 0, 3) < 1).astype(jnp.int32), jax.random.fold_in(keys[5], 1), 0, 1),
        "qkv_master": draw_qkv_master(jax.random.fold_in(keys[21], 71), 0),
        "proj_master": draw_proj_master(jax.random.fold_in(keys[21], 71), 0),
        "up_master": draw_up_master(jax.random.fold_in(keys[21], 71), 0),
        "down_master": draw_down_master(jax.random.fold_in(keys[21], 71), 0),
        "vectors": draw_vectors(jax.random.fold_in(keys[21], 71), 0),
        "qkv_first": centred(keys[11], (3, D, D), (0.11 / (4 * D * D + 2 * D * FF) ** 0.5), 0.00024414062, ((1, 8), (2, 4)), jnp.float32),
        "proj_first": centred(keys[12], (D, D), (0.11 / (4 * D * D + 2 * D * FF) ** 0.5), 0.00024414062, ((0, 4), (1, 8)), jnp.float32),
        "up_first": centred(keys[13], (D, FF), (0.11 / (4 * D * D + 2 * D * FF) ** 0.5), 0.00024414062, ((0, 8), (1, 4)), jnp.float32),
        "down_first": centred(keys[14], (FF, D), (0.11 / (4 * D * D + 2 * D * FF) ** 0.5), 0.00024414062, ((0, 4), (1, 8)), jnp.float32),
        "qkv_second": jnp.clip(jnp.exp(math.log(5.65140323427471e-10) - 1.3862944 * jax.random.uniform(keys[15], (3, D, D), jnp.float32) ** steps_of(keys[15], (3, D, D), ((1, 8), (2, 4)), -0.2, 0.2)), 1.4128508085686775e-10, 5.65140323427471e-10),
        "proj_second": jnp.clip(jnp.exp(math.log(5.65140323427471e-10) - 1.3862944 * jax.random.uniform(keys[16], (D, D), jnp.float32) ** steps_of(keys[16], (D, D), ((0, 4), (1, 8)), -0.2, 0.2)), 1.4128508085686775e-10, 5.65140323427471e-10),
        "up_second": jnp.clip(jnp.exp(math.log(5.65140323427471e-10) - 1.3862944 * jax.random.uniform(keys[17], (D, FF), jnp.float32) ** steps_of(keys[17], (D, FF), ((0, 8), (1, 4)), -0.2, 0.2)), 1.4128508085686775e-10, 5.65140323427471e-10),
        "down_second": jnp.clip(jnp.exp(math.log(5.65140323427471e-10) - 1.3862944 * jax.random.uniform(keys[18], (FF, D), jnp.float32) ** steps_of(keys[18], (FF, D), ((0, 4), (1, 8)), -0.2, 0.2)), 1.4128508085686775e-10, 5.65140323427471e-10),
        "vector_first": centred(keys[19], (NVEC, D), (0.35 / (4 * D * D + 2 * D * FF) ** 0.5), 0.0008544922, ((1, 32),), jnp.float32),
        "vector_second": jnp.clip(jnp.exp(math.log(5.6514033452970125e-09) - 1.3862944 * jax.random.uniform(keys[20], (NVEC, D), jnp.float32) ** steps_of(keys[20], (NVEC, D), ((1, 32),), -0.2, 0.2)), 1.4128508363242531e-09, 5.6514033452970125e-09),
    }


LN_EPS = 1e-06
BETA_ONE = 0.9
BETA_TWO = 0.999
ADAM_EPS = 1e-08
WEIGHT_DECAY = 0.01
CLIP_NORM = 1.0
VECTOR_RATE = 1.0
MATRIX_RATE = 2.0
NEG_FILL = -1e+30
HIGHEST = lax.Precision.HIGHEST

@jax.custom_vjp
def low(v):
    return lax.optimization_barrier(v.astype(jnp.bfloat16)).astype(jnp.float32)

@jax.custom_vjp
def low_back(v):
    return v

def low_keep(v):
    return (low(v), None)

def low_pass(kept, grad):
    return (grad,)

def back_keep(v):
    return (v, None)

def back_low(kept, grad):
    return (low(grad),)
low.defvjp(low_keep, low_pass)
low_back.defvjp(back_keep, back_low)

def layer_norm(summed, gain_row, offset_row):
    average = lax.optimization_barrier(jnp.mean(summed, -1, keepdims=True))
    centered = summed - average
    variance = lax.optimization_barrier(jnp.mean(centered * centered, -1, keepdims=True))
    return centered * lax.rsqrt(variance + LN_EPS) * gain_row + offset_row

def matmul(left, right):
    return jnp.dot(left, right, precision=HIGHEST, preferred_element_type=jnp.float32)

def attend_sequence(operands):
    queries, keys_seq, values_seq, key_valid = operands
    raw = low_back(jnp.einsum('qhd,khd->hqk', queries, keys_seq, precision=HIGHEST))
    scores = jnp.where(key_valid[None, None, :], raw * HDIM ** (-0.5), NEG_FILL)
    probs = jax.nn.softmax(scores, axis=-1)
    return jnp.einsum('hqk,khd->qhd', low(probs), values_seq, precision=HIGHEST)

def forward(inputs, weights, key_valid):
    qkv_master, proj_master, up_master, down_master, vectors = weights
    group_rows = inputs.shape[0]
    seq_count = group_rows // LEN
    w_query = low(qkv_master[0])
    w_key = low(qkv_master[1])
    w_value = low(qkv_master[2])
    w_proj = low(proj_master)
    w_up = low(up_master)
    w_down = low(down_master)
    bias_up = vectors[8:].reshape(FF)
    queries = low_back(low(matmul(inputs, w_query) + vectors[0]))
    keys_all = low_back(low(matmul(inputs, w_key)))
    values_all = low_back(low(matmul(inputs, w_value) + vectors[1]))
    shaped = (seq_count, LEN, HEADS, HDIM)
    attended = lax.map(jax.checkpoint(attend_sequence), (queries.reshape(shaped), keys_all.reshape(shaped), values_all.reshape(shaped), key_valid))
    mixed = low_back(low(attended.reshape(group_rows, D)))
    branch = low_back(matmul(mixed, w_proj))
    first_sum = inputs + branch + vectors[2]
    normed = layer_norm(first_sum, vectors[3], vectors[4])
    pre_act = low_back(matmul(low(normed), w_up) + bias_up)
    activated = low(jax.nn.gelu(pre_act, approximate=False))
    feed = low_back(matmul(activated, w_down))
    second_sum = normed + feed + vectors[5]
    return layer_norm(second_sum, vectors[6], vectors[7])

def row_weights(lengths, starts, ends, flags):
    positions = jnp.arange(TOKENS, dtype=jnp.int32)
    seq_of = positions // LEN
    within = positions % LEN
    valid = (within < lengths[seq_of]).astype(jnp.float32)
    flag_row = flags[seq_of].astype(jnp.float32)
    answer = (within == starts[seq_of]).astype(jnp.float32) + (within == ends[seq_of]).astype(jnp.float32)
    opening = (within == 0).astype(jnp.float32)
    return valid * (1.0 + 2.0 * (1.0 - flag_row) * answer + 4.0 * flag_row * opening)

def adamw(weight, grad, first, second, rate, decay, clip_factor):
    clipped = grad * clip_factor
    first_new = BETA_ONE * first + (1.0 - BETA_ONE) * clipped
    second_new = BETA_TWO * second + (1.0 - BETA_TWO) * clipped * clipped
    first_hat = first_new / (1.0 - BETA_ONE ** STEP)
    second_hat = second_new / (1.0 - BETA_TWO ** STEP)
    updated = weight * (1.0 - rate * decay) - rate * first_hat / (jnp.sqrt(second_hat) + ADAM_EPS)
    return (clipped, first_new, second_new, updated)

def reference(tokens, out_cotangent, lengths, starts, ends, flags, qkv_master, proj_master, up_master, down_master, vectors, qkv_first, proj_first, up_first, down_first, qkv_second, proj_second, up_second, down_second, vector_first, vector_second):
    group_rows = SEQ_DEV * LEN
    group_count = TOKENS // group_rows
    cotangent = out_cotangent.astype(jnp.float32) * row_weights(lengths, starts, ends, flags)[:, None]
    weights_all = (qkv_master, proj_master, up_master, down_master, vectors)

    def one_group(totals, items):
        inputs, cot_rows, group_lengths = items
        key_valid = jnp.arange(LEN, dtype=jnp.int32)[None, :] < group_lengths[:, None]

        def layer_fn(layer_in, layer_weights):
            return forward(layer_in, layer_weights, key_valid)
        outputs, backward = jax.vjp(layer_fn, inputs, weights_all)
        grad_in, weight_grads = backward(cot_rows)
        totals = jax.tree.map(jnp.add, totals, weight_grads)
        return (totals, (outputs.astype(jnp.bfloat16), grad_in))
    start_totals = jax.tree.map(jnp.zeros_like, weights_all)
    totals, (outs_grouped, grads_grouped) = lax.scan(one_group, start_totals, (tokens.astype(jnp.float32).reshape(group_count, group_rows, D), cotangent.reshape(group_count, group_rows, D), lengths.reshape(group_count, SEQ_DEV)))
    block_out = outs_grouped.reshape(TOKENS, D)
    input_grad = grads_grouped.reshape(TOKENS, D)
    squares = jnp.zeros((), jnp.float32)
    for leaf in totals:
        squares = squares + jnp.sum(leaf * leaf)
    grad_norm = jnp.sqrt(squares)
    clip_factor = jnp.minimum(1.0, CLIP_NORM / (grad_norm + 1e-06))
    matrix_rate = MATRIX_RATE / math.sqrt(D)
    qkv_set = adamw(qkv_master, totals[0], qkv_first, qkv_second, matrix_rate, WEIGHT_DECAY, clip_factor)
    proj_set = adamw(proj_master, totals[1], proj_first, proj_second, matrix_rate, WEIGHT_DECAY, clip_factor)
    up_set = adamw(up_master, totals[2], up_first, up_second, matrix_rate, WEIGHT_DECAY, clip_factor)
    down_set = adamw(down_master, totals[3], down_first, down_second, matrix_rate, WEIGHT_DECAY, clip_factor)
    vector_set = adamw(vectors, totals[4], vector_first, vector_second, VECTOR_RATE, 0.0, clip_factor)
    return (block_out, input_grad, grad_norm, qkv_set[0], qkv_set[1], qkv_set[2], qkv_set[3], proj_set[0], proj_set[1], proj_set[2], proj_set[3], up_set[0], up_set[1], up_set[2], up_set[3], down_set[0], down_set[1], down_set[2], down_set[3], vector_set[0], vector_set[1], vector_set[2], vector_set[3])
```

```python
from functools import partial
import math

import jax
import jax.numpy as jnp
import numpy as np
from jax import lax
from jax.experimental import pallas as pl
from jax.experimental.pallas import tpu as pltpu
from jax.sharding import PartitionSpec as P

D = 768
HEADS = 12
HDIM = 64
FF = 3072
LEN = 1024
STEP = 10

LN_EPS = 1e-06
BETA_ONE = 0.9
BETA_TWO = 0.999
ADAM_EPS = 1e-08
WEIGHT_DECAY = 0.01
CLIP_NORM = 1.0
VECTOR_RATE = 1.0
MATRIX_RATE = 2.0
NEG_FILL = -1e30

BF = jnp.bfloat16
F32 = jnp.float32
AXES = ("dp", "mp")
BLK = 256
ROWS = 768
PAIRS = HEADS // 2
RB = 8
RP = D // RB
VMEM_LIMIT = 60 * 1024 * 1024

KEY_BLOCKS = np.array(
    [
        [[0, 1, 2, 3]] * 3,
        [[3, 4, 5, 0], [1, 2, 6, 7], [1, 2, 6, 7]],
        [[6, 7, 0, 1], [6, 7, 0, 1], [2, 3, 4, 5]],
        [[5, 0, 1, 2]] * 3,
    ],
    np.int32,
)
BLOCK_SEQ = np.array(
    [[0, 0, 0, 0, 0, 0, 0, 0], [0, 1, 1, 0, 0, 0, 1, 1], [1, 1, 2, 2, 2, 2, 1, 1], [2, 2, 2, 2, 2, 2, 2, 2]], np.int32
)
BLOCK_PLACE = np.array(
    [[0, 1, 2, 3, 4, 4, 4, 4], [3, 0, 1, 0, 1, 2, 2, 3], [2, 3, 0, 1, 2, 3, 0, 1], [1, 2, 3, 4, 4, 0, 4, 4]], np.int32
)


def dot_nn(left, right):
    return jnp.dot(left, right, preferred_element_type=F32)


def dot_nt(left, right):
    return lax.dot_general(left, right, (((1,), (1,)), ((), ())), preferred_element_type=F32)


def lane_ids(rows):
    return lax.broadcasted_iota(jnp.int32, (rows, 128), 1)


def assemble(core, same_ref, other_ref, part, target, col):
    width = same_ref.shape[-1]
    for pos in range(RB // 2):
        same = same_ref[pos, part]
        other = other_ref[pos, part]
        first = jnp.where(core == 0, same, other)
        second = jnp.where(core == 0, other, same)
        target[2 * pos * RP : (2 * pos + 1) * RP, col : col + width] = first
        target[(2 * pos + 1) * RP : (2 * pos + 2) * RP, col : col + width] = second


def key_sides(k, count):
    rows = k.shape[0]
    lane = lane_ids(rows)
    place = lane % HDIM
    row = lax.broadcasted_iota(jnp.int32, (rows, 128), 0)
    mask = jnp.where(row >= count, NEG_FILL, 0.0)
    extra = jnp.where(place == 0, mask, jnp.where(place <= 3, 1.0, 0.0)).astype(BF)
    low = lane < HDIM
    return jnp.where(low, k, extra), jnp.where(low, extra, k)


def split_three(value):
    high = value.astype(BF)
    rest = value - high.astype(F32)
    mid = rest.astype(BF)
    low = (rest - mid.astype(F32)).astype(BF)
    return high, mid, low


def attend_kernel(
    tab, own_ref, nb_ref, mid_ref, same_ref, other_ref, vec_ref, o_ref, qe_ref, qo_ref, k_ref, v_ref, w_s, ka_e, ka_o, va_e, va_o
):
    core = tab[20]
    for part in range(3):
        assemble(core, same_ref, other_ref, part, w_s, 128 * part)
    bias_q = vec_ref[0:1, :]
    bias_v = vec_ref[1:2, :]
    low = lane_ids(BLK) < HDIM
    place = lane_ids(BLK) % HDIM
    ones = jnp.ones((BLK, 128), BF)
    for b in range(8):
        src, at = (own_ref, b) if b < 3 else (nb_ref, b - 3) if b < 6 else (mid_ref, b - 6)
        kv = dot_nn(src[at * BLK : (at + 1) * BLK, :], w_s[:, 128:384])
        k = kv[:, :128].astype(BF)
        v = (kv[:, 128:] + bias_v).astype(BF)
        k_ref[b * BLK : (b + 1) * BLK, :] = k
        v_ref[b * BLK : (b + 1) * BLK, :] = v
        k_even, k_odd = key_sides(k, tab[12 + b])
        ka_e[b] = k_even
        ka_o[b] = k_odd
        va_e[b] = jnp.where(low, v, ones)
        va_o[b] = jnp.where(low, ones, v)
    q_extra = jnp.where(place == 0, 1.0, 0.0).astype(BF)
    for i in range(3):
        q = (dot_nn(own_ref[i * BLK : (i + 1) * BLK, :], w_s[:, :128]) + bias_q).astype(BF) * jnp.asarray(0.125, BF)
        outs = []
        for head, (ka, va) in enumerate(((ka_e, va_e), (ka_o, va_o))):
            qa = jnp.where(low, q, q_extra) if head == 0 else jnp.where(low, q_extra, q)
            scores = [dot_nt(qa, ka[tab[4 * i + j]]) for j in range(4)]
            peak = jnp.max(
                jnp.maximum(jnp.maximum(scores[0], scores[1]), jnp.maximum(scores[2], scores[3])), -1, keepdims=True
            )
            acc = None
            for j in range(4):
                probs = jnp.exp(scores[j] - peak).astype(BF)
                part = dot_nn(probs, va[tab[4 * i + j]])
                acc = part if acc is None else acc + part
            log_sum = peak + jnp.log(acc)
            high, mid, small = split_three(-log_sum)
            extra = jnp.where(place == 0, 1.0, 0.0).astype(BF)
            extra = jnp.where(place == 1, high, extra)
            extra = jnp.where(place == 2, mid, extra)
            extra = jnp.where(place == 3, small, extra)
            if head == 0:
                qe_ref[i * BLK : (i + 1) * BLK, :] = jnp.where(low, q, extra)
            else:
                qo_ref[i * BLK : (i + 1) * BLK, :] = jnp.where(low, extra, q)
            outs.append(acc)
        total = jnp.where(low, outs[1], outs[0])
        value = jnp.where(low, outs[0], outs[1])
        o_ref[i * BLK : (i + 1) * BLK, :] = (value / pltpu.roll(total, HDIM, 1)).astype(BF)


def attend_back_kernel(
    tab,
    qe_ref,
    qo_ref,
    k_ref,
    v_ref,
    do_ref,
    o_ref,
    xt_ref,
    dq_ref,
    dk_ref,
    dv_ref,
    dw_ref,
    db_ref,
    ka_e,
    ka_o,
    vb_e,
    vb_o,
    kt_s,
    dk_s,
    dv_s,
    dkv_s,
):
    low = lane_ids(BLK) < HDIM
    place = lane_ids(BLK) % HDIM
    v_extra = jnp.where(place < 3, 1.0, 0.0).astype(BF)
    zero = jnp.zeros((BLK, 128), BF)
    for b in range(8):
        k = k_ref[b * BLK : (b + 1) * BLK, :]
        v = v_ref[b * BLK : (b + 1) * BLK, :]
        k_even, k_odd = key_sides(k, tab[12 + b])
        ka_e[b] = k_even
        ka_o[b] = k_odd
        vb_e[b] = jnp.where(low, v, v_extra)
        vb_o[b] = jnp.where(low, v_extra, v)
        kt_s[b] = k.T
        dk_s[b] = jnp.zeros((BLK, 128), F32)
        dv_s[b] = jnp.zeros((BLK, 128), F32)
    for i in range(3):
        rows = slice(i * BLK, (i + 1) * BLK)
        d_out = do_ref[rows, :]
        product = d_out.astype(F32) * o_ref[rows, :].astype(F32)
        qas = (qe_ref[rows, :], qo_ref[rows, :])
        sides = []
        for head in range(2):
            mine = low if head == 0 else jnp.logical_not(low)
            delta = jnp.sum(jnp.where(mine, product, 0.0), -1, keepdims=True)
            high, mid, small = split_three(-delta)
            extra = jnp.where(place == 0, high, jnp.where(place == 1, mid, jnp.where(place == 2, small, zero)))
            sides.append((jnp.where(mine, d_out, extra), jnp.where(mine, d_out, zero), jnp.where(mine, qas[head], zero)))
        dqt = [None, None]
        for j in range(4):
            b = tab[4 * i + j]
            dv_part = None
            dk_part = None
            for head, (ka, vb) in enumerate(((ka_e, vb_e), (ka_o, vb_o))):
                d_aug, d_only, q_only = sides[head]
                probs = jnp.exp(dot_nt(ka[b], qas[head]))
                d_probs = dot_nt(vb[b], d_aug)
                d_scores = (probs * d_probs).astype(BF)
                v_add = dot_nn(probs.astype(BF), d_only)
                k_add = dot_nn(d_scores, q_only)
                dv_part = v_add if dv_part is None else dv_part + v_add
                dk_part = k_add if dk_part is None else dk_part + k_add
                q_add = dot_nn(kt_s[b, head * HDIM : (head + 1) * HDIM, :], d_scores)
                dqt[head] = q_add if dqt[head] is None else dqt[head] + q_add
            dv_s[b] += dv_part
            dk_s[b] += dk_part
        dq_ref[rows, :] = (jnp.concatenate(dqt, 0).T * 0.125).astype(BF)
    for b in range(8):
        dk = dk_s[b].astype(BF)
        dv = dv_s[b].astype(BF)
        dk_ref[b * BLK : (b + 1) * BLK, :] = dk
        dv_ref[b * BLK : (b + 1) * BLK, :] = dv
        dkv_s[b * BLK : (b + 1) * BLK, :128] = dk
        dkv_s[b * BLK : (b + 1) * BLK, 128:] = dv
    dq_all = dq_ref[...]
    db_ref[0:1, :] = jnp.sum(dq_all.astype(F32), 0, keepdims=True)
    db_ref[1:2, :] = jnp.sum(dkv_s[:, 128:].astype(F32), 0, keepdims=True)
    dw_ref[:, 0] = dot_nn(xt_ref[:, :ROWS], dq_all).astype(BF).reshape(RB, RP, 128)
    dw_kv = dot_nn(xt_ref[...], dkv_s[...]).astype(BF)
    dw_ref[:, 1] = dw_kv[:, :128].reshape(RB, RP, 128)
    dw_ref[:, 2] = dw_kv[:, 128:].reshape(RB, RP, 128)


def gelu_both(pre):
    size = jnp.abs(pre)
    bell = jnp.exp(pre * pre * -0.5)
    t = 1.0 / (1.0 + size * (0.3275911 * math.sqrt(0.5)))
    poly = t * (
        0.5 * 0.254829592
        + t * (0.5 * -0.284496736 + t * (0.5 * 1.421413741 + t * (0.5 * -1.453152027 + t * (0.5 * 1.061405429))))
    )
    tail = poly * bell
    phi = jnp.where(pre >= 0, 1.0 - tail, tail)
    return pre * phi, phi + pre * bell * (1.0 / math.sqrt(2.0 * math.pi))


def norm_parts(summed):
    average = jnp.mean(summed, -1, keepdims=True)
    centered = summed - average
    variance = jnp.mean(centered * centered, -1, keepdims=True)
    root = lax.rsqrt(variance + LN_EPS)
    return centered * root, root


def norm_back(cot, gain, hat, root):
    gz = cot * gain
    return root * (gz - jnp.mean(gz, -1, keepdims=True) - hat * jnp.mean(gz * hat, -1, keepdims=True))


def feed_kernel(
    tab,
    o_ref,
    x_ref,
    same_ref,
    other_ref,
    vec_ref,
    w_ref,
    cot_ref,
    weight_ref,
    u_ref,
    gp_ref,
    out_ref,
    dz2_ref,
    e2_ref,
    e2t_ref,
    h1t_ref,
    hat1_ref,
    root1_ref,
    sums_ref,
    wo_s,
    h1_s,
    h1b_s,
    z2_s,
):
    step = pl.program_id(0)

    @pl.when(step == 0)
    def _():
        assemble(tab[20], same_ref, other_ref, 0, wo_s, 0)
        for i in range(3):
            rows = slice(i * BLK, (i + 1) * BLK)
            z1 = x_ref[rows, :].astype(F32) + dot_nt(o_ref[rows, :], wo_s[...]) + vec_ref[2:3, :]
            hat, root = norm_parts(z1)
            h1 = hat * vec_ref[3:4, :] + vec_ref[4:5, :]
            hat1_ref[rows, :] = hat
            root1_ref[rows, :] = root
            h1_s[rows, :] = h1
            h1b = h1.astype(BF)
            h1b_s[rows, :] = h1b
            h1t_ref[:, rows] = h1b.T

    w1 = w_ref[:, 0, 0].reshape(D, D)
    w2t = w_ref[:, 0, 1].reshape(D, D)
    bias = vec_ref[pl.ds(8 + step, 1), :]
    for i in range(3):
        rows = slice(i * BLK, (i + 1) * BLK)
        pre = dot_nn(h1b_s[rows, :], w1) + bias
        act, slope = gelu_both(pre)
        act = act.astype(BF)
        u_ref[rows, :] = act
        gp_ref[rows, :] = slope.astype(BF)
        feed = dot_nt(act, w2t)

        @pl.when(step == 0)
        def _():
            z2_s[rows, :] = feed

        @pl.when(step > 0)
        def _():
            z2_s[rows, :] += feed

    @pl.when(step == 3)
    def _():
        sums = [jnp.zeros((1, D), F32) for _ in range(3)]
        for i in range(3):
            rows = slice(i * BLK, (i + 1) * BLK)
            z2 = h1_s[rows, :] + z2_s[rows, :] + vec_ref[5:6, :]
            hat, root = norm_parts(z2)
            out_ref[rows, :] = (hat * vec_ref[6:7, :] + vec_ref[7:8, :]).astype(BF)
            cot = cot_ref[rows, :].astype(F32) * weight_ref[rows, :]
            dz2 = norm_back(cot, vec_ref[6:7, :], hat, root)
            dz2_ref[rows, :] = dz2
            e2 = dz2.astype(BF)
            e2_ref[rows, :] = e2
            e2t_ref[:, rows] = e2.T
            sums[0] += jnp.sum(dz2, 0, keepdims=True)
            sums[1] += jnp.sum(cot * hat, 0, keepdims=True)
            sums[2] += jnp.sum(cot, 0, keepdims=True)
        for n in range(3):
            sums_ref[n : n + 1, :] = sums[n]


def feed_back_kernel(
    tab,
    e2_ref,
    e2t_ref,
    h1t_ref,
    u_ref,
    gp_ref,
    w_ref,
    dz2_ref,
    hat1_ref,
    root1_ref,
    o_ref,
    same_ref,
    other_ref,
    vec_ref,
    dw_ref,
    dz1_ref,
    do_ref,
    dwo_ref,
    sums_ref,
    db1_ref,
    ep_s,
    dh_s,
    wo_s,
    e1t_s,
):
    step = pl.program_id(0)
    w1 = w_ref[:, 0, 0].reshape(D, D)
    w2t = w_ref[:, 0, 1].reshape(D, D)
    db1 = jnp.zeros((1, D), F32)
    for i in range(3):
        rows = slice(i * BLK, (i + 1) * BLK)
        du = dot_nn(e2_ref[rows, :], w2t)
        ep = (gp_ref[rows, :].astype(F32) * du).astype(BF)
        ep_s[rows, :] = ep
        db1 += jnp.sum(ep.astype(F32), 0, keepdims=True)
        back = dot_nt(ep, w1)

        @pl.when(step == 0)
        def _():
            dh_s[rows, :] = back + dz2_ref[rows, :]

        @pl.when(step > 0)
        def _():
            dh_s[rows, :] += back

    db1_ref[pl.ds(step, 1), :] = db1
    dw_ref[:, 0, 0] = dot_nn(h1t_ref[...], ep_s[...]).astype(BF).reshape(RB, RP, D)
    dw_ref[:, 0, 1] = dot_nn(e2t_ref[...], u_ref[...]).astype(BF).reshape(RB, RP, D)

    @pl.when(step == 3)
    def _():
        assemble(tab[20], same_ref, other_ref, 0, wo_s, 0)
        sums = [jnp.zeros((1, D), F32) for _ in range(3)]
        for i in range(3):
            rows = slice(i * BLK, (i + 1) * BLK)
            dh = dh_s[rows, :]
            hat = hat1_ref[rows, :]
            dz1 = norm_back(dh, vec_ref[3:4, :], hat, root1_ref[rows, :])
            dz1_ref[rows, :] = dz1
            e1 = dz1.astype(BF)
            e1t_s[:, rows] = e1.T
            do_ref[rows, :] = dot_nn(e1, wo_s[...]).astype(BF)
            sums[0] += jnp.sum(dz1, 0, keepdims=True)
            sums[1] += jnp.sum(dh * hat, 0, keepdims=True)
            sums[2] += jnp.sum(dh, 0, keepdims=True)
        for n in range(3):
            sums_ref[n : n + 1, :] = sums[n]
        dwo_ref[...] = dot_nn(e1t_s[...], o_ref[...]).astype(BF).reshape(RB, RP, D)


def input_kernel(tab, dq_ref, dk_ref, dv_ref, same_ref, other_ref, dz1_ref, own_ref, rest_ref, w_s):
    step = pl.program_id(0)

    @pl.when(step == 0)
    def _():
        for part in range(3):
            assemble(tab[20], same_ref, other_ref, part, w_s, D * part)

    back = dot_nt(dk_ref[...], w_s[:, D : 2 * D]) + dot_nt(dv_ref[...], w_s[:, 2 * D :])

    @pl.when(step < 3)
    def _():
        own_ref[...] = back + dot_nt(dq_ref[...], w_s[:, :D]) + dz1_ref[...]

    @pl.when(step >= 3)
    def _():
        rest_ref[...] = back.astype(BF)


def call(kernel, grid, in_specs, out_specs, out_shape, scratch, flops, bytes_accessed, name):
    return pl.pallas_call(
        kernel,
        grid_spec=pltpu.PrefetchScalarGridSpec(
            num_scalar_prefetch=1, grid=(grid,), in_specs=in_specs, out_specs=out_specs, scratch_shapes=scratch
        ),
        out_shape=out_shape,
        compiler_params=pltpu.CompilerParams(
            dimension_semantics=("arbitrary",), vmem_limit_bytes=VMEM_LIMIT
        ),
        cost_estimate=pl.CostEstimate(flops=flops, bytes_accessed=bytes_accessed, transcendentals=0),
        name=name,
    )


def whole(*shape):
    return pl.BlockSpec(shape, lambda s, t: (0,) * len(shape))


def columns(rows, width=128):
    return pl.BlockSpec((rows, width), lambda s, t: (0, s))


def shape_of(shape, dtype):
    return jax.ShapeDtypeStruct(shape, dtype)


def vm(shape, dtype):
    return pltpu.VMEM(shape, dtype)


def attend(tab, own, nb, mid, same, other, vectors):
    w_spec = pl.BlockSpec((4, 3, RP, 128), lambda s, t: (0, 0, 0, s))
    return call(
        attend_kernel,
        PAIRS,
        [whole(ROWS, D), whole(ROWS, D), whole(2 * BLK, D), w_spec, w_spec, columns(12)],
        [columns(ROWS), columns(ROWS), columns(ROWS), columns(8 * BLK), columns(8 * BLK)],
        [shape_of((ROWS, D), BF)] * 3 + [shape_of((8 * BLK, D), BF)] * 2,
        [vm((D, 384), BF)] + [vm((8, BLK, 128), BF)] * 4,
        28_000_000_000,
        16_000_000,
        "attend",
    )(tab, own, nb, mid, same, other, vectors)


def attend_back(tab, qe, qo, k, v, d_out, o, xt):
    return call(
        attend_back_kernel,
        PAIRS,
        [columns(ROWS), columns(ROWS), columns(8 * BLK), columns(8 * BLK), columns(ROWS), columns(ROWS), whole(D, 8 * BLK)],
        [
            columns(ROWS),
            columns(8 * BLK),
            columns(8 * BLK),
            pl.BlockSpec((RB, 3, RP, 128), lambda s, t: (0, 0, 0, s)),
            columns(2),
        ],
        [
            shape_of((ROWS, D), BF),
            shape_of((8 * BLK, D), BF),
            shape_of((8 * BLK, D), BF),
            shape_of((RB, 3, RP, D), BF),
            shape_of((2, D), F32),
        ],
        [vm((8, BLK, 128), BF)] * 4
        + [vm((8, 128, BLK), BF)]
        + [vm((8, BLK, 128), F32)] * 2
        + [vm((8 * BLK, BLK), BF)],
        50_000_000_000,
        24_000_000,
        "attend_back",
    )(tab, qe, qo, k, v, d_out, o, xt)


def feed(tab, o, x, same, other, vectors, w, cot, weight):
    wo_spec = pl.BlockSpec((4, 1, RP, D), lambda s, t: (0, 3, 0, 0))
    return call(
        feed_kernel,
        4,
        [
            whole(ROWS, D),
            whole(ROWS, D),
            wo_spec,
            wo_spec,
            whole(12, D),
            pl.BlockSpec((RB, 1, 2, RP, D), lambda s, t: (0, s, 0, 0, 0)),
            whole(ROWS, D),
            whole(ROWS, 1),
        ],
        [
            columns(ROWS, D),
            columns(ROWS, D),
            whole(ROWS, D),
            whole(ROWS, D),
            whole(ROWS, D),
            whole(D, ROWS),
            whole(D, ROWS),
            whole(ROWS, D),
            whole(ROWS, 1),
            whole(3, D),
        ],
        [
            shape_of((ROWS, FF), BF),
            shape_of((ROWS, FF), BF),
            shape_of((ROWS, D), BF),
            shape_of((ROWS, D), F32),
            shape_of((ROWS, D), BF),
            shape_of((D, ROWS), BF),
            shape_of((D, ROWS), BF),
            shape_of((ROWS, D), F32),
            shape_of((ROWS, 1), F32),
            shape_of((3, D), F32),
        ],
        [vm((D, D), BF), vm((ROWS, D), F32), vm((ROWS, D), BF), vm((ROWS, D), F32)],
        18_000_000_000,
        40_000_000,
        "feed",
    )(tab, o, x, same, other, vectors, w, cot, weight)


def feed_back(tab, e2, e2t, h1t, u, gp, w, dz2, hat1, root1, o, same, other, vectors):
    wo_spec = pl.BlockSpec((4, 1, RP, D), lambda s, t: (0, 3, 0, 0))
    w_spec = pl.BlockSpec((RB, 1, 2, RP, D), lambda s, t: (0, s, 0, 0, 0))
    return call(
        feed_back_kernel,
        4,
        [
            whole(ROWS, D),
            whole(D, ROWS),
            whole(D, ROWS),
            columns(ROWS, D),
            columns(ROWS, D),
            w_spec,
            whole(ROWS, D),
            whole(ROWS, D),
            whole(ROWS, 1),
            whole(ROWS, D),
            wo_spec,
            wo_spec,
            whole(12, D),
        ],
        [w_spec, whole(ROWS, D), whole(ROWS, D), whole(RB, RP, D), whole(3, D), whole(4, D)],
        [
            shape_of((RB, 4, 2, RP, D), BF),
            shape_of((ROWS, D), F32),
            shape_of((ROWS, D), BF),
            shape_of((RB, RP, D), BF),
            shape_of((3, D), F32),
            shape_of((4, D), F32),
        ],
        [vm((ROWS, D), BF), vm((ROWS, D), F32), vm((D, D), BF), vm((D, ROWS), BF)],
        24_000_000_000,
        48_000_000,
        "feed_back",
    )(tab, e2, e2t, h1t, u, gp, w, dz2, hat1, root1, o, same, other, vectors)


def input_back(tab, dq, dk, dv, same, other, dz1):
    w_spec = pl.BlockSpec((4, 3, RP, D), lambda s, t: (0, 0, 0, 0))
    first = pl.BlockSpec((BLK, D), lambda s, t: (jnp.minimum(s, 2), 0))
    each = pl.BlockSpec((BLK, D), lambda s, t: (s, 0))
    return call(
        input_kernel,
        8,
        [first, each, each, w_spec, w_spec, first],
        [first, pl.BlockSpec((BLK, D), lambda s, t: (jnp.maximum(s - 3, 0), 0))],
        [shape_of((ROWS, D), F32), shape_of((5 * BLK, D), BF)],
        [vm((D, 3 * D), BF)],
        6_000_000_000,
        16_000_000,
        "input_back",
    )(tab, dq, dk, dv, same, other, dz1)


def adamw(weight, grad, first, second, rate, decay, clip_factor):
    clipped = grad * clip_factor
    first_new = BETA_ONE * first + (1.0 - BETA_ONE) * clipped
    second_new = BETA_TWO * second + (1.0 - BETA_TWO) * clipped * clipped
    first_hat = first_new / (1.0 - BETA_ONE**STEP)
    second_hat = second_new / (1.0 - BETA_TWO**STEP)
    updated = weight * (1.0 - rate * decay) - rate * first_hat / (jnp.sqrt(second_hat) + ADAM_EPS)
    return (clipped, first_new, second_new, updated)


def shards(
    tokens,
    out_cotangent,
    lengths,
    starts,
    ends,
    flags,
    qkv_master,
    proj_master,
    up_master,
    down_master,
    vectors,
    qkv_first,
    proj_first,
    up_first,
    down_first,
    qkv_second,
    proj_second,
    up_second,
    down_second,
    vector_first,
    vector_second,
):
    mp_count = lax.axis_size("mp")
    dp_count = lax.axis_size("dp")
    devices = mp_count * dp_count
    z = lax.axis_index("mp")
    dp_index = lax.axis_index("dp")
    core = dp_index % 2
    chips = dp_count // 2
    part = D // dp_count
    head_cols = D // mp_count

    def linear(chip, core_of, z_of):
        return (chip * 2 + core_of) * mp_count + z_of

    planes = [[linear(chip, c, k) for chip in range(chips)] for c in range(2) for k in range(mp_count)]
    swap_core = [
        (linear(chip, c, k), linear(chip, 1 - c, k)) for chip in range(chips) for c in range(2) for k in range(mp_count)
    ]
    swap_z = [
        (linear(chip, c, k), linear(chip, c, k ^ 1)) for chip in range(chips) for c in range(2) for k in range(mp_count)
    ]
    middle = (0, 2, 1, 3)
    swap_mid = [
        (linear(chip, c, k), linear(chip, c, middle[k])) for chip in range(chips) for c in range(2) for k in range(mp_count)
    ]

    def over_plane(value):
        return lax.all_to_all(value, AXES, 0, 0, tiled=True, axis_index_groups=planes)

    def over_z(value):
        return lax.all_to_all(value, "mp", 0, 0, tiled=True)

    mine = jnp.concatenate(
        [qkv_master[0], qkv_master[1], qkv_master[2], proj_master.T], 1
    ).astype(BF)
    along_z = over_z(jnp.broadcast_to(mine[None], (mp_count, part, D)))
    along_z = along_z.reshape(mp_count, part, 4, head_cols).transpose(2, 1, 0, 3).reshape(4, part, D)
    same = over_plane(jnp.broadcast_to(along_z[None], (chips, 4, part, D)))
    other = lax.ppermute(same, AXES, swap_core)
    kernel_core = core
    if part != RP:
        both = jnp.where(core == 0, jnp.stack([same, other], 1), jnp.stack([other, same], 1))
        both = both.transpose(2, 0, 1, 3, 4).reshape(4, RB // 2, 2, RP, D).transpose(1, 2, 0, 3, 4)
        same, other = both[:, 0], both[:, 1]
        kernel_core = jnp.zeros((), jnp.int32)
    feed_mine = jnp.stack([up_master, down_master.T]).astype(BF)
    feed_w = lax.all_gather(feed_mine, AXES, axis=0, tiled=False).reshape(dp_count, mp_count, 2, part, D)
    if part != RP:
        feed_w = feed_w.transpose(1, 2, 0, 3, 4).reshape(mp_count, 2, RB, RP, D).transpose(2, 0, 1, 3, 4)

    mid_at = jnp.where(z == 1, BLK, 0)
    nb = lax.ppermute(tokens, AXES, swap_z)
    mid = lax.ppermute(lax.dynamic_slice_in_dim(tokens, mid_at, 2 * BLK, 0), AXES, swap_mid)
    xt = jnp.concatenate([tokens, nb, mid], 0).T

    place = jnp.asarray(BLOCK_PLACE)[z]
    counts = jnp.clip(lengths[jnp.asarray(BLOCK_SEQ)[z]] - BLK * place, 0, BLK)
    tab = jnp.concatenate(
        [jnp.asarray(KEY_BLOCKS)[z].reshape(12), counts, kernel_core.reshape(1)]
    ).astype(jnp.int32)

    positions = z * ROWS + jnp.arange(ROWS, dtype=jnp.int32)
    seq_of = positions // LEN
    within = positions % LEN
    picker = (seq_of[:, None] == jnp.arange(lengths.shape[0], dtype=jnp.int32)[None, :]).astype(jnp.int32)
    length_row = jnp.sum(picker * lengths[None, :], 1)
    start_row = jnp.sum(picker * starts[None, :], 1)
    end_row = jnp.sum(picker * ends[None, :], 1)
    flag_row = jnp.sum(picker * flags[None, :], 1).astype(F32)
    valid_row = (within < length_row).astype(F32)
    answer = (within == start_row).astype(F32) + (within == end_row).astype(F32)
    opening = (within == 0).astype(F32)
    row_weight = valid_row * (1.0 + 2.0 * (1.0 - flag_row) * answer + 4.0 * flag_row * opening)

    o, qe, qo, k, v = attend(tab, tokens, nb, mid, same, other, vectors)
    u, gp, block_out, dz2, e2, e2t, h1t, hat1, root1, sums_two = feed(
        tab, o, tokens, same, other, vectors, feed_w, out_cotangent, row_weight[:, None]
    )
    feed_dw, dz1, d_o, wo_dw, sums_one, bias_up_grad = feed_back(
        tab, e2, e2t, h1t, u, gp, feed_w, dz2, hat1, root1, o, same, other, vectors
    )

    def to_parts(grad):
        if part == RP:
            return grad
        lead = grad.shape[1:-2]
        moved = jnp.moveaxis(grad, 0, -3).reshape(*lead, dp_count, part, D)
        return jnp.moveaxis(moved, -3, 0)

    feed_dw = to_parts(feed_dw)
    feed_sum = lax.psum_scatter(feed_dw, "dp", scatter_dimension=0, tiled=False)
    feed_sum = lax.psum_scatter(feed_sum, "mp", scatter_dimension=0, tiled=False).astype(F32)

    dq, dk, dv, qkv_dw, sums_head = attend_back(tab, qe, qo, k, v, d_o, o, xt)
    head_dw = to_parts(jnp.concatenate([qkv_dw, wo_dw[:, None]], 1))
    head_dw = head_dw.reshape(chips, 2, 4, part, D)
    keep = lax.dynamic_index_in_dim(head_dw, core, 1, keepdims=False)
    give = lax.dynamic_index_in_dim(head_dw, 1 - core, 1, keepdims=False)
    got = lax.ppermute(give, AXES, swap_core)
    chip_sum = (keep.astype(F32) + got.astype(F32)).astype(BF)
    plane_sum = jnp.sum(over_plane(chip_sum).astype(F32), 0)
    plane_sum = plane_sum.astype(BF).reshape(4, part, mp_count, head_cols).transpose(2, 1, 0, 3)
    head_sum = jnp.sum(over_z(plane_sum.reshape(mp_count, part, D)).astype(F32), 0)

    dx_own, dx_rest = input_back(tab, dq, dk, dv, same, other, dz1)
    from_nb = lax.ppermute(dx_rest[: 3 * BLK], AXES, swap_z)
    from_mid = lax.ppermute(dx_rest[3 * BLK :], AXES, swap_mid)
    zero_block = jnp.zeros((BLK, D), BF)
    from_mid = jnp.where(
        z == 1, jnp.concatenate([zero_block, from_mid], 0), jnp.concatenate([from_mid, zero_block], 0)
    )
    input_grad = dx_own + from_nb.astype(F32) + from_mid.astype(F32)

    vector_part = jnp.concatenate([sums_head, sums_one, sums_two, bias_up_grad], 0)
    vec_columns = D // devices
    vector_part = vector_part.reshape(12, devices, vec_columns).transpose(1, 0, 2)
    vector_grad = jnp.sum(lax.all_to_all(vector_part, AXES, 0, 0, tiled=True), 0)

    qkv_sum = jnp.stack([head_sum[:, n * head_cols : (n + 1) * head_cols] for n in range(3)])
    proj_sum = head_sum[:, 3 * head_cols :].T
    up_sum = feed_sum[0]
    down_sum = feed_sum[1].T
    local_squares = jnp.sum(head_sum * head_sum) + jnp.sum(feed_sum * feed_sum) + jnp.sum(vector_grad * vector_grad)
    squares = lax.all_to_all(jnp.broadcast_to(local_squares, (devices,)), AXES, 0, 0, tiled=True)
    grad_norm = jnp.sqrt(jnp.sum(squares))
    clip_factor = jnp.minimum(1.0, CLIP_NORM / (grad_norm + 1e-06))
    matrix_rate = MATRIX_RATE / math.sqrt(D)
    vec_index = dp_index * mp_count + z
    vector_shard = lax.dynamic_slice_in_dim(vectors, vec_index * vec_columns, vec_columns, 1)
    qkv_set = adamw(qkv_master, qkv_sum, qkv_first, qkv_second, matrix_rate, WEIGHT_DECAY, clip_factor)
    proj_set = adamw(proj_master, proj_sum, proj_first, proj_second, matrix_rate, WEIGHT_DECAY, clip_factor)
    up_set = adamw(up_master, up_sum, up_first, up_second, matrix_rate, WEIGHT_DECAY, clip_factor)
    down_set = adamw(down_master, down_sum, down_first, down_second, matrix_rate, WEIGHT_DECAY, clip_factor)
    vector_set = adamw(vector_shard, vector_grad, vector_first, vector_second, VECTOR_RATE, 0.0, clip_factor)
    return (block_out, input_grad, grad_norm, *qkv_set, *proj_set, *up_set, *down_set, *vector_set)


def solution(mesh):
    rows = P(AXES, None)
    group = P("dp")
    qkv = P(None, "dp", "mp")
    proj = P("mp", "dp")
    up = P("dp", "mp")
    vec = P(None, AXES)
    return jax.shard_map(
        shards,
        mesh=mesh,
        in_specs=(rows, rows, group, group, group, group)
        + (qkv, proj, up, proj, P())
        + (qkv, proj, up, proj) * 2
        + (vec, vec),
        out_specs=(rows, rows, P()) + (qkv,) * 4 + (proj,) * 4 + (up,) * 4 + (proj,) * 4 + (vec,) * 4,
        check_vma=False,
    )
```

```python
from functools import partial
import math

import jax
import jax.numpy as jnp
import numpy as np
from jax import lax
from jax.experimental import pallas as pl
from jax.experimental.pallas import tpu as pltpu
from jax.sharding import PartitionSpec as P

D = 768
HEADS = 12
HDIM = 64
FF = 3072
LEN = 1024
STEP = 10

LN_EPS = 1e-06
BETA_ONE = 0.9
BETA_TWO = 0.999
ADAM_EPS = 1e-08
WEIGHT_DECAY = 0.01
CLIP_NORM = 1.0
VECTOR_RATE = 1.0
MATRIX_RATE = 2.0
NEG_FILL = -1e30

BF = jnp.bfloat16
F32 = jnp.float32
AXES = ("dp", "mp")
BLK = 256
ROWS = 768
PAIRS = HEADS // 2
RB = 8
RP = D // RB
VMEM_LIMIT = 60 * 1024 * 1024

KEY_BLOCKS = np.array(
    [
        [[0, 1, 2, 3]] * 3,
        [[3, 4, 5, 0], [1, 2, 6, 7], [1, 2, 6, 7]],
        [[6, 7, 0, 1], [6, 7, 0, 1], [2, 3, 4, 5]],
        [[5, 0, 1, 2]] * 3,
    ],
    np.int32,
)
BLOCK_SEQ = np.array(
    [[0, 0, 0, 0, 0, 0, 0, 0], [0, 1, 1, 0, 0, 0, 1, 1], [1, 1, 2, 2, 2, 2, 1, 1], [2, 2, 2, 2, 2, 2, 2, 2]], np.int32
)
BLOCK_PLACE = np.array(
    [[0, 1, 2, 3, 4, 4, 4, 4], [3, 0, 1, 0, 1, 2, 2, 3], [2, 3, 0, 1, 2, 3, 0, 1], [1, 2, 3, 4, 4, 0, 4, 4]], np.int32
)


def dot_nn(left, right):
    return jnp.dot(left, right, preferred_element_type=F32)


def dot_nt(left, right):
    return lax.dot_general(left, right, (((1,), (1,)), ((), ())), preferred_element_type=F32)


def lane_ids(rows):
    return lax.broadcasted_iota(jnp.int32, (rows, 128), 1)


def assemble(tab, pieces, part, target, col):
    width = pieces[0].shape[-1]
    core, chip = tab[20], tab[21]
    for n in range(4):
        for half in range(2):
            at = ((n ^ chip) * 2 + (core ^ half)) * RP
            target[pl.ds(pl.multiple_of(at, RP), RP), col : col + width] = pieces[4 * half + n][part]


def key_sides(k, count):
    rows = k.shape[0]
    lane = lane_ids(rows)
    place = lane % HDIM
    row = lax.broadcasted_iota(jnp.int32, (rows, 128), 0)
    mask = jnp.where(row >= count, NEG_FILL, 0.0)
    extra = jnp.where(place == 0, mask, jnp.where(place <= 3, 1.0, 0.0)).astype(BF)
    low = lane < HDIM
    return jnp.where(low, k, extra), jnp.where(low, extra, k)


def split_three(value):
    high = value.astype(BF)
    rest = value - high.astype(F32)
    mid = rest.astype(BF)
    low = (rest - mid.astype(F32)).astype(BF)
    return high, mid, low


def attend_kernel(
    tab, own_ref, nb_ref, mid_ref, *refs
):
    pieces = refs[:8]
    vec_ref, o_ref, qe_ref, qo_ref, k_ref, v_ref, xt_ref, w_s, ka_e, ka_o, va_e, va_o = refs[8:]
    mine = pl.ds(pl.multiple_of(pl.program_id(0) * 128, 128), 128)
    for part in range(3):
        assemble(tab, pieces, part, w_s, 128 * part)
    bias_q = vec_ref[0:1, :]
    bias_v = vec_ref[1:2, :]
    low = lane_ids(BLK) < HDIM
    place = lane_ids(BLK) % HDIM
    ones = jnp.ones((BLK, 128), BF)
    for b in range(8):
        src, at = (own_ref, b) if b < 3 else (nb_ref, b - 3) if b < 6 else (mid_ref, b - 6)
        xt_ref[:, b * BLK : (b + 1) * BLK] = src[at * BLK : (at + 1) * BLK, mine].T
        kv = dot_nn(src[at * BLK : (at + 1) * BLK, :], w_s[:, 128:384])
        k = kv[:, :128].astype(BF)
        v = (kv[:, 128:] + bias_v).astype(BF)
        k_ref[b * BLK : (b + 1) * BLK, :] = k
        v_ref[b * BLK : (b + 1) * BLK, :] = v
        k_even, k_odd = key_sides(k, tab[12 + b])
        ka_e[b] = k_even
        ka_o[b] = k_odd
        va_e[b] = jnp.where(low, v, ones)
        va_o[b] = jnp.where(low, ones, v)
    q_extra = jnp.where(place == 0, 1.0, 0.0).astype(BF)
    for i in range(3):
        q = (dot_nn(own_ref[i * BLK : (i + 1) * BLK, :], w_s[:, :128]) + bias_q).astype(BF) * jnp.asarray(0.125, BF)
        outs = []
        for head, (ka, va) in enumerate(((ka_e, va_e), (ka_o, va_o))):
            qa = jnp.where(low, q, q_extra) if head == 0 else jnp.where(low, q_extra, q)
            scores = [dot_nt(qa, ka[tab[4 * i + j]]) for j in range(4)]
            peak = jnp.max(
                jnp.maximum(jnp.maximum(scores[0], scores[1]), jnp.maximum(scores[2], scores[3])), -1, keepdims=True
            )
            acc = None
            for j in range(4):
                probs = jnp.exp(scores[j] - peak).astype(BF)
                part = dot_nn(probs, va[tab[4 * i + j]])
                acc = part if acc is None else acc + part
            log_sum = peak + jnp.log(acc)
            high, mid, small = split_three(-log_sum)
            extra = jnp.where(place == 0, 1.0, 0.0).astype(BF)
            extra = jnp.where(place == 1, high, extra)
            extra = jnp.where(place == 2, mid, extra)
            extra = jnp.where(place == 3, small, extra)
            if head == 0:
                qe_ref[i * BLK : (i + 1) * BLK, :] = jnp.where(low, q, extra)
            else:
                qo_ref[i * BLK : (i + 1) * BLK, :] = jnp.where(low, extra, q)
            outs.append(acc)
        total = jnp.where(low, outs[1], outs[0])
        value = jnp.where(low, outs[0], outs[1])
        o_ref[i * BLK : (i + 1) * BLK, :] = (value / pltpu.roll(total, HDIM, 1)).astype(BF)


def attend_back_kernel(
    tab,
    qe_ref,
    qo_ref,
    k_ref,
    v_ref,
    do_ref,
    o_ref,
    xt_ref,
    dq_ref,
    dk_ref,
    dv_ref,
    keep_ref,
    give_ref,
    db_ref,
    ka_e,
    ka_o,
    vb_e,
    vb_o,
    kt_s,
    dk_s,
    dv_s,
    dkv_s,
):
    low = lane_ids(BLK) < HDIM
    place = lane_ids(BLK) % HDIM
    v_extra = jnp.where(place < 3, 1.0, 0.0).astype(BF)
    zero = jnp.zeros((BLK, 128), BF)
    for b in range(8):
        k = k_ref[b * BLK : (b + 1) * BLK, :]
        v = v_ref[b * BLK : (b + 1) * BLK, :]
        k_even, k_odd = key_sides(k, tab[12 + b])
        ka_e[b] = k_even
        ka_o[b] = k_odd
        vb_e[b] = jnp.where(low, v, v_extra)
        vb_o[b] = jnp.where(low, v_extra, v)
        kt_s[b] = k.T
        dk_s[b] = jnp.zeros((BLK, 128), F32)
        dv_s[b] = jnp.zeros((BLK, 128), F32)
    for i in range(3):
        rows = slice(i * BLK, (i + 1) * BLK)
        d_out = do_ref[rows, :]
        product = d_out.astype(F32) * o_ref[rows, :].astype(F32)
        qas = (qe_ref[rows, :], qo_ref[rows, :])
        sides = []
        for head in range(2):
            mine = low if head == 0 else jnp.logical_not(low)
            delta = jnp.sum(jnp.where(mine, product, 0.0), -1, keepdims=True)
            high, mid, small = split_three(-delta)
            extra = jnp.where(place == 0, high, jnp.where(place == 1, mid, jnp.where(place == 2, small, zero)))
            sides.append((jnp.where(mine, d_out, extra), jnp.where(mine, d_out, zero), jnp.where(mine, qas[head], zero)))
        dqt = [None, None]
        for j in range(4):
            b = tab[4 * i + j]
            dv_part = None
            dk_part = None
            for head, (ka, vb) in enumerate(((ka_e, vb_e), (ka_o, vb_o))):
                d_aug, d_only, q_only = sides[head]
                probs = jnp.exp(dot_nt(ka[b], qas[head]))
                d_probs = dot_nt(vb[b], d_aug)
                d_scores = (probs * d_probs).astype(BF)
                v_add = dot_nn(probs.astype(BF), d_only)
                k_add = dot_nn(d_scores, q_only)
                dv_part = v_add if dv_part is None else dv_part + v_add
                dk_part = k_add if dk_part is None else dk_part + k_add
                q_add = dot_nn(kt_s[b, head * HDIM : (head + 1) * HDIM, :], d_scores)
                dqt[head] = q_add if dqt[head] is None else dqt[head] + q_add
            dv_s[b] += dv_part
            dk_s[b] += dk_part
        dq_ref[rows, :] = (jnp.concatenate(dqt, 0).T * 0.125).astype(BF)
    for b in range(8):
        dk = dk_s[b].astype(BF)
        dv = dv_s[b].astype(BF)
        dk_ref[b * BLK : (b + 1) * BLK, :] = dk
        dv_ref[b * BLK : (b + 1) * BLK, :] = dv
        dkv_s[b * BLK : (b + 1) * BLK, :128] = dk
        dkv_s[b * BLK : (b + 1) * BLK, 128:] = dv
    dq_all = dq_ref[...]
    db_ref[0:1, :] = jnp.sum(dq_all.astype(F32), 0, keepdims=True)
    db_ref[1:2, :] = jnp.sum(dkv_s[:, 128:].astype(F32), 0, keepdims=True)
    dw_q = dot_nn(xt_ref[:, :ROWS], dq_all).astype(BF)
    dw_kv = dot_nn(xt_ref[...], dkv_s[...]).astype(BF)
    for n, grad in enumerate((dw_q, dw_kv[:, :128], dw_kv[:, 128:])):
        grad = grad.reshape(RB // 2, 2, RP, 128)
        for pos in range(RB // 2):
            keep_ref[pos ^ tab[21], n] = jnp.where(tab[20] == 0, grad[pos, 0], grad[pos, 1])
            give_ref[pos ^ tab[21], n] = jnp.where(tab[20] == 0, grad[pos, 1], grad[pos, 0])


def gelu_both(pre):
    size = jnp.abs(pre)
    bell = jnp.exp(pre * pre * -0.5)
    t = 1.0 / (1.0 + size * (0.3275911 * math.sqrt(0.5)))
    poly = t * (
        0.5 * 0.254829592
        + t * (0.5 * -0.284496736 + t * (0.5 * 1.421413741 + t * (0.5 * -1.453152027 + t * (0.5 * 1.061405429))))
    )
    tail = poly * bell
    phi = jnp.where(pre >= 0, 1.0 - tail, tail)
    return pre * phi, phi + pre * bell * (1.0 / math.sqrt(2.0 * math.pi))


def norm_parts(summed):
    average = jnp.mean(summed, -1, keepdims=True)
    centered = summed - average
    variance = jnp.mean(centered * centered, -1, keepdims=True)
    root = lax.rsqrt(variance + LN_EPS)
    return centered * root, root


def norm_back(cot, gain, hat, root):
    gz = cot * gain
    return root * (gz - jnp.mean(gz, -1, keepdims=True) - hat * jnp.mean(gz * hat, -1, keepdims=True))


def feed_kernel(
    tab,
    o_ref,
    x_ref,
    *refs,
):
    pieces = refs[:8]
    (vec_ref, w_ref, cot_ref, weight_ref, u_ref, gp_ref, out_ref, dz2_ref, e2_ref, e2t_ref) = refs[8:18]
    (h1t_ref, hat1_ref, root1_ref, sums_ref, wo_s, h1_s, h1b_s, z2_s) = refs[18:]
    step = pl.program_id(0)

    @pl.when(step == 0)
    def _():
        assemble(tab, pieces, 0, wo_s, 0)
        for i in range(3):
            rows = slice(i * BLK, (i + 1) * BLK)
            z1 = x_ref[rows, :].astype(F32) + dot_nt(o_ref[rows, :], wo_s[...]) + vec_ref[2:3, :]
            hat, root = norm_parts(z1)
            h1 = hat * vec_ref[3:4, :] + vec_ref[4:5, :]
            hat1_ref[rows, :] = hat
            root1_ref[rows, :] = root
            h1_s[rows, :] = h1
            h1b = h1.astype(BF)
            h1b_s[rows, :] = h1b
            h1t_ref[:, rows] = h1b.T

    w1 = w_ref[:, 0, 0].reshape(D, D)
    w2t = w_ref[:, 0, 1].reshape(D, D)
    bias = vec_ref[pl.ds(8 + step, 1), :]
    for i in range(3):
        rows = slice(i * BLK, (i + 1) * BLK)
        pre = dot_nn(h1b_s[rows, :], w1) + bias
        act, slope = gelu_both(pre)
        act = act.astype(BF)
        u_ref[rows, :] = act
        gp_ref[rows, :] = slope.astype(BF)
        feed = dot_nt(act, w2t)

        @pl.when(step == 0)
        def _():
            z2_s[rows, :] = feed

        @pl.when(step > 0)
        def _():
            z2_s[rows, :] += feed

    @pl.when(step == 3)
    def _():
        sums = [jnp.zeros((1, D), F32) for _ in range(3)]
        for i in range(3):
            rows = slice(i * BLK, (i + 1) * BLK)
            z2 = h1_s[rows, :] + z2_s[rows, :] + vec_ref[5:6, :]
            hat, root = norm_parts(z2)
            out_ref[rows, :] = (hat * vec_ref[6:7, :] + vec_ref[7:8, :]).astype(BF)
            cot = cot_ref[rows, :].astype(F32) * weight_ref[rows, :]
            dz2 = norm_back(cot, vec_ref[6:7, :], hat, root)
            dz2_ref[rows, :] = dz2
            e2 = dz2.astype(BF)
            e2_ref[rows, :] = e2
            e2t_ref[:, rows] = e2.T
            sums[0] += jnp.sum(dz2, 0, keepdims=True)
            sums[1] += jnp.sum(cot * hat, 0, keepdims=True)
            sums[2] += jnp.sum(cot, 0, keepdims=True)
        for n in range(3):
            sums_ref[n : n + 1, :] = sums[n]


def feed_back_kernel(
    tab,
    e2_ref,
    e2t_ref,
    h1t_ref,
    u_ref,
    gp_ref,
    w_ref,
    dz2_ref,
    hat1_ref,
    root1_ref,
    o_ref,
    *refs,
):
    pieces = refs[:8]
    vec_ref, dw_ref, dz1_ref, do_ref, sums_ref, db1_ref, ep_s, dh_s, wo_s, e1t_s = refs[8:]
    step = pl.program_id(0)
    @pl.when(step < 4)
    def _():
        w1 = w_ref[:, 0, 0].reshape(D, D)
        w2t = w_ref[:, 0, 1].reshape(D, D)
        db1 = jnp.zeros((1, D), F32)
        for i in range(3):
            rows = slice(i * BLK, (i + 1) * BLK)
            du = dot_nn(e2_ref[rows, :], w2t)
            ep = (gp_ref[rows, :].astype(F32) * du).astype(BF)
            ep_s[rows, :] = ep
            db1 += jnp.sum(ep.astype(F32), 0, keepdims=True)
            back = dot_nt(ep, w1)

            @pl.when(step == 0)
            def _():
                dh_s[rows, :] = back + dz2_ref[rows, :]

            @pl.when(step > 0)
            def _():
                dh_s[rows, :] += back

        db1_ref[pl.ds(step, 1), :] = db1
        dw_ref[:, 0, 0] = dot_nn(h1t_ref[...], ep_s[...]).astype(BF).reshape(RB, RP, D)
        dw_ref[:, 0, 1] = dot_nn(e2t_ref[...], u_ref[...]).astype(BF).reshape(RB, RP, D)

    @pl.when(step == 4)
    def _():
        assemble(tab, pieces, 0, wo_s, 0)
        sums = [jnp.zeros((1, D), F32) for _ in range(3)]
        for i in range(3):
            rows = slice(i * BLK, (i + 1) * BLK)
            dh = dh_s[rows, :]
            hat = hat1_ref[rows, :]
            dz1 = norm_back(dh, vec_ref[3:4, :], hat, root1_ref[rows, :])
            dz1_ref[rows, :] = dz1
            e1 = dz1.astype(BF)
            e1t_s[:, rows] = e1.T
            do_ref[rows, :] = dot_nn(e1, wo_s[...]).astype(BF)
            sums[0] += jnp.sum(dz1, 0, keepdims=True)
            sums[1] += jnp.sum(dh * hat, 0, keepdims=True)
            sums[2] += jnp.sum(dh, 0, keepdims=True)
        for n in range(3):
            sums_ref[n : n + 1, :] = sums[n]
        dw_ref[:, 0, 0] = dot_nn(e1t_s[...], o_ref[...]).astype(BF).reshape(RB, RP, D)
        dw_ref[:, 0, 1] = jnp.zeros((RB, RP, D), BF)


def pack_kernel(tab, own_ref, *rest):
    others, out_ref, line_s = rest[:-2], rest[-2], rest[-1]
    line_s[0] = own_ref[...]
    for n, ref in enumerate(others):
        line_s[n + 1] = ref[...]
    width = own_ref.shape[-1] // 4
    for m in range(4):
        shard = line_s[m ^ tab[0]]
        for n in range(4):
            out_ref[n, :, m * width : (m + 1) * width] = shard[:, n * width : (n + 1) * width]


def input_rest_kernel(tab, dk_ref, dv_ref, *refs):
    pieces, (nb_ref, mid_ref, w_s) = refs[:8], refs[8:]
    step = pl.program_id(0)

    @pl.when(step == 0)
    def _():
        for part in range(2):
            assemble(tab, pieces, part + 1, w_s, D * part)

    back = (dot_nt(dk_ref[...], w_s[:, :D]) + dot_nt(dv_ref[...], w_s[:, D:])).astype(BF)

    @pl.when(step < 3)
    def _():
        nb_ref[...] = back

    @pl.when(step >= 3)
    def _():
        mid_ref[...] = back


def input_own_kernel(tab, dq_ref, dk_ref, dv_ref, *refs):
    pieces, (dz1_ref, own_ref, w_s) = refs[:8], refs[8:]

    @pl.when(pl.program_id(0) == 0)
    def _():
        for part in range(3):
            assemble(tab, pieces, part, w_s, D * part)

    back = dot_nt(dk_ref[...], w_s[:, D : 2 * D]) + dot_nt(dv_ref[...], w_s[:, 2 * D :])
    own_ref[...] = back + dot_nt(dq_ref[...], w_s[:, :D]) + dz1_ref[...]


def line_kernel(tab, own_ref, *refs):
    chips, (feed_ref, *outs) = refs[:-5], refs[-5:]
    total = own_ref[...].astype(F32)
    for ref in chips:
        total = total + ref[...].astype(F32)
    total = total.astype(BF)
    width = total.shape[-1] // 4
    for n in range(4):
        m = n ^ tab[0]
        outs[n][:, :D] = feed_ref[m, 0]
        outs[n][:, D : 2 * D] = feed_ref[m, 1]
        for other in range(4):

            @pl.when(m == other)
            def _():
                at = slice(other * width, (other + 1) * width)
                for kind in range(3):
                    outs[n][:, 2 * D + kind * width : 2 * D + (kind + 1) * width] = total[kind, :, at]
                outs[n][:, 2 * D + 3 * width :] = feed_ref[4, 0, :, at]


def call(kernel, grid, in_specs, out_specs, out_shape, scratch, flops, bytes_accessed, name):
    return pl.pallas_call(
        kernel,
        grid_spec=pltpu.PrefetchScalarGridSpec(
            num_scalar_prefetch=1, grid=(grid,), in_specs=in_specs, out_specs=out_specs, scratch_shapes=scratch
        ),
        out_shape=out_shape,
        compiler_params=pltpu.CompilerParams(
            dimension_semantics=("arbitrary",), vmem_limit_bytes=VMEM_LIMIT
        ),
        cost_estimate=pl.CostEstimate(flops=flops, bytes_accessed=bytes_accessed, transcendentals=0),
        name=name,
    )


def whole(*shape):
    return pl.BlockSpec(shape, lambda s, t: (0,) * len(shape))


def columns(rows, width=128):
    return pl.BlockSpec((rows, width), lambda s, t: (0, s))


def shape_of(shape, dtype):
    return jax.ShapeDtypeStruct(shape, dtype)


def vm(shape, dtype):
    return pltpu.VMEM(shape, dtype)


def attend(tab, own, nb, mid, pieces, vectors):
    w_spec = pl.BlockSpec((3, RP, 128), lambda s, t: (0, 0, s))
    return call(
        attend_kernel,
        PAIRS,
        [whole(ROWS, D), whole(ROWS, D), whole(2 * BLK, D)] + [w_spec] * 8 + [columns(12)],
        [columns(ROWS), columns(ROWS), columns(ROWS), columns(8 * BLK), columns(8 * BLK)]
        + [pl.BlockSpec((128, 8 * BLK), lambda s, t: (s, 0))],
        [shape_of((ROWS, D), BF)] * 3 + [shape_of((8 * BLK, D), BF)] * 2 + [shape_of((D, 8 * BLK), BF)],
        [vm((D, 384), BF)] + [vm((8, BLK, 128), BF)] * 4,
        5_000_000_000,
        16_000_000,
        "attend",
    )(tab, own, nb, mid, *pieces, vectors)


def attend_back(tab, qe, qo, k, v, d_out, o, xt):
    return call(
        attend_back_kernel,
        PAIRS,
        [columns(ROWS), columns(ROWS), columns(8 * BLK), columns(8 * BLK), columns(ROWS), columns(ROWS), whole(D, 8 * BLK)],
        [
            columns(ROWS),
            columns(8 * BLK),
            columns(8 * BLK),
            pl.BlockSpec((RB // 2, 3, RP, 128), lambda s, t: (0, 0, 0, s)),
            pl.BlockSpec((RB // 2, 3, RP, 128), lambda s, t: (0, 0, 0, s)),
            columns(2),
        ],
        [
            shape_of((ROWS, D), BF),
            shape_of((8 * BLK, D), BF),
            shape_of((8 * BLK, D), BF),
            shape_of((RB // 2, 3, RP, D), BF),
            shape_of((RB // 2, 3, RP, D), BF),
            shape_of((2, D), F32),
        ],
        [vm((8, BLK, 128), BF)] * 4
        + [vm((8, 128, BLK), BF)]
        + [vm((8, BLK, 128), F32)] * 2
        + [vm((8 * BLK, BLK), BF)],
        50_000_000_000,
        24_000_000,
        "attend_back",
    )(tab, qe, qo, k, v, d_out, o, xt)


def feed(tab, o, x, pieces, vectors, w, cot, weight):
    wo_spec = pl.BlockSpec((1, RP, D), lambda s, t: (3, 0, 0))
    return call(
        feed_kernel,
        4,
        [
            whole(ROWS, D),
            whole(ROWS, D),
            *[wo_spec] * 8,
            whole(12, D),
            pl.BlockSpec((RB, 1, 2, RP, D), lambda s, t: (0, s, 0, 0, 0)),
            whole(ROWS, D),
            whole(ROWS, 1),
        ],
        [
            columns(ROWS, D),
            columns(ROWS, D),
            whole(ROWS, D),
            whole(ROWS, D),
            whole(ROWS, D),
            whole(D, ROWS),
            whole(D, ROWS),
            whole(ROWS, D),
            whole(ROWS, 1),
            whole(3, D),
        ],
        [
            shape_of((ROWS, FF), BF),
            shape_of((ROWS, FF), BF),
            shape_of((ROWS, D), BF),
            shape_of((ROWS, D), F32),
            shape_of((ROWS, D), BF),
            shape_of((D, ROWS), BF),
            shape_of((D, ROWS), BF),
            shape_of((ROWS, D), F32),
            shape_of((ROWS, 1), F32),
            shape_of((3, D), F32),
        ],
        [vm((D, D), BF), vm((ROWS, D), F32), vm((ROWS, D), BF), vm((ROWS, D), F32)],
        18_000_000_000,
        40_000_000,
        "feed",
    )(tab, o, x, *pieces, vectors, w, cot, weight)


def feed_back(tab, e2, e2t, h1t, u, gp, w, dz2, hat1, root1, o, pieces, vectors):
    wo_spec = pl.BlockSpec((1, RP, D), lambda s, t: (3, 0, 0))

    def late(s):
        return jnp.minimum(s, 3)

    return call(
        feed_back_kernel,
        5,
        [
            whole(ROWS, D),
            whole(D, ROWS),
            whole(D, ROWS),
            pl.BlockSpec((ROWS, D), lambda s, t: (0, late(s))),
            pl.BlockSpec((ROWS, D), lambda s, t: (0, late(s))),
            pl.BlockSpec((RB, 1, 2, RP, D), lambda s, t: (0, late(s), 0, 0, 0)),
            whole(ROWS, D),
            whole(ROWS, D),
            whole(ROWS, 1),
            whole(ROWS, D),
            *[wo_spec] * 8,
            whole(12, D),
        ],
        [
            pl.BlockSpec((RB, 1, 2, RP, D), lambda s, t: (0, s, 0, 0, 0)),
            whole(ROWS, D),
            whole(ROWS, D),
            whole(3, D),
            whole(4, D),
        ],
        [
            shape_of((RB, 5, 2, RP, D), BF),
            shape_of((ROWS, D), F32),
            shape_of((ROWS, D), BF),
            shape_of((3, D), F32),
            shape_of((4, D), F32),
        ],
        [vm((ROWS, D), BF), vm((ROWS, D), F32), vm((D, D), BF), vm((D, ROWS), BF)],
        24_000_000_000,
        48_000_000,
        "feed_back",
    )(tab, e2, e2t, h1t, u, gp, w, dz2, hat1, root1, o, *pieces, vectors)


def round_kernel(qkv_ref, proj_ref, up_ref, down_ref, mine_ref, feed_ref):
    width = qkv_ref.shape[-1]
    for n in range(3):
        mine_ref[:, n * width : (n + 1) * width] = qkv_ref[n].astype(BF)
    mine_ref[:, 3 * width :] = proj_ref[...].T.astype(BF)
    feed_ref[0] = up_ref[...].astype(BF)
    feed_ref[1] = down_ref[...].astype(BF)


def round_shards(qkv, proj, up, down):
    rows = up.shape[0]
    return pl.pallas_call(
        round_kernel,
        in_specs=[pl.BlockSpec(memory_space=pltpu.VMEM)] * 4,
        out_specs=[pl.BlockSpec(memory_space=pltpu.VMEM)] * 2,
        out_shape=[shape_of((rows, D), BF), shape_of((2, rows, D), BF)],
        cost_estimate=pl.CostEstimate(flops=1_000_000, bytes_accessed=1_500_000, transcendentals=0),
        name="round_shards",
    )(qkv, proj, up, down)


def pack_line(z, own, others):
    rows, width = own.shape
    return call(
        pack_kernel,
        1,
        [whole(rows, width)] * 4,
        whole(4, rows, D),
        shape_of((4, rows, D), BF),
        [vm((4, rows, width), BF)],
        60_000_000_000,
        1_000_000,
        "pack_line",
    )(z.reshape(1).astype(jnp.int32), own, *others)


def input_rest(tab, dk, dv, pieces):
    w_spec = whole(3, RP, D)
    each = pl.BlockSpec((BLK, D), lambda s, t: (s + 3, 0))
    return call(
        input_rest_kernel,
        5,
        [each, each] + [w_spec] * 8,
        [
            pl.BlockSpec((BLK, D), lambda s, t: (jnp.minimum(s, 2), 0)),
            pl.BlockSpec((BLK, D), lambda s, t: (jnp.maximum(s - 3, 0), 0)),
        ],
        [shape_of((3 * BLK, D), BF), shape_of((2 * BLK, D), BF)],
        [vm((D, 2 * D), BF)],
        8_000_000_000,
        12_000_000,
        "input_rest",
    )(tab, dk, dv, *pieces)


def input_own(tab, dq, dk, dv, pieces, dz1):
    w_spec = whole(3, RP, D)
    each = pl.BlockSpec((BLK, D), lambda s, t: (s, 0))
    return call(
        input_own_kernel,
        3,
        [each, each, each] + [w_spec] * 8 + [each],
        each,
        shape_of((ROWS, D), F32),
        [vm((D, 3 * D), BF)],
        5_000_000_000,
        12_000_000,
        "input_own",
    )(tab, dq, dk, dv, *pieces, dz1)


def line_parts(z, own, others, fed):
    rows = own.shape[1]
    return call(
        line_kernel,
        1,
        [whole(3, rows, D)] * (1 + len(others)) + [whole(5, 2, rows, D)],
        [whole(rows, 3 * D)] * 4,
        [shape_of((rows, 3 * D), BF)] * 4,
        [],
        2_000_000,
        4_000_000,
        "line_parts",
    )(z.reshape(1).astype(jnp.int32), own, *others, fed)


def adamw(weight, clipped, first, second, rate, decay):
    first_new = BETA_ONE * first + (1.0 - BETA_ONE) * clipped
    second_new = BETA_TWO * second + (1.0 - BETA_TWO) * clipped * clipped
    first_hat = first_new / (1.0 - BETA_ONE**STEP)
    second_hat = second_new / (1.0 - BETA_TWO**STEP)
    updated = weight * (1.0 - rate * decay) - rate * first_hat / (jnp.sqrt(second_hat) + ADAM_EPS)
    return (clipped, first_new, second_new, updated)


def update_kernel(clip_ref, sum_ref, vec_ref, *refs):
    ins, outs = refs[:15], refs[15:]
    clip = clip_ref[0, 0]
    sums = sum_ref[...]
    width = D // 4
    grads = (
        [sums[:, 2 * D + n * width : 2 * D + (n + 1) * width] for n in range(3)],
        [sums[:, 2 * D + 3 * width :].T],
        [sums[:, :D]],
        [sums[:, D : 2 * D]],
        [vec_ref[...]],
    )
    for kind, parts in enumerate(grads):
        rate, decay = (VECTOR_RATE, 0.0) if kind == 4 else (MATRIX_RATE / math.sqrt(D), WEIGHT_DECAY)
        for n, grad in enumerate(parts):
            at = n if kind == 0 else Ellipsis
            results = adamw(ins[kind][at], grad * clip, ins[5 + kind][at], ins[10 + kind][at], rate, decay)
            for m, result in enumerate(results):
                outs[4 * kind + m][at] = result


def update(clip, sums, vec, weights, firsts, seconds):
    shapes = [shape_of(one.shape, F32) for one in weights for _ in range(4)]
    return pl.pallas_call(
        update_kernel,
        in_specs=[pl.BlockSpec(memory_space=pltpu.SMEM)] + [pl.BlockSpec(memory_space=pltpu.VMEM)] * 17,
        out_specs=[pl.BlockSpec(memory_space=pltpu.VMEM)] * 20,
        out_shape=shapes,
        compiler_params=pltpu.CompilerParams(vmem_limit_bytes=VMEM_LIMIT),
        cost_estimate=pl.CostEstimate(flops=10_000_000, bytes_accessed=8_000_000, transcendentals=0),
        name="update",
    )(clip, sums, vec, *weights, *firsts, *seconds)


def total_kernel(vec_ref, *refs):
    parts, (sum_out, square_out) = refs[:4], refs[4:]
    sums = parts[0][...].astype(F32)
    for ref in parts[1:]:
        sums = sums + ref[...].astype(F32)
    sum_out[...] = sums
    vec = vec_ref[...]
    square_out[0, 0] = jnp.sum(sums * sums) + jnp.sum(vec * vec)


def total(vec, parts):
    vmem = pl.BlockSpec(memory_space=pltpu.VMEM)
    return pl.pallas_call(
        total_kernel,
        in_specs=[vmem] * 5,
        out_specs=[vmem, pl.BlockSpec(memory_space=pltpu.SMEM)],
        out_shape=[shape_of(parts[0].shape, F32), shape_of((1, 1), F32)],
        compiler_params=pltpu.CompilerParams(vmem_limit_bytes=VMEM_LIMIT),
        cost_estimate=pl.CostEstimate(flops=2_000_000, bytes_accessed=4_000_000, transcendentals=0),
        name="total",
    )(vec, *parts)


def shards(
    tokens,
    out_cotangent,
    lengths,
    starts,
    ends,
    flags,
    qkv_master,
    proj_master,
    up_master,
    down_master,
    vectors,
    qkv_first,
    proj_first,
    up_first,
    down_first,
    qkv_second,
    proj_second,
    up_second,
    down_second,
    vector_first,
    vector_second,
):
    mp_count = lax.axis_size("mp")
    dp_count = lax.axis_size("dp")
    devices = mp_count * dp_count
    z = lax.axis_index("mp")
    dp_index = lax.axis_index("dp")
    core = dp_index % 2
    chips = dp_count // 2
    part = D // dp_count
    head_cols = D // mp_count

    def linear(chip, core_of, z_of):
        return (chip * 2 + core_of) * mp_count + z_of

    def permutation(move):
        return [
            (linear(chip, c, k), linear(*move(chip, c, k)))
            for chip in range(chips)
            for c in range(2)
            for k in range(mp_count)
        ]

    planes = [[linear(chip, c, k) for chip in range(chips)] for c in range(2) for k in range(mp_count)]
    swap_core = permutation(lambda chip, c, k: (chip, 1 - c, k))
    swap_z = [permutation(lambda chip, c, k, n=n: (chip, c, k ^ n)) for n in range(mp_count)]
    swap_chip = [permutation(lambda chip, c, k, n=n: (chip ^ n, c, k)) for n in range(chips)]
    middle = (0, 2, 1, 3)
    swap_mid = permutation(lambda chip, c, k: (chip, c, middle[k]))
    chip_index = dp_index // 2

    def over_plane(value):
        return lax.all_to_all(value, AXES, 0, 0, tiled=True, axis_index_groups=planes)

    def over_z(value):
        return lax.all_to_all(value, "mp", 0, 0, tiled=True)

    def absolute(same, other):
        order = jnp.arange(chips, dtype=jnp.int32) ^ chip_index
        same, other = jnp.stack(same)[order], jnp.stack(other)[order]
        both = jnp.where(core == 0, jnp.stack([same, other], 1), jnp.stack([other, same], 1))
        kinds = both.shape[2]
        both = both.transpose(2, 0, 1, 3, 4).reshape(kinds, RB // 2, 2, RP, D).transpose(1, 2, 0, 3, 4)
        return [both[n, half] for half in range(2) for n in range(RB // 2)]

    mine, feed_mine = round_shards(qkv_master, proj_master, up_master, down_master.T)
    feed_w = lax.all_gather(feed_mine, AXES, axis=0, tiled=False).reshape(dp_count, mp_count, 2, part, D)
    line = [lax.ppermute(mine, AXES, swap_z[n]) for n in range(1, mp_count)]
    tokens_late, mine, *line = lax.optimization_barrier((tokens, mine, *line))
    along_z = pack_line(z, mine, line)
    mid_at = jnp.where(z == 1, BLK, 0)
    nb = lax.ppermute(tokens_late, AXES, swap_z[1])
    mid = lax.ppermute(lax.dynamic_slice_in_dim(tokens_late, mid_at, 2 * BLK, 0), AXES, swap_mid)
    same = [along_z] + [lax.ppermute(along_z, AXES, swap_chip[n]) for n in range(1, chips)]
    first, same[1] = lax.optimization_barrier((along_z, same[1]))
    other = [lax.ppermute(one, AXES, swap_core) for one in [first] + same[1:]]
    pieces = same + other
    kernel_core, kernel_chip = core, chip_index
    if part != RP:
        pieces = absolute(same, other)
        feed_w = feed_w.transpose(1, 2, 0, 3, 4).reshape(mp_count, 2, RB, RP, D).transpose(2, 0, 1, 3, 4)
        kernel_core = kernel_chip = jnp.zeros((), jnp.int32)

    place = jnp.asarray(BLOCK_PLACE)[z]
    counts = jnp.clip(lengths[jnp.asarray(BLOCK_SEQ)[z]] - BLK * place, 0, BLK)
    tab = jnp.concatenate(
        [jnp.asarray(KEY_BLOCKS)[z].reshape(12), counts, kernel_core.reshape(1), kernel_chip.reshape(1)]
    ).astype(jnp.int32)

    positions = z * ROWS + jnp.arange(ROWS, dtype=jnp.int32)
    seq_of = positions // LEN
    within = positions % LEN
    picker = (seq_of[:, None] == jnp.arange(lengths.shape[0], dtype=jnp.int32)[None, :]).astype(jnp.int32)
    length_row = jnp.sum(picker * lengths[None, :], 1)
    start_row = jnp.sum(picker * starts[None, :], 1)
    end_row = jnp.sum(picker * ends[None, :], 1)
    flag_row = jnp.sum(picker * flags[None, :], 1).astype(F32)
    valid_row = (within < length_row).astype(F32)
    answer = (within == start_row).astype(F32) + (within == end_row).astype(F32)
    opening = (within == 0).astype(F32)
    row_weight = valid_row * (1.0 + 2.0 * (1.0 - flag_row) * answer + 4.0 * flag_row * opening)

    o, qe, qo, k, v, xt = attend(tab, tokens, nb, mid, pieces, vectors)
    u, gp, block_out, dz2, e2, e2t, h1t, hat1, root1, sums_two = feed(
        tab, o, tokens, pieces, vectors, feed_w, out_cotangent, row_weight[:, None]
    )

    def to_parts(grad):
        if part == RP:
            return grad
        lead = grad.shape[1:-2]
        moved = jnp.moveaxis(grad, 0, -3).reshape(*lead, dp_count, part, D)
        return jnp.moveaxis(moved, -3, 0)

    feed_dw, dz1, d_o, sums_one, bias_up_grad = feed_back(
        tab, e2, e2t, h1t, u, gp, feed_w, dz2, hat1, root1, o, pieces, vectors
    )
    feed_part = lax.psum_scatter(to_parts(feed_dw), "dp", scatter_dimension=0, tiled=False)

    dq, dk, dv, keep, give, sums_head = attend_back(tab, qe, qo, k, v, d_o, o, xt)
    if part != RP:
        both = jnp.stack([keep, give], 1).reshape(RB, 3, RP, D)
        both = to_parts(both).reshape(chips, 2, 3, part, D)
        order = jnp.arange(chips, dtype=jnp.int32) ^ chip_index
        keep = lax.dynamic_index_in_dim(both, core, 1, keepdims=False)[order]
        give = lax.dynamic_index_in_dim(both, 1 - core, 1, keepdims=False)[order]
    got = lax.ppermute(give, AXES, swap_core)
    chip_sum = (keep.astype(F32) + got.astype(F32)).astype(BF)
    to_nb, to_mid = input_rest(tab, dk, dv, pieces)
    chip_sum, dq, dk, dv, sums_head, to_nb, to_mid = lax.optimization_barrier(
        (chip_sum, dq, dk, dv, sums_head, to_nb, to_mid)
    )
    from_chips = [lax.ppermute(chip_sum[n], AXES, swap_chip[n]) for n in range(1, chips)]
    from_nb = lax.ppermute(to_nb, AXES, swap_z[1])
    from_mid = lax.ppermute(to_mid, AXES, swap_mid)
    dx_own = input_own(tab, dq, dk, dv, pieces, dz1)
    vector_part = jnp.concatenate([sums_head, sums_one, sums_two, bias_up_grad], 0)
    vec_columns = D // devices
    vector_part = vector_part.reshape(12, devices, vec_columns).transpose(1, 0, 2)
    vector_grad = jnp.sum(lax.all_to_all(vector_part, AXES, 0, 0, tiled=True), 0)
    vector_grad, feed_part, dx_own, from_nb, from_mid, *from_chips = lax.optimization_barrier(
        (vector_grad, feed_part, dx_own, from_nb, from_mid, *from_chips)
    )
    line_own, *line_rest = line_parts(z, chip_sum[0], from_chips, feed_part)
    line_rest = [lax.ppermute(one, AXES, swap_z[n + 1]) for n, one in enumerate(line_rest)]
    zero_block = jnp.zeros((BLK, D), BF)
    from_mid = jnp.where(
        z == 1, jnp.concatenate([zero_block, from_mid], 0), jnp.concatenate([from_mid, zero_block], 0)
    )
    input_grad = dx_own + from_nb.astype(F32) + from_mid.astype(F32)

    sums, local_squares = total(vector_grad, [line_own] + line_rest)
    squares = lax.all_to_all(jnp.broadcast_to(local_squares.reshape(1), (devices,)), AXES, 0, 0, tiled=True)
    grad_norm = jnp.sqrt(jnp.sum(squares))
    clip_factor = jnp.minimum(1.0, CLIP_NORM / (grad_norm + 1e-06))
    vec_index = dp_index * mp_count + z
    vector_shard = lax.dynamic_slice_in_dim(vectors, vec_index * vec_columns, vec_columns, 1)
    results = update(
        clip_factor.reshape(1, 1),
        sums,
        vector_grad,
        (qkv_master, proj_master, up_master, down_master.T, vector_shard),
        (qkv_first, proj_first, up_first, down_first.T, vector_first),
        (qkv_second, proj_second, up_second, down_second.T, vector_second),
    )
    down_set = [one.T for one in results[12:16]]
    return (block_out, input_grad, grad_norm, *results[:12], *down_set, *results[16:])


def solution(mesh):
    rows = P(AXES, None)
    group = P("dp")
    qkv = P(None, "dp", "mp")
    proj = P("mp", "dp")
    up = P("dp", "mp")
    vec = P(None, AXES)
    return jax.shard_map(
        shards,
        mesh=mesh,
        in_specs=(rows, rows, group, group, group, group)
        + (qkv, proj, up, proj, P())
        + (qkv, proj, up, proj) * 2
        + (vec, vec),
        out_specs=(rows, rows, P()) + (qkv,) * 4 + (proj,) * 4 + (up,) * 4 + (proj,) * 4 + (vec,) * 4,
        check_vma=False,
    )
```

```python
from functools import partial
import math

import jax
import jax.numpy as jnp
import numpy as np
from jax import lax
from jax.experimental import pallas as pl
from jax.experimental.pallas import tpu as pltpu
from jax.sharding import PartitionSpec as P

D = 768
HEADS = 12
HDIM = 64
FF = 3072
LEN = 1024
STEP = 10

LN_EPS = 1e-06
BETA_ONE = 0.9
BETA_TWO = 0.999
ADAM_EPS = 1e-08
WEIGHT_DECAY = 0.01
CLIP_NORM = 1.0
VECTOR_RATE = 1.0
MATRIX_RATE = 2.0
NEG_FILL = -1e30

BF = jnp.bfloat16
F32 = jnp.float32
AXES = ("dp", "mp")
BLK = 256
ROWS = 768
PAIRS = HEADS // 2
RB = 8
RP = D // RB
VMEM_LIMIT = 60 * 1024 * 1024

KEY_BLOCKS = np.array(
    [
        [[0, 1, 2, 3]] * 3,
        [[3, 4, 5, 0], [1, 2, 6, 7], [1, 2, 6, 7]],
        [[6, 7, 0, 1], [6, 7, 0, 1], [2, 3, 4, 5]],
        [[5, 0, 1, 2]] * 3,
    ],
    np.int32,
)
BLOCK_SEQ = np.array(
    [[0, 0, 0, 0, 0, 0, 0, 0], [0, 1, 1, 0, 0, 0, 1, 1], [1, 1, 2, 2, 2, 2, 1, 1], [2, 2, 2, 2, 2, 2, 2, 2]], np.int32
)
BLOCK_PLACE = np.array(
    [[0, 1, 2, 3, 4, 4, 4, 4], [3, 0, 1, 0, 1, 2, 2, 3], [2, 3, 0, 1, 2, 3, 0, 1], [1, 2, 3, 4, 4, 0, 4, 4]], np.int32
)


def dot_nn(left, right):
    return jnp.dot(left, right, preferred_element_type=F32)


def dot_nt(left, right):
    return lax.dot_general(left, right, (((1,), (1,)), ((), ())), preferred_element_type=F32)


def lane_ids(rows):
    return lax.broadcasted_iota(jnp.int32, (rows, 128), 1)


def assemble(tab, pieces, part, target, col):
    width = pieces[0].shape[-1]
    core, chip = tab[20], tab[21]
    for n in range(4):
        for half in range(2):
            at = ((n ^ chip) * 2 + (core ^ half)) * RP
            target[pl.ds(pl.multiple_of(at, RP), RP), col : col + width] = pieces[4 * half + n][part]


def key_extra(count):
    place = lane_ids(BLK) % HDIM
    row = lax.broadcasted_iota(jnp.int32, (BLK, 128), 0)
    mask = jnp.where(row >= count, NEG_FILL, 0.0)
    return jnp.where(place == 0, mask, jnp.where(place <= 3, 1.0, 0.0)).astype(BF)


def split_three(value):
    high = value.astype(BF)
    rest = value - high.astype(F32)
    mid = rest.astype(BF)
    low = (rest - mid.astype(F32)).astype(BF)
    return high, mid, low


def attend_kernel(
    tab, own_ref, nb_ref, mid_ref, *refs
):
    pieces = refs[:8]
    vec_ref, o_ref, qe_ref, qo_ref, k_ref, v_ref, xt_ref, w_s, ka_e, ka_o, va_s, extra_s = refs[8:]
    mine = pl.ds(pl.multiple_of(pl.program_id(0) * 128, 128), 128)

    @pl.when(pl.program_id(0) == 0)
    def _():
        for b in range(8):
            extra_s[b] = key_extra(tab[12 + b])

    for part in range(3):
        assemble(tab, pieces, part, w_s, 128 * part)
    bias_q = vec_ref[0:1, :]
    bias_v = vec_ref[1:2, :]
    low = lane_ids(BLK) < HDIM
    place = lane_ids(BLK) % HDIM
    ones = jnp.ones((BLK, 128), BF)
    for src, first, count in ((own_ref, 0, 3), (nb_ref, 3, 3), (mid_ref, 6, 2)):
        at = slice(first * BLK, (first + count) * BLK)
        xt_ref[:, at] = src[:, mine].T
        kv = dot_nn(src[...], w_s[:, 128:384])
        k_ref[at, :] = kv[:, :128].astype(BF)
        v_ref[at, :] = (kv[:, 128:] + bias_v).astype(BF)
    for b in range(8):
        at = slice(b * BLK, (b + 1) * BLK)
        k = k_ref[at, :]
        ka_e[b] = jnp.where(low, k, extra_s[b])
        ka_o[b] = jnp.where(low, extra_s[b], k)
        va_s[0, b] = jnp.where(low, v_ref[at, :], ones)
        va_s[1, b] = jnp.where(low, ones, v_ref[at, :])
    q_extra = jnp.where(place == 0, 1.0, 0.0).astype(BF)
    queries = []
    for i in range(3):
        q = (dot_nn(own_ref[i * BLK : (i + 1) * BLK, :], w_s[:, :128]) + bias_q).astype(BF) * jnp.asarray(0.125, BF)
        queries.append((jnp.where(low, q, q_extra), jnp.where(low, q_extra, q)))
    keys = (ka_e, ka_o)

    def score(unit, j):
        i, head = unit
        return dot_nt(queries[i][head], keys[head][tab[4 * i + j]])

    units = [(i, head) for i in range(3) for head in range(2)]
    now = [score(units[0], j) for j in range(4)]
    for n, (i, head) in enumerate(units):
        peak = jnp.max(jnp.maximum(jnp.maximum(now[0], now[1]), jnp.maximum(now[2], now[3])), -1, keepdims=True)
        acc = jnp.zeros((BLK, 128), F32)
        later = []
        for j in range(4):
            if n + 1 < len(units):
                later.append(score(units[n + 1], j))
            probs = jnp.exp(now[j] - peak).astype(BF)
            acc = acc + dot_nn(probs, va_s[head, tab[4 * i + j]])
        now = later
        rows = slice(i * BLK, (i + 1) * BLK)
        high, mid, small = split_three(-(peak + jnp.log(acc)))
        extra = jnp.where(place == 0, 1.0, 0.0).astype(BF)
        extra = jnp.where(place == 1, high, extra)
        extra = jnp.where(place == 2, mid, extra)
        extra = jnp.where(place == 3, small, extra)
        if head == 0:
            qe_ref[rows, :] = jnp.where(low, queries[i][0], extra)
            even = acc
        else:
            qo_ref[rows, :] = jnp.where(low, extra, queries[i][1])
            total = jnp.where(low, acc, even)
            value = jnp.where(low, even, acc)
            o_ref[rows, :] = (value / pltpu.roll(total, HDIM, 1)).astype(BF)


def attend_back_kernel(
    tab,
    qe_ref,
    qo_ref,
    k_ref,
    v_ref,
    do_ref,
    o_ref,
    xt_ref,
    dq_ref,
    dk_ref,
    dv_ref,
    keep_ref,
    give_ref,
    db_ref,
    ka_e,
    ka_o,
    vb_e,
    vb_o,
    extra_s,
    dk_s,
    dv_s,
    dkv_s,
):
    @pl.when(pl.program_id(0) == 0)
    def _():
        for b in range(8):
            extra_s[b] = key_extra(tab[12 + b])

    low = lane_ids(BLK) < HDIM
    place = lane_ids(BLK) % HDIM
    v_extra = jnp.where(place < 3, 1.0, 0.0).astype(BF)
    zero = jnp.zeros((BLK, 128), BF)
    for b in range(8):
        at = slice(b * BLK, (b + 1) * BLK)
        k = k_ref[at, :]
        v = v_ref[at, :]
        ka_e[b] = jnp.where(low, k, extra_s[b])
        ka_o[b] = jnp.where(low, extra_s[b], k)
        vb_e[b] = jnp.where(low, v, v_extra)
        vb_o[b] = jnp.where(low, v_extra, v)
    dk_s[...] = jnp.zeros(dk_s.shape, F32)
    dv_s[...] = jnp.zeros(dv_s.shape, F32)
    sides = ((ka_e, vb_e), (ka_o, vb_o))
    given = []
    for i in range(3):
        rows = slice(i * BLK, (i + 1) * BLK)
        d_out = do_ref[rows, :]
        product = d_out.astype(F32) * o_ref[rows, :].astype(F32)
        qas = (qe_ref[rows, :], qo_ref[rows, :])
        d_augs = []
        for head in range(2):
            mine = low if head == 0 else jnp.logical_not(low)
            delta = jnp.sum(jnp.where(mine, product, 0.0), -1, keepdims=True)
            high, mid, small = split_three(-delta)
            extra = jnp.where(place == 0, high, jnp.where(place == 1, mid, jnp.where(place == 2, small, zero)))
            d_augs.append(jnp.where(mine, d_out, extra))
        given.append((qas, d_augs, d_out.T, jnp.where(low, qas[0], qas[1]).T))

    def score(unit, j):
        i, head = unit
        b = tab[4 * i + j]
        qas, d_augs = given[i][:2]
        return dot_nt(qas[head], sides[head][0][b]), dot_nt(d_augs[head], sides[head][1][b])

    units = [(i, head) for i in range(3) for head in range(2)]
    now = [score(units[0], j) for j in range(4)]
    for n, (i, head) in enumerate(units):
        lanes = slice(head * HDIM, (head + 1) * HDIM)
        dot_t, qt = given[i][2:]
        dq = jnp.zeros((BLK, 128), F32)
        later = []
        for j in range(4):
            if n + 1 < len(units):
                later.append(score(units[n + 1], j))
            b = tab[4 * i + j]
            probs = jnp.exp(now[j][0])
            d_scores = (probs * now[j][1]).astype(BF)
            dv_s[b, lanes, :] += dot_nn(dot_t[lanes, :], probs.astype(BF))
            dk_s[b, lanes, :] += dot_nn(qt[lanes, :], d_scores)
            dq = dq + dot_nn(d_scores, k_ref[pl.ds(pl.multiple_of(b * BLK, BLK), BLK), :])
        now = later
        if head == 0:
            even = dq
        else:
            dq_ref[i * BLK : (i + 1) * BLK, :] = (jnp.where(low, even, dq) * 0.125).astype(BF)
    for b in range(8):
        dk = dk_s[b].T.astype(BF)
        dv = dv_s[b].T.astype(BF)
        dk_ref[b * BLK : (b + 1) * BLK, :] = dk
        dv_ref[b * BLK : (b + 1) * BLK, :] = dv
        dkv_s[b * BLK : (b + 1) * BLK, :128] = dk
        dkv_s[b * BLK : (b + 1) * BLK, 128:] = dv
    dq_all = dq_ref[...]
    db_ref[0:1, :] = jnp.sum(dq_all.astype(F32), 0, keepdims=True)
    db_ref[1:2, :] = jnp.sum(dkv_s[:, 128:].astype(F32), 0, keepdims=True)
    dw_q = dot_nn(xt_ref[:, :ROWS], dq_all).astype(BF)
    dw_kv = dot_nn(xt_ref[...], dkv_s[...]).astype(BF)
    for n, grad in enumerate((dw_q, dw_kv[:, :128], dw_kv[:, 128:])):
        grad = grad.reshape(RB // 2, 2, RP, 128)
        for pos in range(RB // 2):
            keep_ref[pos ^ tab[21], n] = jnp.where(tab[20] == 0, grad[pos, 0], grad[pos, 1])
            give_ref[pos ^ tab[21], n] = jnp.where(tab[20] == 0, grad[pos, 1], grad[pos, 0])


def gelu_both(pre):
    size = jnp.abs(pre)
    bell = jnp.exp(pre * pre * -0.5)
    t = 1.0 / (1.0 + size * (0.3275911 * math.sqrt(0.5)))
    poly = t * (
        0.5 * 0.254829592
        + t * (0.5 * -0.284496736 + t * (0.5 * 1.421413741 + t * (0.5 * -1.453152027 + t * (0.5 * 1.061405429))))
    )
    tail = poly * bell
    phi = jnp.where(pre >= 0, 1.0 - tail, tail)
    return pre * phi, phi + pre * bell * (1.0 / math.sqrt(2.0 * math.pi))


def norm_parts(summed):
    average = jnp.mean(summed, -1, keepdims=True)
    centered = summed - average
    variance = jnp.mean(centered * centered, -1, keepdims=True)
    root = lax.rsqrt(variance + LN_EPS)
    return centered * root, root


def norm_back(cot, gain, hat, root):
    gz = cot * gain
    return root * (gz - jnp.mean(gz, -1, keepdims=True) - hat * jnp.mean(gz * hat, -1, keepdims=True))


def feed_kernel(tab, o_ref, x_ref, *refs):
    pieces = refs[:8]
    vec_ref, w_ref, cot_ref, weight_ref, out_ref, dw_ref, dz1_ref, do_ref, sums_ref, db1_ref = refs[8:18]
    wo_s, h1b_s, h1t_s, hat1_s, root1_s, z2_s, u_s, gp_s, e2_s, e2t_s, ep_s = refs[18:]
    step = pl.program_id(0)
    blocks = [slice(i * BLK, (i + 1) * BLK) for i in range(3)]

    @pl.when(step == 0)
    def _():
        assemble(tab, pieces, 0, wo_s, 0)
        for rows in blocks:
            z1 = x_ref[rows, :].astype(F32) + dot_nt(o_ref[rows, :], wo_s[...]) + vec_ref[2:3, :]
            hat, root = norm_parts(z1)
            h1 = hat * vec_ref[3:4, :] + vec_ref[4:5, :]
            hat1_s[rows, :] = hat
            root1_s[rows, :] = root
            z2_s[rows, :] = h1 + vec_ref[5:6, :]
            h1b = h1.astype(BF)
            h1b_s[rows, :] = h1b
            h1t_s[:, rows] = h1b.T

    @pl.when(step < 4)
    def _():
        w1 = w_ref[:, 0, 0].reshape(D, D)
        w2t = w_ref[:, 0, 1].reshape(D, D)
        bias = vec_ref[pl.ds(8 + step, 1), :]
        now = dot_nn(h1b_s[:BLK, :], w1)
        for i, rows in enumerate(blocks):
            later = dot_nn(h1b_s[blocks[i + 1], :], w1) if i < 2 else None
            act, slope = gelu_both(now + bias)
            act = act.astype(BF)
            u_s[step, rows, :] = act
            gp_s[step, rows, :] = slope.astype(BF)
            z2_s[rows, :] += dot_nt(act, w2t)
            now = later

    @pl.when(step == 3)
    def _():
        sums = [jnp.zeros((1, D), F32) for _ in range(3)]
        for rows in blocks:
            hat, root = norm_parts(z2_s[rows, :])
            out_ref[rows, :] = (hat * vec_ref[6:7, :] + vec_ref[7:8, :]).astype(BF)
            cot = cot_ref[rows, :].astype(F32) * weight_ref[rows, :]
            dz2 = norm_back(cot, vec_ref[6:7, :], hat, root)
            z2_s[rows, :] = dz2
            e2 = dz2.astype(BF)
            e2_s[rows, :] = e2
            e2t_s[:, rows] = e2.T
            sums[0] += jnp.sum(dz2, 0, keepdims=True)
            sums[1] += jnp.sum(cot * hat, 0, keepdims=True)
            sums[2] += jnp.sum(cot, 0, keepdims=True)
        for n in range(3):
            sums_ref[3 + n : 4 + n, :] = sums[n]

    @pl.when(jnp.logical_and(step >= 4, step < 8))
    def _():
        m = step - 4
        w1 = w_ref[:, 0, 0].reshape(D, D)
        w2t = w_ref[:, 0, 1].reshape(D, D)
        db1 = jnp.zeros((1, D), F32)
        now = dot_nn(e2_s[:BLK, :], w2t)
        for i, rows in enumerate(blocks):
            later = dot_nn(e2_s[blocks[i + 1], :], w2t) if i < 2 else None
            ep = (gp_s[m, rows, :].astype(F32) * now).astype(BF)
            ep_s[rows, :] = ep
            db1 += jnp.sum(ep.astype(F32), 0, keepdims=True)
            z2_s[rows, :] += dot_nt(ep, w1)
            now = later
        db1_ref[pl.ds(m, 1), :] = db1
        dw_ref[:, 0, 0] = dot_nn(h1t_s[...], ep_s[...]).astype(BF).reshape(RB, RP, D)
        dw_ref[:, 0, 1] = dot_nn(e2t_s[...], u_s[m]).astype(BF).reshape(RB, RP, D)

    @pl.when(step == 8)
    def _():
        sums = [jnp.zeros((1, D), F32) for _ in range(3)]
        for rows in blocks:
            dh = z2_s[rows, :]
            hat = hat1_s[rows, :]
            dz1 = norm_back(dh, vec_ref[3:4, :], hat, root1_s[rows, :])
            dz1_ref[rows, :] = dz1
            e1 = dz1.astype(BF)
            e2t_s[:, rows] = e1.T
            do_ref[rows, :] = dot_nn(e1, wo_s[...]).astype(BF)
            sums[0] += jnp.sum(dz1, 0, keepdims=True)
            sums[1] += jnp.sum(dh * hat, 0, keepdims=True)
            sums[2] += jnp.sum(dh, 0, keepdims=True)
        for n in range(3):
            sums_ref[n : n + 1, :] = sums[n]
        dw_ref[:, 0, 0] = dot_nn(e2t_s[...], o_ref[...]).astype(BF).reshape(RB, RP, D)
        dw_ref[:, 0, 1] = jnp.zeros((RB, RP, D), BF)


def pack_kernel(tab, own_ref, *rest):
    others, out_ref, line_s = rest[:-2], rest[-2], rest[-1]
    line_s[0] = own_ref[...]
    for n, ref in enumerate(others):
        line_s[n + 1] = ref[...]
    width = own_ref.shape[-1] // 4
    for m in range(4):
        shard = line_s[m ^ tab[0]]
        for n in range(4):
            out_ref[n, :, m * width : (m + 1) * width] = shard[:, n * width : (n + 1) * width]


def input_rest_kernel(tab, dk_ref, dv_ref, *refs):
    pieces, (nb_ref, mid_ref, w_s) = refs[:8], refs[8:]
    step = pl.program_id(0)

    @pl.when(step == 0)
    def _():
        for part in range(2):
            assemble(tab, pieces, part + 1, w_s, D * part)

    back = (dot_nt(dk_ref[...], w_s[:, :D]) + dot_nt(dv_ref[...], w_s[:, D:])).astype(BF)

    @pl.when(step < 3)
    def _():
        nb_ref[...] = back

    @pl.when(step >= 3)
    def _():
        mid_ref[...] = back


def input_own_kernel(tab, dq_ref, dk_ref, dv_ref, *refs):
    pieces, (dz1_ref, own_ref, w_s) = refs[:8], refs[8:]

    @pl.when(pl.program_id(0) == 0)
    def _():
        for part in range(3):
            assemble(tab, pieces, part, w_s, D * part)

    back = dot_nt(dk_ref[...], w_s[:, D : 2 * D]) + dot_nt(dv_ref[...], w_s[:, 2 * D :])
    own_ref[...] = back + dot_nt(dq_ref[...], w_s[:, :D]) + dz1_ref[...]


def line_kernel(tab, own_ref, *refs):
    chips, (feed_ref, *outs) = refs[:-5], refs[-5:]
    total = own_ref[...].astype(F32)
    for ref in chips:
        total = total + ref[...].astype(F32)
    total = total.astype(BF)
    width = total.shape[-1] // 4
    for n in range(4):
        m = n ^ tab[0]
        outs[n][:, :D] = feed_ref[m, 0]
        outs[n][:, D : 2 * D] = feed_ref[m, 1]
        for other in range(4):

            @pl.when(m == other)
            def _():
                at = slice(other * width, (other + 1) * width)
                for kind in range(3):
                    outs[n][:, 2 * D + kind * width : 2 * D + (kind + 1) * width] = total[kind, :, at]
                outs[n][:, 2 * D + 3 * width :] = feed_ref[4, 0, :, at]


def call(kernel, grid, in_specs, out_specs, out_shape, scratch, flops, bytes_accessed, name):
    return pl.pallas_call(
        kernel,
        grid_spec=pltpu.PrefetchScalarGridSpec(
            num_scalar_prefetch=1, grid=(grid,), in_specs=in_specs, out_specs=out_specs, scratch_shapes=scratch
        ),
        out_shape=out_shape,
        compiler_params=pltpu.CompilerParams(
            dimension_semantics=("arbitrary",), vmem_limit_bytes=VMEM_LIMIT
        ),
        cost_estimate=pl.CostEstimate(flops=flops, bytes_accessed=bytes_accessed, transcendentals=0),
        name=name,
    )


def whole(*shape):
    return pl.BlockSpec(shape, lambda s, t: (0,) * len(shape))


def columns(rows, width=128):
    return pl.BlockSpec((rows, width), lambda s, t: (0, s))


def shape_of(shape, dtype):
    return jax.ShapeDtypeStruct(shape, dtype)


def vm(shape, dtype):
    return pltpu.VMEM(shape, dtype)


def attend(tab, own, nb, mid, pieces, vectors):
    w_spec = pl.BlockSpec((3, RP, 128), lambda s, t: (0, 0, s))
    return call(
        attend_kernel,
        PAIRS,
        [whole(ROWS, D), whole(ROWS, D), whole(2 * BLK, D)] + [w_spec] * 8 + [columns(12)],
        [columns(ROWS), columns(ROWS), columns(ROWS), columns(8 * BLK), columns(8 * BLK)]
        + [pl.BlockSpec((128, 8 * BLK), lambda s, t: (s, 0))],
        [shape_of((ROWS, D), BF)] * 3 + [shape_of((8 * BLK, D), BF)] * 2 + [shape_of((D, 8 * BLK), BF)],
        [vm((D, 384), BF)] + [vm((8, BLK, 128), BF)] * 2 + [vm((2, 8, BLK, 128), BF), vm((8, BLK, 128), BF)],
        5_000_000_000,
        16_000_000,
        "attend",
    )(tab, own, nb, mid, *pieces, vectors)


def attend_back(tab, qe, qo, k, v, d_out, o, xt):
    return call(
        attend_back_kernel,
        PAIRS,
        [columns(ROWS), columns(ROWS), columns(8 * BLK), columns(8 * BLK), columns(ROWS), columns(ROWS), whole(D, 8 * BLK)],
        [
            columns(ROWS),
            columns(8 * BLK),
            columns(8 * BLK),
            pl.BlockSpec((RB // 2, 3, RP, 128), lambda s, t: (0, 0, 0, s)),
            pl.BlockSpec((RB // 2, 3, RP, 128), lambda s, t: (0, 0, 0, s)),
            columns(2),
        ],
        [
            shape_of((ROWS, D), BF),
            shape_of((8 * BLK, D), BF),
            shape_of((8 * BLK, D), BF),
            shape_of((RB // 2, 3, RP, D), BF),
            shape_of((RB // 2, 3, RP, D), BF),
            shape_of((2, D), F32),
        ],
        [vm((8, BLK, 128), BF)] * 5
        + [vm((8, 128, BLK), F32)] * 2
        + [vm((8 * BLK, BLK), BF)],
        50_000_000_000,
        24_000_000,
        "attend_back",
    )(tab, qe, qo, k, v, d_out, o, xt)


def feed(tab, o, x, pieces, vectors, w, cot, weight):
    wo_spec = pl.BlockSpec((1, RP, D), lambda s, t: (3, 0, 0))

    def group(s):
        return jnp.where(s < 4, s, jnp.minimum(s - 4, 3))

    return call(
        feed_kernel,
        9,
        [
            whole(ROWS, D),
            whole(ROWS, D),
            *[wo_spec] * 8,
            whole(12, D),
            pl.BlockSpec((RB, 1, 2, RP, D), lambda s, t: (0, group(s), 0, 0, 0)),
            whole(ROWS, D),
            whole(ROWS, 1),
        ],
        [
            whole(ROWS, D),
            pl.BlockSpec((RB, 1, 2, RP, D), lambda s, t: (0, jnp.maximum(s - 4, 0), 0, 0, 0)),
            whole(ROWS, D),
            whole(ROWS, D),
            whole(6, D),
            whole(4, D),
        ],
        [
            shape_of((ROWS, D), BF),
            shape_of((RB, 5, 2, RP, D), BF),
            shape_of((ROWS, D), F32),
            shape_of((ROWS, D), BF),
            shape_of((6, D), F32),
            shape_of((4, D), F32),
        ],
        [
            vm((D, D), BF),
            vm((ROWS, D), BF),
            vm((D, ROWS), BF),
            vm((ROWS, D), F32),
            vm((ROWS, 1), F32),
            vm((ROWS, D), F32),
            vm((4, ROWS, D), BF),
            vm((4, ROWS, D), BF),
            vm((ROWS, D), BF),
            vm((D, ROWS), BF),
            vm((ROWS, D), BF),
        ],
        40_000_000_000,
        48_000_000,
        "feed",
    )(tab, o, x, *pieces, vectors, w, cot, weight)


def round_kernel(qkv_ref, proj_ref, up_ref, down_ref, mine_ref, feed_ref):
    width = qkv_ref.shape[-1]
    for n in range(3):
        mine_ref[:, n * width : (n + 1) * width] = qkv_ref[n].astype(BF)
    mine_ref[:, 3 * width :] = proj_ref[...].T.astype(BF)
    feed_ref[0] = up_ref[...].astype(BF)
    feed_ref[1] = down_ref[...].astype(BF)


def round_shards(qkv, proj, up, down):
    rows = up.shape[0]
    return pl.pallas_call(
        round_kernel,
        in_specs=[pl.BlockSpec(memory_space=pltpu.VMEM)] * 4,
        out_specs=[pl.BlockSpec(memory_space=pltpu.VMEM)] * 2,
        out_shape=[shape_of((rows, D), BF), shape_of((2, rows, D), BF)],
        cost_estimate=pl.CostEstimate(flops=1_000_000, bytes_accessed=1_500_000, transcendentals=0),
        name="round_shards",
    )(qkv, proj, up, down)


def pack_line(z, own, others):
    rows, width = own.shape
    return call(
        pack_kernel,
        1,
        [whole(rows, width)] * 4,
        whole(4, rows, D),
        shape_of((4, rows, D), BF),
        [vm((4, rows, width), BF)],
        60_000_000_000,
        1_000_000,
        "pack_line",
    )(z.reshape(1).astype(jnp.int32), own, *others)


def input_rest(tab, dk, dv, pieces):
    w_spec = whole(3, RP, D)
    each = pl.BlockSpec((BLK, D), lambda s, t: (s + 3, 0))
    return call(
        input_rest_kernel,
        5,
        [each, each] + [w_spec] * 8,
        [
            pl.BlockSpec((BLK, D), lambda s, t: (jnp.minimum(s, 2), 0)),
            pl.BlockSpec((BLK, D), lambda s, t: (jnp.maximum(s - 3, 0), 0)),
        ],
        [shape_of((3 * BLK, D), BF), shape_of((2 * BLK, D), BF)],
        [vm((D, 2 * D), BF)],
        8_000_000_000,
        12_000_000,
        "input_rest",
    )(tab, dk, dv, *pieces)


def input_own(tab, dq, dk, dv, pieces, dz1):
    w_spec = whole(3, RP, D)
    each = pl.BlockSpec((BLK, D), lambda s, t: (s, 0))
    return call(
        input_own_kernel,
        3,
        [each, each, each] + [w_spec] * 8 + [each],
        each,
        shape_of((ROWS, D), F32),
        [vm((D, 3 * D), BF)],
        5_000_000_000,
        12_000_000,
        "input_own",
    )(tab, dq, dk, dv, *pieces, dz1)


def line_parts(z, own, others, fed):
    rows = own.shape[1]
    return call(
        line_kernel,
        1,
        [whole(3, rows, D)] * (1 + len(others)) + [whole(5, 2, rows, D)],
        [whole(rows, 3 * D)] * 4,
        [shape_of((rows, 3 * D), BF)] * 4,
        [],
        2_000_000,
        4_000_000,
        "line_parts",
    )(z.reshape(1).astype(jnp.int32), own, *others, fed)


def adamw(weight, clipped, first, second, rate, decay):
    first_new = BETA_ONE * first + (1.0 - BETA_ONE) * clipped
    second_new = BETA_TWO * second + (1.0 - BETA_TWO) * clipped * clipped
    first_hat = first_new / (1.0 - BETA_ONE**STEP)
    second_hat = second_new / (1.0 - BETA_TWO**STEP)
    updated = weight * (1.0 - rate * decay) - rate * first_hat / (jnp.sqrt(second_hat) + ADAM_EPS)
    return (clipped, first_new, second_new, updated)


def update_kernel(clip_ref, sum_ref, vec_ref, *refs):
    ins, outs = refs[:15], refs[15:]
    clip = clip_ref[0, 0]
    sums = sum_ref[...]
    width = D // 4
    grads = (
        [sums[:, 2 * D + n * width : 2 * D + (n + 1) * width] for n in range(3)],
        [sums[:, 2 * D + 3 * width :].T],
        [sums[:, :D]],
        [sums[:, D : 2 * D]],
        [vec_ref[...]],
    )
    for kind, parts in enumerate(grads):
        rate, decay = (VECTOR_RATE, 0.0) if kind == 4 else (MATRIX_RATE / math.sqrt(D), WEIGHT_DECAY)
        for n, grad in enumerate(parts):
            at = n if kind == 0 else Ellipsis
            results = adamw(ins[kind][at], grad * clip, ins[5 + kind][at], ins[10 + kind][at], rate, decay)
            for m, result in enumerate(results):
                outs[4 * kind + m][at] = result


def update(clip, sums, vec, weights, firsts, seconds):
    shapes = [shape_of(one.shape, F32) for one in weights for _ in range(4)]
    return pl.pallas_call(
        update_kernel,
        in_specs=[pl.BlockSpec(memory_space=pltpu.SMEM)] + [pl.BlockSpec(memory_space=pltpu.VMEM)] * 17,
        out_specs=[pl.BlockSpec(memory_space=pltpu.VMEM)] * 20,
        out_shape=shapes,
        compiler_params=pltpu.CompilerParams(vmem_limit_bytes=VMEM_LIMIT),
        cost_estimate=pl.CostEstimate(flops=10_000_000, bytes_accessed=8_000_000, transcendentals=0),
        name="update",
    )(clip, sums, vec, *weights, *firsts, *seconds)


def total_kernel(vec_ref, *refs):
    parts, (sum_out, square_out) = refs[:4], refs[4:]
    sums = parts[0][...].astype(F32)
    for ref in parts[1:]:
        sums = sums + ref[...].astype(F32)
    sum_out[...] = sums
    vec = vec_ref[...]
    square_out[0, 0] = jnp.sum(sums * sums) + jnp.sum(vec * vec)


def total(vec, parts):
    vmem = pl.BlockSpec(memory_space=pltpu.VMEM)
    return pl.pallas_call(
        total_kernel,
        in_specs=[vmem] * 5,
        out_specs=[vmem, pl.BlockSpec(memory_space=pltpu.SMEM)],
        out_shape=[shape_of(parts[0].shape, F32), shape_of((1, 1), F32)],
        compiler_params=pltpu.CompilerParams(vmem_limit_bytes=VMEM_LIMIT),
        cost_estimate=pl.CostEstimate(flops=2_000_000, bytes_accessed=4_000_000, transcendentals=0),
        name="total",
    )(vec, *parts)


def shards(
    tokens,
    out_cotangent,
    lengths,
    starts,
    ends,
    flags,
    qkv_master,
    proj_master,
    up_master,
    down_master,
    vectors,
    qkv_first,
    proj_first,
    up_first,
    down_first,
    qkv_second,
    proj_second,
    up_second,
    down_second,
    vector_first,
    vector_second,
):
    mp_count = lax.axis_size("mp")
    dp_count = lax.axis_size("dp")
    devices = mp_count * dp_count
    z = lax.axis_index("mp")
    dp_index = lax.axis_index("dp")
    core = dp_index % 2
    chips = dp_count // 2
    part = D // dp_count
    head_cols = D // mp_count

    def linear(chip, core_of, z_of):
        return (chip * 2 + core_of) * mp_count + z_of

    def permutation(move):
        return [
            (linear(chip, c, k), linear(*move(chip, c, k)))
            for chip in range(chips)
            for c in range(2)
            for k in range(mp_count)
        ]

    planes = [[linear(chip, c, k) for chip in range(chips)] for c in range(2) for k in range(mp_count)]
    swap_core = permutation(lambda chip, c, k: (chip, 1 - c, k))
    swap_z = [permutation(lambda chip, c, k, n=n: (chip, c, k ^ n)) for n in range(mp_count)]
    swap_chip = [permutation(lambda chip, c, k, n=n: (chip ^ n, c, k)) for n in range(chips)]
    middle = (0, 2, 1, 3)
    swap_mid = permutation(lambda chip, c, k: (chip, c, middle[k]))
    chip_index = dp_index // 2

    def over_plane(value):
        return lax.all_to_all(value, AXES, 0, 0, tiled=True, axis_index_groups=planes)

    def over_z(value):
        return lax.all_to_all(value, "mp", 0, 0, tiled=True)

    def absolute(same, other):
        order = jnp.arange(chips, dtype=jnp.int32) ^ chip_index
        same, other = jnp.stack(same)[order], jnp.stack(other)[order]
        both = jnp.where(core == 0, jnp.stack([same, other], 1), jnp.stack([other, same], 1))
        kinds = both.shape[2]
        both = both.transpose(2, 0, 1, 3, 4).reshape(kinds, RB // 2, 2, RP, D).transpose(1, 2, 0, 3, 4)
        return [both[n, half] for half in range(2) for n in range(RB // 2)]

    mine, feed_mine = round_shards(qkv_master, proj_master, up_master, down_master.T)
    feed_w = lax.all_gather(feed_mine, AXES, axis=0, tiled=False).reshape(dp_count, mp_count, 2, part, D)
    line = [lax.ppermute(mine, AXES, swap_z[n]) for n in range(1, mp_count)]
    tokens_late, mine, *line = lax.optimization_barrier((tokens, mine, *line))
    along_z = pack_line(z, mine, line)
    mid_at = jnp.where(z == 1, BLK, 0)
    nb = lax.ppermute(tokens_late, AXES, swap_z[1])
    mid = lax.ppermute(lax.dynamic_slice_in_dim(tokens_late, mid_at, 2 * BLK, 0), AXES, swap_mid)
    same = [along_z] + [lax.ppermute(along_z, AXES, swap_chip[n]) for n in range(1, chips)]
    first, same[1] = lax.optimization_barrier((along_z, same[1]))
    other = [lax.ppermute(one, AXES, swap_core) for one in [first] + same[1:]]
    pieces = same + other
    kernel_core, kernel_chip = core, chip_index
    if part != RP:
        pieces = absolute(same, other)
        feed_w = feed_w.transpose(1, 2, 0, 3, 4).reshape(mp_count, 2, RB, RP, D).transpose(2, 0, 1, 3, 4)
        kernel_core = kernel_chip = jnp.zeros((), jnp.int32)

    place = jnp.asarray(BLOCK_PLACE)[z]
    counts = jnp.clip(lengths[jnp.asarray(BLOCK_SEQ)[z]] - BLK * place, 0, BLK)
    tab = jnp.concatenate(
        [jnp.asarray(KEY_BLOCKS)[z].reshape(12), counts, kernel_core.reshape(1), kernel_chip.reshape(1)]
    ).astype(jnp.int32)

    positions = z * ROWS + jnp.arange(ROWS, dtype=jnp.int32)
    seq_of = positions // LEN
    within = positions % LEN
    picker = (seq_of[:, None] == jnp.arange(lengths.shape[0], dtype=jnp.int32)[None, :]).astype(jnp.int32)
    length_row = jnp.sum(picker * lengths[None, :], 1)
    start_row = jnp.sum(picker * starts[None, :], 1)
    end_row = jnp.sum(picker * ends[None, :], 1)
    flag_row = jnp.sum(picker * flags[None, :], 1).astype(F32)
    valid_row = (within < length_row).astype(F32)
    answer = (within == start_row).astype(F32) + (within == end_row).astype(F32)
    opening = (within == 0).astype(F32)
    row_weight = valid_row * (1.0 + 2.0 * (1.0 - flag_row) * answer + 4.0 * flag_row * opening)

    o, qe, qo, k, v, xt = attend(tab, tokens, nb, mid, pieces, vectors)
    block_out, feed_dw, dz1, d_o, sums_norm, bias_up_grad = feed(
        tab, o, tokens, pieces, vectors, feed_w, out_cotangent, row_weight[:, None]
    )

    def to_parts(grad):
        if part == RP:
            return grad
        lead = grad.shape[1:-2]
        moved = jnp.moveaxis(grad, 0, -3).reshape(*lead, dp_count, part, D)
        return jnp.moveaxis(moved, -3, 0)

    feed_part = lax.psum_scatter(to_parts(feed_dw), "dp", scatter_dimension=0, tiled=False)

    dq, dk, dv, keep, give, sums_head = attend_back(tab, qe, qo, k, v, d_o, o, xt)
    if part != RP:
        both = jnp.stack([keep, give], 1).reshape(RB, 3, RP, D)
        both = to_parts(both).reshape(chips, 2, 3, part, D)
        order = jnp.arange(chips, dtype=jnp.int32) ^ chip_index
        keep = lax.dynamic_index_in_dim(both, core, 1, keepdims=False)[order]
        give = lax.dynamic_index_in_dim(both, 1 - core, 1, keepdims=False)[order]
    got = lax.ppermute(give, AXES, swap_core)
    chip_sum = (keep.astype(F32) + got.astype(F32)).astype(BF)
    to_nb, to_mid = input_rest(tab, dk, dv, pieces)
    chip_sum, dq, dk, dv, sums_head, to_nb, to_mid = lax.optimization_barrier(
        (chip_sum, dq, dk, dv, sums_head, to_nb, to_mid)
    )
    from_chips = [lax.ppermute(chip_sum[n], AXES, swap_chip[n]) for n in range(1, chips)]
    from_nb = lax.ppermute(to_nb, AXES, swap_z[1])
    from_mid = lax.ppermute(to_mid, AXES, swap_mid)
    dx_own = input_own(tab, dq, dk, dv, pieces, dz1)
    vector_part = jnp.concatenate([sums_head, sums_norm, bias_up_grad], 0)
    vec_columns = D // devices
    vector_part = vector_part.reshape(12, devices, vec_columns).transpose(1, 0, 2)
    vector_grad = jnp.sum(lax.all_to_all(vector_part, AXES, 0, 0, tiled=True), 0)
    vector_grad, feed_part, dx_own, from_nb, from_mid, *from_chips = lax.optimization_barrier(
        (vector_grad, feed_part, dx_own, from_nb, from_mid, *from_chips)
    )
    line_own, *line_rest = line_parts(z, chip_sum[0], from_chips, feed_part)
    line_rest = [lax.ppermute(one, AXES, swap_z[n + 1]) for n, one in enumerate(line_rest)]
    zero_block = jnp.zeros((BLK, D), BF)
    from_mid = jnp.where(
        z == 1, jnp.concatenate([zero_block, from_mid], 0), jnp.concatenate([from_mid, zero_block], 0)
    )
    input_grad = dx_own + from_nb.astype(F32) + from_mid.astype(F32)

    sums, local_squares = total(vector_grad, [line_own] + line_rest)
    squares = lax.all_to_all(jnp.broadcast_to(local_squares.reshape(1), (devices,)), AXES, 0, 0, tiled=True)
    grad_norm = jnp.sqrt(jnp.sum(squares))
    clip_factor = jnp.minimum(1.0, CLIP_NORM / (grad_norm + 1e-06))
    vec_index = dp_index * mp_count + z
    vector_shard = lax.dynamic_slice_in_dim(vectors, vec_index * vec_columns, vec_columns, 1)
    results = update(
        clip_factor.reshape(1, 1),
        sums,
        vector_grad,
        (qkv_master, proj_master, up_master, down_master.T, vector_shard),
        (qkv_first, proj_first, up_first, down_first.T, vector_first),
        (qkv_second, proj_second, up_second, down_second.T, vector_second),
    )
    down_set = [one.T for one in results[12:16]]
    return (block_out, input_grad, grad_norm, *results[:12], *down_set, *results[16:])


def solution(mesh):
    rows = P(AXES, None)
    group = P("dp")
    qkv = P(None, "dp", "mp")
    proj = P("mp", "dp")
    up = P("dp", "mp")
    vec = P(None, AXES)
    return jax.shard_map(
        shards,
        mesh=mesh,
        in_specs=(rows, rows, group, group, group, group)
        + (qkv, proj, up, proj, P())
        + (qkv, proj, up, proj) * 2
        + (vec, vec),
        out_specs=(rows, rows, P()) + (qkv,) * 4 + (proj,) * 4 + (up,) * 4 + (proj,) * 4 + (vec,) * 4,
        check_vma=False,
    )
```

```python
from functools import partial
import math

import jax
import jax.numpy as jnp
import numpy as np
from jax import lax
from jax.experimental import pallas as pl
from jax.experimental.pallas import tpu as pltpu
from jax.sharding import PartitionSpec as P

D = 768
HEADS = 12
HDIM = 64
FF = 3072
LEN = 1024
STEP = 10

LN_EPS = 1e-06
BETA_ONE = 0.9
BETA_TWO = 0.999
ADAM_EPS = 1e-08
WEIGHT_DECAY = 0.01
CLIP_NORM = 1.0
VECTOR_RATE = 1.0
MATRIX_RATE = 2.0
NEG_FILL = -1e30

BF = jnp.bfloat16
F32 = jnp.float32
AXES = ("dp", "mp")
BLK = 256
ROWS = 768
PAIRS = HEADS // 2
RB = 8
RP = D // RB
VMEM_LIMIT = 60 * 1024 * 1024

KEY_BLOCKS = np.array(
    [
        [[0, 1, 2, 3]] * 3,
        [[3, 4, 5, 0], [1, 2, 6, 7], [1, 2, 6, 7]],
        [[6, 7, 0, 1], [6, 7, 0, 1], [2, 3, 4, 5]],
        [[5, 0, 1, 2]] * 3,
    ],
    np.int32,
)
BLOCK_SEQ = np.array(
    [[0, 0, 0, 0, 0, 0, 0, 0], [0, 1, 1, 0, 0, 0, 1, 1], [1, 1, 2, 2, 2, 2, 1, 1], [2, 2, 2, 2, 2, 2, 2, 2]], np.int32
)
BLOCK_PLACE = np.array(
    [[0, 1, 2, 3, 4, 4, 4, 4], [3, 0, 1, 0, 1, 2, 2, 3], [2, 3, 0, 1, 2, 3, 0, 1], [1, 2, 3, 4, 4, 0, 4, 4]], np.int32
)


def dot_nn(left, right):
    return jnp.dot(left, right, preferred_element_type=F32)


def dot_nt(left, right):
    return lax.dot_general(left, right, (((1,), (1,)), ((), ())), preferred_element_type=F32)


def lane_ids(rows):
    return lax.broadcasted_iota(jnp.int32, (rows, 128), 1)


def assemble(tab, pieces, part, target, col):
    width = pieces[0].shape[-1]
    core, chip = tab[20], tab[21]
    for n in range(4):
        for half in range(2):
            at = ((n ^ chip) * 2 + (core ^ half)) * RP
            target[pl.ds(pl.multiple_of(at, RP), RP), col : col + width] = pieces[4 * half + n][part]


def key_extra(count):
    place = lane_ids(BLK) % HDIM
    row = lax.broadcasted_iota(jnp.int32, (BLK, 128), 0)
    mask = jnp.where(row >= count, NEG_FILL, 0.0)
    return jnp.where(place == 0, mask, jnp.where(place <= 3, 1.0, 0.0)).astype(BF)


def split_three(value):
    high = value.astype(BF)
    rest = value - high.astype(F32)
    mid = rest.astype(BF)
    low = (rest - mid.astype(F32)).astype(BF)
    return high, mid, low


def attend_kernel(
    tab, own_ref, nb_ref, mid_ref, *refs
):
    pieces = refs[:8]
    vec_ref, o_ref, qe_ref, qo_ref, k_ref, v_ref, xt_ref, w_s, ka_e, ka_o, va_s, extra_s = refs[8:]
    mine = pl.ds(pl.multiple_of(pl.program_id(0) * 128, 128), 128)

    @pl.when(pl.program_id(0) == 0)
    def _():
        for b in range(8):
            extra_s[b] = key_extra(tab[12 + b])

    for part in range(3):
        assemble(tab, pieces, part, w_s, 128 * part)
    bias_q = vec_ref[0:1, :]
    bias_v = vec_ref[1:2, :]
    low = lane_ids(BLK) < HDIM
    place = lane_ids(BLK) % HDIM
    ones = jnp.ones((BLK, 128), BF)
    for src, first, count in ((own_ref, 0, 3), (nb_ref, 3, 3), (mid_ref, 6, 2)):
        at = slice(first * BLK, (first + count) * BLK)
        xt_ref[:, at] = src[:, mine].T
        kv = dot_nn(src[...], w_s[:, 128:384])
        k_ref[at, :] = kv[:, :128].astype(BF)
        v_ref[at, :] = (kv[:, 128:] + bias_v).astype(BF)
    for b in range(8):
        at = slice(b * BLK, (b + 1) * BLK)
        k = k_ref[at, :]
        ka_e[b] = jnp.where(low, k, extra_s[b])
        ka_o[b] = jnp.where(low, extra_s[b], k)
        va_s[0, b] = jnp.where(low, v_ref[at, :], ones)
        va_s[1, b] = jnp.where(low, ones, v_ref[at, :])
    q_extra = jnp.where(place == 0, 1.0, 0.0).astype(BF)
    queries = []
    for i in range(3):
        q = (dot_nn(own_ref[i * BLK : (i + 1) * BLK, :], w_s[:, :128]) + bias_q).astype(BF) * jnp.asarray(0.125, BF)
        queries.append((jnp.where(low, q, q_extra), jnp.where(low, q_extra, q)))
    keys = (ka_e, ka_o)

    def score(unit, j):
        i, head = unit
        return dot_nt(queries[i][head], keys[head][tab[4 * i + j]])

    units = [(i, head) for i in range(3) for head in range(2)]
    now = [score(units[0], j) for j in range(4)]
    for n, (i, head) in enumerate(units):
        peak = jnp.max(jnp.maximum(jnp.maximum(now[0], now[1]), jnp.maximum(now[2], now[3])), -1, keepdims=True)
        acc = jnp.zeros((BLK, 128), F32)
        later = []
        for j in range(4):
            if n + 1 < len(units):
                later.append(score(units[n + 1], j))
            probs = jnp.exp(now[j] - peak).astype(BF)
            acc = acc + dot_nn(probs, va_s[head, tab[4 * i + j]])
        now = later
        rows = slice(i * BLK, (i + 1) * BLK)
        high, mid, small = split_three(-(peak + jnp.log(acc)))
        extra = jnp.where(place == 0, 1.0, 0.0).astype(BF)
        extra = jnp.where(place == 1, high, extra)
        extra = jnp.where(place == 2, mid, extra)
        extra = jnp.where(place == 3, small, extra)
        if head == 0:
            qe_ref[rows, :] = jnp.where(low, queries[i][0], extra)
            even = acc
        else:
            qo_ref[rows, :] = jnp.where(low, extra, queries[i][1])
            total = jnp.where(low, acc, even)
            value = jnp.where(low, even, acc)
            o_ref[rows, :] = (value / pltpu.roll(total, HDIM, 1)).astype(BF)


def attend_back_kernel(
    tab,
    qe_ref,
    qo_ref,
    k_ref,
    v_ref,
    do_ref,
    o_ref,
    xt_ref,
    dq_ref,
    dk_ref,
    dv_ref,
    keep_ref,
    give_ref,
    db_ref,
    ka_e,
    ka_o,
    vb_e,
    vb_o,
    extra_s,
    dk_s,
    dv_s,
    dkv_s,
):
    @pl.when(pl.program_id(0) == 0)
    def _():
        for b in range(8):
            extra_s[b] = key_extra(tab[12 + b])

    low = lane_ids(BLK) < HDIM
    place = lane_ids(BLK) % HDIM
    v_extra = jnp.where(place < 3, 1.0, 0.0).astype(BF)
    zero = jnp.zeros((BLK, 128), BF)
    for b in range(8):
        at = slice(b * BLK, (b + 1) * BLK)
        k = k_ref[at, :]
        v = v_ref[at, :]
        ka_e[b] = jnp.where(low, k, extra_s[b])
        ka_o[b] = jnp.where(low, extra_s[b], k)
        vb_e[b] = jnp.where(low, v, v_extra)
        vb_o[b] = jnp.where(low, v_extra, v)
    dk_s[...] = jnp.zeros(dk_s.shape, F32)
    dv_s[...] = jnp.zeros(dv_s.shape, F32)
    sides = ((ka_e, vb_e), (ka_o, vb_o))
    given = []
    for i in range(3):
        rows = slice(i * BLK, (i + 1) * BLK)
        d_out = do_ref[rows, :]
        product = d_out.astype(F32) * o_ref[rows, :].astype(F32)
        qas = (qe_ref[rows, :], qo_ref[rows, :])
        d_augs = []
        for head in range(2):
            mine = low if head == 0 else jnp.logical_not(low)
            delta = jnp.sum(jnp.where(mine, product, 0.0), -1, keepdims=True)
            high, mid, small = split_three(-delta)
            extra = jnp.where(place == 0, high, jnp.where(place == 1, mid, jnp.where(place == 2, small, zero)))
            d_augs.append(jnp.where(mine, d_out, extra))
        given.append((qas, d_augs, d_out.T, jnp.where(low, qas[0], qas[1]).T))

    def score(unit, j):
        i, head = unit
        b = tab[4 * i + j]
        qas, d_augs = given[i][:2]
        return dot_nt(qas[head], sides[head][0][b]), dot_nt(d_augs[head], sides[head][1][b])

    units = [(i, head) for i in range(3) for head in range(2)]
    now = [score(units[0], j) for j in range(4)]
    for n, (i, head) in enumerate(units):
        lanes = slice(head * HDIM, (head + 1) * HDIM)
        dot_t, qt = given[i][2:]
        dq = jnp.zeros((BLK, 128), F32)
        later = []
        for j in range(4):
            if n + 1 < len(units):
                later.append(score(units[n + 1], j))
            b = tab[4 * i + j]
            probs = jnp.exp(now[j][0])
            d_scores = (probs * now[j][1]).astype(BF)
            dv_s[b, lanes, :] += dot_nn(dot_t[lanes, :], probs.astype(BF))
            dk_s[b, lanes, :] += dot_nn(qt[lanes, :], d_scores)
            dq = dq + dot_nn(d_scores, k_ref[pl.ds(pl.multiple_of(b * BLK, BLK), BLK), :])
        now = later
        if head == 0:
            even = dq
        else:
            dq_ref[i * BLK : (i + 1) * BLK, :] = (jnp.where(low, even, dq) * 0.125).astype(BF)
    for b in range(8):
        dk = dk_s[b].T.astype(BF)
        dv = dv_s[b].T.astype(BF)
        dk_ref[b * BLK : (b + 1) * BLK, :] = dk
        dv_ref[b * BLK : (b + 1) * BLK, :] = dv
        dkv_s[b * BLK : (b + 1) * BLK, :128] = dk
        dkv_s[b * BLK : (b + 1) * BLK, 128:] = dv
    dq_all = dq_ref[...]
    db_ref[0:1, :] = jnp.sum(dq_all.astype(F32), 0, keepdims=True)
    db_ref[1:2, :] = jnp.sum(dkv_s[:, 128:].astype(F32), 0, keepdims=True)
    dw_q = dot_nn(xt_ref[:, :ROWS], dq_all).astype(BF)
    dw_kv = dot_nn(xt_ref[...], dkv_s[...]).astype(BF)
    for n, grad in enumerate((dw_q, dw_kv[:, :128], dw_kv[:, 128:])):
        grad = grad.reshape(RB // 2, 2, RP, 128)
        for pos in range(RB // 2):
            keep_ref[pos ^ tab[21], n] = jnp.where(tab[20] == 0, grad[pos, 0], grad[pos, 1])
            give_ref[pos ^ tab[21], n] = jnp.where(tab[20] == 0, grad[pos, 1], grad[pos, 0])


def gelu_both(pre):
    size = jnp.abs(pre)
    bell = jnp.exp(pre * pre * -0.5)
    t = 1.0 / (1.0 + size * (0.3275911 * math.sqrt(0.5)))
    poly = t * (
        0.5 * 0.254829592
        + t * (0.5 * -0.284496736 + t * (0.5 * 1.421413741 + t * (0.5 * -1.453152027 + t * (0.5 * 1.061405429))))
    )
    tail = poly * bell
    phi = jnp.where(pre >= 0, 1.0 - tail, tail)
    return pre * phi, phi + pre * bell * (1.0 / math.sqrt(2.0 * math.pi))


def norm_parts(summed):
    average = jnp.mean(summed, -1, keepdims=True)
    centered = summed - average
    variance = jnp.mean(centered * centered, -1, keepdims=True)
    root = lax.rsqrt(variance + LN_EPS)
    return centered * root, root


def norm_back(cot, gain, hat, root):
    gz = cot * gain
    return root * (gz - jnp.mean(gz, -1, keepdims=True) - hat * jnp.mean(gz * hat, -1, keepdims=True))


def feed_kernel(tab, o_ref, x_ref, *refs):
    pieces = refs[:8]
    vec_ref, w_ref, cot_ref, weight_ref, out_ref, dw_ref, dz1_ref, do_ref, sums_ref, db1_ref = refs[8:18]
    wo_s, h1b_s, h1t_s, hat1_s, root1_s, z2_s, u_s, gp_s, e2_s, e2t_s, ep_s = refs[18:]
    step = pl.program_id(0)
    blocks = [slice(i * BLK, (i + 1) * BLK) for i in range(3)]

    @pl.when(step == 0)
    def _():
        assemble(tab, pieces, 0, wo_s, 0)
        for rows in blocks:
            z1 = x_ref[rows, :].astype(F32) + dot_nt(o_ref[rows, :], wo_s[...]) + vec_ref[2:3, :]
            hat, root = norm_parts(z1)
            h1 = hat * vec_ref[3:4, :] + vec_ref[4:5, :]
            hat1_s[rows, :] = hat
            root1_s[rows, :] = root
            z2_s[rows, :] = h1 + vec_ref[5:6, :]
            h1b = h1.astype(BF)
            h1b_s[rows, :] = h1b
            h1t_s[:, rows] = h1b.T

    @pl.when(step < 4)
    def _():
        w1 = w_ref[:, 0, 0].reshape(D, D)
        w2t = w_ref[:, 0, 1].reshape(D, D)
        bias = vec_ref[pl.ds(8 + step, 1), :]
        now = dot_nn(h1b_s[:BLK, :], w1)
        for i, rows in enumerate(blocks):
            later = dot_nn(h1b_s[blocks[i + 1], :], w1) if i < 2 else None
            act, slope = gelu_both(now + bias)
            act = act.astype(BF)
            u_s[step, rows, :] = act
            gp_s[step, rows, :] = slope.astype(BF)
            z2_s[rows, :] += dot_nt(act, w2t)
            now = later

    @pl.when(step == 3)
    def _():
        sums = [jnp.zeros((1, D), F32) for _ in range(3)]
        for rows in blocks:
            hat, root = norm_parts(z2_s[rows, :])
            out_ref[rows, :] = (hat * vec_ref[6:7, :] + vec_ref[7:8, :]).astype(BF)
            cot = cot_ref[rows, :].astype(F32) * weight_ref[rows, :]
            dz2 = norm_back(cot, vec_ref[6:7, :], hat, root)
            z2_s[rows, :] = dz2
            e2 = dz2.astype(BF)
            e2_s[rows, :] = e2
            e2t_s[:, rows] = e2.T
            sums[0] += jnp.sum(dz2, 0, keepdims=True)
            sums[1] += jnp.sum(cot * hat, 0, keepdims=True)
            sums[2] += jnp.sum(cot, 0, keepdims=True)
        for n in range(3):
            sums_ref[3 + n : 4 + n, :] = sums[n]

    @pl.when(jnp.logical_and(step >= 4, step < 8))
    def _():
        m = step - 4
        w1 = w_ref[:, 0, 0].reshape(D, D)
        w2t = w_ref[:, 0, 1].reshape(D, D)
        db1 = jnp.zeros((1, D), F32)
        now = dot_nn(e2_s[:BLK, :], w2t)
        for i, rows in enumerate(blocks):
            later = dot_nn(e2_s[blocks[i + 1], :], w2t) if i < 2 else None
            ep = (gp_s[m, rows, :].astype(F32) * now).astype(BF)
            ep_s[rows, :] = ep
            db1 += jnp.sum(ep.astype(F32), 0, keepdims=True)
            z2_s[rows, :] += dot_nt(ep, w1)
            now = later
        db1_ref[pl.ds(m, 1), :] = db1
        dw_ref[:, :RP] = dot_nn(h1t_s[...], ep_s[...]).astype(BF).reshape(RB, RP, D)
        dw_ref[:, RP:] = dot_nn(e2t_s[...], u_s[m]).astype(BF).reshape(RB, RP, D)

    @pl.when(step == 8)
    def _():
        sums = [jnp.zeros((1, D), F32) for _ in range(3)]
        for rows in blocks:
            dh = z2_s[rows, :]
            hat = hat1_s[rows, :]
            dz1 = norm_back(dh, vec_ref[3:4, :], hat, root1_s[rows, :])
            dz1_ref[rows, :] = dz1
            e1 = dz1.astype(BF)
            e2t_s[:, rows] = e1.T
            do_ref[rows, :] = dot_nn(e1, wo_s[...]).astype(BF)
            sums[0] += jnp.sum(dz1, 0, keepdims=True)
            sums[1] += jnp.sum(dh * hat, 0, keepdims=True)
            sums[2] += jnp.sum(dh, 0, keepdims=True)
        for n in range(3):
            sums_ref[n : n + 1, :] = sums[n]
        dw_ref[:, :RP] = dot_nn(e2t_s[...], o_ref[...]).astype(BF).reshape(RB, RP, D)


def pack_kernel(tab, own_ref, *rest):
    others, out_ref, line_s = rest[:-2], rest[-2], rest[-1]
    line_s[0] = own_ref[...]
    for n, ref in enumerate(others):
        line_s[n + 1] = ref[...]
    width = own_ref.shape[-1] // 4
    for m in range(4):
        shard = line_s[m ^ tab[0]]
        for n in range(4):
            out_ref[n, :, m * width : (m + 1) * width] = shard[:, n * width : (n + 1) * width]


def input_rest_kernel(tab, dk_ref, dv_ref, *refs):
    pieces, (nb_ref, mid_ref, w_s) = refs[:8], refs[8:]
    step = pl.program_id(0)

    @pl.when(step == 0)
    def _():
        for part in range(2):
            assemble(tab, pieces, part + 1, w_s, D * part)

    back = (dot_nt(dk_ref[...], w_s[:, :D]) + dot_nt(dv_ref[...], w_s[:, D:])).astype(BF)

    @pl.when(step < 3)
    def _():
        nb_ref[...] = back

    @pl.when(step >= 3)
    def _():
        mid_ref[...] = back


def input_own_kernel(tab, dq_ref, dk_ref, dv_ref, *refs):
    pieces, (dz1_ref, own_ref, w_s) = refs[:8], refs[8:]

    @pl.when(pl.program_id(0) == 0)
    def _():
        for part in range(3):
            assemble(tab, pieces, part, w_s, D * part)

    back = dot_nt(dk_ref[...], w_s[:, D : 2 * D]) + dot_nt(dv_ref[...], w_s[:, 2 * D :])
    own_ref[...] = back + dot_nt(dq_ref[...], w_s[:, :D]) + dz1_ref[...]


def head_line_kernel(z_ref, own_ref, *refs):
    others, outs = refs[:-4], refs[-4:]
    total = own_ref[...].astype(F32)
    for ref in others:
        total = total + ref[...].astype(F32)
    total = total.astype(BF)
    width = D // 4
    for m in range(4):
        at = slice(m * width, (m + 1) * width)
        mine = jnp.concatenate([total[kind, :, at] for kind in range(3)], 1)
        for n, ref in enumerate(outs):

            @pl.when((m ^ z_ref[0]) == n)
            def _():
                ref[...] = mine


def feed_line_kernel(z_ref, feed_ref, *outs):
    width = D // 4
    rows = outs[0].shape[0]
    for m in range(4):
        for n, ref in enumerate(outs):

            @pl.when((m ^ z_ref[0]) == n)
            def _():
                ref[:, :D] = feed_ref[2 * m * rows : (2 * m + 1) * rows, :]
                ref[:, D : 2 * D] = feed_ref[(2 * m + 1) * rows : (2 * m + 2) * rows, :]
                ref[:, 2 * D :] = feed_ref[8 * rows :, m * width : (m + 1) * width]


def call(kernel, grid, in_specs, out_specs, out_shape, scratch, flops, bytes_accessed, name):
    return pl.pallas_call(
        kernel,
        grid_spec=pltpu.PrefetchScalarGridSpec(
            num_scalar_prefetch=1, grid=(grid,), in_specs=in_specs, out_specs=out_specs, scratch_shapes=scratch
        ),
        out_shape=out_shape,
        compiler_params=pltpu.CompilerParams(
            dimension_semantics=("arbitrary",), vmem_limit_bytes=VMEM_LIMIT
        ),
        cost_estimate=pl.CostEstimate(flops=flops, bytes_accessed=bytes_accessed, transcendentals=0),
        name=name,
    )


def whole(*shape):
    return pl.BlockSpec(shape, lambda s, t: (0,) * len(shape))


def columns(rows, width=128):
    return pl.BlockSpec((rows, width), lambda s, t: (0, s))


def shape_of(shape, dtype):
    return jax.ShapeDtypeStruct(shape, dtype)


def vm(shape, dtype):
    return pltpu.VMEM(shape, dtype)


def attend(tab, own, nb, mid, pieces, vectors):
    w_spec = pl.BlockSpec((3, RP, 128), lambda s, t: (0, 0, s))
    return call(
        attend_kernel,
        PAIRS,
        [whole(ROWS, D), whole(ROWS, D), whole(2 * BLK, D)] + [w_spec] * 8 + [columns(12)],
        [columns(ROWS), columns(ROWS), columns(ROWS), columns(8 * BLK), columns(8 * BLK)]
        + [pl.BlockSpec((128, 8 * BLK), lambda s, t: (s, 0))],
        [shape_of((ROWS, D), BF)] * 3 + [shape_of((8 * BLK, D), BF)] * 2 + [shape_of((D, 8 * BLK), BF)],
        [vm((D, 384), BF)] + [vm((8, BLK, 128), BF)] * 2 + [vm((2, 8, BLK, 128), BF), vm((8, BLK, 128), BF)],
        5_000_000_000,
        16_000_000,
        "attend",
    )(tab, own, nb, mid, *pieces, vectors)


def attend_back(tab, qe, qo, k, v, d_out, o, xt):
    return call(
        attend_back_kernel,
        PAIRS,
        [columns(ROWS), columns(ROWS), columns(8 * BLK), columns(8 * BLK), columns(ROWS), columns(ROWS), whole(D, 8 * BLK)],
        [
            columns(ROWS),
            columns(8 * BLK),
            columns(8 * BLK),
            pl.BlockSpec((RB // 2, 3, RP, 128), lambda s, t: (0, 0, 0, s)),
            pl.BlockSpec((RB // 2, 3, RP, 128), lambda s, t: (0, 0, 0, s)),
            columns(2),
        ],
        [
            shape_of((ROWS, D), BF),
            shape_of((8 * BLK, D), BF),
            shape_of((8 * BLK, D), BF),
            shape_of((RB // 2, 3, RP, D), BF),
            shape_of((RB // 2, 3, RP, D), BF),
            shape_of((2, D), F32),
        ],
        [vm((8, BLK, 128), BF)] * 5
        + [vm((8, 128, BLK), F32)] * 2
        + [vm((8 * BLK, BLK), BF)],
        50_000_000_000,
        24_000_000,
        "attend_back",
    )(tab, qe, qo, k, v, d_out, o, xt)


def feed(tab, o, x, pieces, vectors, w, cot, weight):
    wo_spec = pl.BlockSpec((1, RP, D), lambda s, t: (3, 0, 0))

    def group(s):
        return jnp.where(s < 4, s, jnp.minimum(s - 4, 3))

    return call(
        feed_kernel,
        9,
        [
            whole(ROWS, D),
            whole(ROWS, D),
            *[wo_spec] * 8,
            whole(12, D),
            pl.BlockSpec((RB, 1, 2, RP, D), lambda s, t: (0, group(s), 0, 0, 0)),
            whole(ROWS, D),
            whole(ROWS, 1),
        ],
        [
            whole(ROWS, D),
            pl.BlockSpec((RB, 2 * RP, D), lambda s, t: (0, jnp.maximum(s - 4, 0), 0)),
            whole(ROWS, D),
            whole(ROWS, D),
            whole(6, D),
            whole(4, D),
        ],
        [
            shape_of((ROWS, D), BF),
            shape_of((RB, 9 * RP, D), BF),
            shape_of((ROWS, D), F32),
            shape_of((ROWS, D), BF),
            shape_of((6, D), F32),
            shape_of((4, D), F32),
        ],
        [
            vm((D, D), BF),
            vm((ROWS, D), BF),
            vm((D, ROWS), BF),
            vm((ROWS, D), F32),
            vm((ROWS, 1), F32),
            vm((ROWS, D), F32),
            vm((4, ROWS, D), BF),
            vm((4, ROWS, D), BF),
            vm((ROWS, D), BF),
            vm((D, ROWS), BF),
            vm((ROWS, D), BF),
        ],
        40_000_000_000,
        48_000_000,
        "feed",
    )(tab, o, x, *pieces, vectors, w, cot, weight)


def round_kernel(qkv_ref, proj_ref, up_ref, down_ref, mine_ref, feed_ref):
    width = qkv_ref.shape[-1]
    for n in range(3):
        mine_ref[:, n * width : (n + 1) * width] = qkv_ref[n].astype(BF)
    mine_ref[:, 3 * width :] = proj_ref[...].T.astype(BF)
    feed_ref[0] = up_ref[...].astype(BF)
    feed_ref[1] = down_ref[...].astype(BF)


def round_shards(qkv, proj, up, down):
    rows = up.shape[0]
    return pl.pallas_call(
        round_kernel,
        in_specs=[pl.BlockSpec(memory_space=pltpu.VMEM)] * 4,
        out_specs=[pl.BlockSpec(memory_space=pltpu.VMEM)] * 2,
        out_shape=[shape_of((rows, D), BF), shape_of((2, rows, D), BF)],
        cost_estimate=pl.CostEstimate(flops=1_000_000, bytes_accessed=1_500_000, transcendentals=0),
        name="round_shards",
    )(qkv, proj, up, down)


def pack_line(z, own, others):
    rows, width = own.shape
    return call(
        pack_kernel,
        1,
        [whole(rows, width)] * 4,
        whole(4, rows, D),
        shape_of((4, rows, D), BF),
        [vm((4, rows, width), BF)],
        60_000_000_000,
        1_000_000,
        "pack_line",
    )(z.reshape(1).astype(jnp.int32), own, *others)


def input_rest(tab, dk, dv, pieces):
    w_spec = whole(3, RP, D)
    each = pl.BlockSpec((BLK, D), lambda s, t: (s + 3, 0))
    return call(
        input_rest_kernel,
        5,
        [each, each] + [w_spec] * 8,
        [
            pl.BlockSpec((BLK, D), lambda s, t: (jnp.minimum(s, 2), 0)),
            pl.BlockSpec((BLK, D), lambda s, t: (jnp.maximum(s - 3, 0), 0)),
        ],
        [shape_of((3 * BLK, D), BF), shape_of((2 * BLK, D), BF)],
        [vm((D, 2 * D), BF)],
        8_000_000_000,
        12_000_000,
        "input_rest",
    )(tab, dk, dv, *pieces)


def input_own(tab, dq, dk, dv, pieces, dz1):
    w_spec = whole(3, RP, D)
    each = pl.BlockSpec((BLK, D), lambda s, t: (s, 0))
    return call(
        input_own_kernel,
        3,
        [each, each, each] + [w_spec] * 8 + [each],
        each,
        shape_of((ROWS, D), F32),
        [vm((D, 3 * D), BF)],
        5_000_000_000,
        12_000_000,
        "input_own",
    )(tab, dq, dk, dv, *pieces, dz1)


def in_line(kernel, name, rows, width, z, *parts):
    return pl.pallas_call(
        kernel,
        in_specs=[pl.BlockSpec(memory_space=pltpu.SMEM)] + [pl.BlockSpec(memory_space=pltpu.VMEM)] * len(parts),
        out_specs=[pl.BlockSpec(memory_space=pltpu.VMEM)] * 4,
        out_shape=[shape_of((rows, width), BF)] * 4,
        compiler_params=pltpu.CompilerParams(vmem_limit_bytes=VMEM_LIMIT),
        cost_estimate=pl.CostEstimate(flops=2_000_000, bytes_accessed=4_000_000, transcendentals=0),
        name=name,
    )(z.reshape(1).astype(jnp.int32), *parts)


def adamw(weight, clipped, first, second, rate, decay):
    first_new = BETA_ONE * first + (1.0 - BETA_ONE) * clipped
    second_new = BETA_TWO * second + (1.0 - BETA_TWO) * clipped * clipped
    first_hat = first_new / (1.0 - BETA_ONE**STEP)
    second_hat = second_new / (1.0 - BETA_TWO**STEP)
    updated = weight * (1.0 - rate * decay) - rate * first_hat / (jnp.sqrt(second_hat) + ADAM_EPS)
    return (clipped, first_new, second_new, updated)


def update_kernel(squares_ref, head_ref, feed_ref, vec_ref, *refs):
    ins, norm_ref, outs = refs[:15], refs[15], refs[16:]
    norm = jnp.sqrt(jnp.sum(squares_ref[...], keepdims=True))
    norm_ref[...] = norm
    clip = jnp.minimum(1.0, CLIP_NORM / (norm + 1e-06))
    head = head_ref[...]
    fed = feed_ref[...]
    width = D // 4
    grads = (
        [head[:, n * width : (n + 1) * width] for n in range(3)],
        [fed[:, 2 * D :].T],
        [fed[:, :D]],
        [fed[:, D : 2 * D]],
        [vec_ref[...]],
    )
    for kind, parts in enumerate(grads):
        rate, decay = (VECTOR_RATE, 0.0) if kind == 4 else (MATRIX_RATE / math.sqrt(D), WEIGHT_DECAY)
        for n, grad in enumerate(parts):
            at = n if kind == 0 else Ellipsis
            results = adamw(ins[kind][at], grad * clip, ins[5 + kind][at], ins[10 + kind][at], rate, decay)
            for m, result in enumerate(results):
                outs[4 * kind + m][at] = result


def update(squares, sums, vec, weights, firsts, seconds):
    vmem = pl.BlockSpec(memory_space=pltpu.VMEM)
    return pl.pallas_call(
        update_kernel,
        in_specs=[vmem] * 19,
        out_specs=[vmem] * 21,
        out_shape=[shape_of((1, 1), F32)] + [shape_of(one.shape, F32) for one in weights for _ in range(4)],
        compiler_params=pltpu.CompilerParams(vmem_limit_bytes=VMEM_LIMIT),
        cost_estimate=pl.CostEstimate(flops=10_000_000, bytes_accessed=8_000_000, transcendentals=0),
        name="update",
    )(squares, *sums, vec, *weights, *firsts, *seconds)


def total_kernel(vec_ref, *refs):
    vec = vec_ref[...]
    square = jnp.sum(vec * vec, keepdims=True)
    for n in range(2):
        sums = refs[4 * n][...].astype(F32)
        for ref in refs[4 * n + 1 : 4 * n + 4]:
            sums = sums + ref[...].astype(F32)
        refs[8 + n][...] = sums
        square = square + jnp.sum(sums * sums, keepdims=True)
    refs[10][...] = jnp.broadcast_to(square, refs[10].shape)


def total(vec, groups, devices):
    vmem = pl.BlockSpec(memory_space=pltpu.VMEM)
    *sums, square = pl.pallas_call(
        total_kernel,
        in_specs=[vmem] * 9,
        out_specs=[vmem] * 3,
        out_shape=[shape_of(group[0].shape, F32) for group in groups] + [shape_of((devices, 1), F32)],
        compiler_params=pltpu.CompilerParams(vmem_limit_bytes=VMEM_LIMIT),
        cost_estimate=pl.CostEstimate(flops=2_000_000, bytes_accessed=4_000_000, transcendentals=0),
        name="total",
    )(vec, *[one for group in groups for one in group])
    return sums, square


def shards(
    tokens,
    out_cotangent,
    lengths,
    starts,
    ends,
    flags,
    qkv_master,
    proj_master,
    up_master,
    down_master,
    vectors,
    qkv_first,
    proj_first,
    up_first,
    down_first,
    qkv_second,
    proj_second,
    up_second,
    down_second,
    vector_first,
    vector_second,
):
    mp_count = lax.axis_size("mp")
    dp_count = lax.axis_size("dp")
    devices = mp_count * dp_count
    z = lax.axis_index("mp")
    dp_index = lax.axis_index("dp")
    core = dp_index % 2
    chips = dp_count // 2
    part = D // dp_count
    head_cols = D // mp_count

    def linear(chip, core_of, z_of):
        return (chip * 2 + core_of) * mp_count + z_of

    def permutation(move):
        return [
            (linear(chip, c, k), linear(*move(chip, c, k)))
            for chip in range(chips)
            for c in range(2)
            for k in range(mp_count)
        ]

    planes = [[linear(chip, c, k) for chip in range(chips)] for c in range(2) for k in range(mp_count)]
    swap_core = permutation(lambda chip, c, k: (chip, 1 - c, k))
    swap_z = [permutation(lambda chip, c, k, n=n: (chip, c, k ^ n)) for n in range(mp_count)]
    swap_chip = [permutation(lambda chip, c, k, n=n: (chip ^ n, c, k)) for n in range(chips)]
    middle = (0, 2, 1, 3)
    swap_mid = permutation(lambda chip, c, k: (chip, c, middle[k]))
    chip_index = dp_index // 2

    def over_plane(value):
        return lax.all_to_all(value, AXES, 0, 0, tiled=True, axis_index_groups=planes)

    def over_z(value):
        return lax.all_to_all(value, "mp", 0, 0, tiled=True)

    def absolute(same, other):
        order = jnp.arange(chips, dtype=jnp.int32) ^ chip_index
        same, other = jnp.stack(same)[order], jnp.stack(other)[order]
        both = jnp.where(core == 0, jnp.stack([same, other], 1), jnp.stack([other, same], 1))
        kinds = both.shape[2]
        both = both.transpose(2, 0, 1, 3, 4).reshape(kinds, RB // 2, 2, RP, D).transpose(1, 2, 0, 3, 4)
        return [both[n, half] for half in range(2) for n in range(RB // 2)]

    mine, feed_mine = round_shards(qkv_master, proj_master, up_master, down_master.T)
    feed_w = lax.all_gather(feed_mine, AXES, axis=0, tiled=False).reshape(dp_count, mp_count, 2, part, D)
    line = [lax.ppermute(mine, AXES, swap_z[n]) for n in range(1, mp_count)]
    tokens_late, mine, *line = lax.optimization_barrier((tokens, mine, *line))
    along_z = pack_line(z, mine, line)
    mid_at = jnp.where(z == 1, BLK, 0)
    nb = lax.ppermute(tokens_late, AXES, swap_z[1])
    mid = lax.ppermute(lax.dynamic_slice_in_dim(tokens_late, mid_at, 2 * BLK, 0), AXES, swap_mid)
    same = [along_z] + [lax.ppermute(along_z, AXES, swap_chip[n]) for n in range(1, chips)]
    first, same[1] = lax.optimization_barrier((along_z, same[1]))
    other = [lax.ppermute(one, AXES, swap_core) for one in [first] + same[1:]]
    pieces = same + other
    kernel_core, kernel_chip = core, chip_index
    if part != RP:
        pieces = absolute(same, other)
        feed_w = feed_w.transpose(1, 2, 0, 3, 4).reshape(mp_count, 2, RB, RP, D).transpose(2, 0, 1, 3, 4)
        kernel_core = kernel_chip = jnp.zeros((), jnp.int32)

    place = jnp.asarray(BLOCK_PLACE)[z]
    counts = jnp.clip(lengths[jnp.asarray(BLOCK_SEQ)[z]] - BLK * place, 0, BLK)
    tab = jnp.concatenate(
        [jnp.asarray(KEY_BLOCKS)[z].reshape(12), counts, kernel_core.reshape(1), kernel_chip.reshape(1)]
    ).astype(jnp.int32)

    positions = z * ROWS + jnp.arange(ROWS, dtype=jnp.int32)
    seq_of = positions // LEN
    within = positions % LEN
    picker = (seq_of[:, None] == jnp.arange(lengths.shape[0], dtype=jnp.int32)[None, :]).astype(jnp.int32)
    length_row = jnp.sum(picker * lengths[None, :], 1)
    start_row = jnp.sum(picker * starts[None, :], 1)
    end_row = jnp.sum(picker * ends[None, :], 1)
    flag_row = jnp.sum(picker * flags[None, :], 1).astype(F32)
    valid_row = (within < length_row).astype(F32)
    answer = (within == start_row).astype(F32) + (within == end_row).astype(F32)
    opening = (within == 0).astype(F32)
    row_weight = valid_row * (1.0 + 2.0 * (1.0 - flag_row) * answer + 4.0 * flag_row * opening)

    o, qe, qo, k, v, xt = attend(tab, tokens, nb, mid, pieces, vectors)
    block_out, feed_dw, dz1, d_o, sums_norm, bias_up_grad = feed(
        tab, o, tokens, pieces, vectors, feed_w, out_cotangent, row_weight[:, None]
    )

    def to_parts(grad):
        if part == RP:
            return grad
        lead = grad.shape[1:-2]
        moved = jnp.moveaxis(grad, 0, -3).reshape(*lead, dp_count, part, D)
        return jnp.moveaxis(moved, -3, 0)

    if part != RP:
        feed_dw = to_parts(feed_dw.reshape(RB, 9, RP, D)).reshape(dp_count, 9 * part, D)
    feed_part = lax.psum_scatter(feed_dw, "dp", scatter_dimension=0, tiled=False)

    dq, dk, dv, keep, give, sums_head = attend_back(tab, qe, qo, k, v, d_o, o, xt)
    if part != RP:
        both = jnp.stack([keep, give], 1).reshape(RB, 3, RP, D)
        both = to_parts(both).reshape(chips, 2, 3, part, D)
        order = jnp.arange(chips, dtype=jnp.int32) ^ chip_index
        keep = lax.dynamic_index_in_dim(both, core, 1, keepdims=False)[order]
        give = lax.dynamic_index_in_dim(both, 1 - core, 1, keepdims=False)[order]
    got = lax.ppermute(give, AXES, swap_core)
    chip_sum = (keep.astype(F32) + got.astype(F32)).astype(BF)
    to_nb, to_mid = input_rest(tab, dk, dv, pieces)
    chip_sum, dq, dk, dv, sums_head, to_nb, to_mid = lax.optimization_barrier(
        (chip_sum, dq, dk, dv, sums_head, to_nb, to_mid)
    )
    from_chips = [lax.ppermute(chip_sum[n], AXES, swap_chip[n]) for n in range(1, chips)]
    from_nb = lax.ppermute(to_nb, AXES, swap_z[1])
    from_mid = lax.ppermute(to_mid, AXES, swap_mid)
    dx_own = input_own(tab, dq, dk, dv, pieces, dz1)
    vector_part = jnp.concatenate([sums_head, sums_norm, bias_up_grad], 0)
    vec_columns = D // devices
    vector_part = vector_part.reshape(12, devices, vec_columns).transpose(1, 0, 2)
    vector_grad = jnp.sum(lax.all_to_all(vector_part, AXES, 0, 0, tiled=True), 0)
    vector_grad, dx_own, from_nb, from_mid, *from_chips = lax.optimization_barrier(
        (vector_grad, dx_own, from_nb, from_mid, *from_chips)
    )

    def along_line(parts):
        return [parts[0]] + [lax.ppermute(parts[n], AXES, swap_z[n]) for n in range(1, mp_count)]

    head_line = along_line(in_line(head_line_kernel, "head_line", part, 3 * D // 4, z, chip_sum[0], *from_chips))
    feed_part, *head_line = lax.optimization_barrier((feed_part, *head_line))
    feed_line = along_line(in_line(feed_line_kernel, "feed_line", part, 2 * D + D // 4, z, feed_part))
    zero_block = jnp.zeros((BLK, D), BF)
    from_mid = jnp.where(
        z == 1, jnp.concatenate([zero_block, from_mid], 0), jnp.concatenate([from_mid, zero_block], 0)
    )
    input_grad = dx_own + from_nb.astype(F32) + from_mid.astype(F32)

    sums, square = total(vector_grad, (head_line, feed_line), devices)
    squares = lax.all_to_all(square, AXES, 0, 0, tiled=True)
    vec_index = dp_index * mp_count + z
    vector_shard = lax.dynamic_slice_in_dim(vectors, vec_index * vec_columns, vec_columns, 1)
    grad_norm, *results = update(
        squares,
        sums,
        vector_grad,
        (qkv_master, proj_master, up_master, down_master.T, vector_shard),
        (qkv_first, proj_first, up_first, down_first.T, vector_first),
        (qkv_second, proj_second, up_second, down_second.T, vector_second),
    )
    down_set = [one.T for one in results[12:16]]
    return (block_out, input_grad, grad_norm.reshape(()), *results[:12], *down_set, *results[16:])


def solution(mesh):
    rows = P(AXES, None)
    group = P("dp")
    qkv = P(None, "dp", "mp")
    proj = P("mp", "dp")
    up = P("dp", "mp")
    vec = P(None, AXES)
    return jax.shard_map(
        shards,
        mesh=mesh,
        in_specs=(rows, rows, group, group, group, group)
        + (qkv, proj, up, proj, P())
        + (qkv, proj, up, proj) * 2
        + (vec, vec),
        out_specs=(rows, rows, P()) + (qkv,) * 4 + (proj,) * 4 + (up,) * 4 + (proj,) * 4 + (vec,) * 4,
        check_vma=False,
    )
```

```python
from functools import partial
import math

import jax
import jax.numpy as jnp
import numpy as np
from jax import lax
from jax.experimental import pallas as pl
from jax.experimental.pallas import tpu as pltpu
from jax.sharding import PartitionSpec as P

D = 768
HEADS = 12
HDIM = 64
FF = 3072
LEN = 1024
STEP = 10

LN_EPS = 1e-06
BETA_ONE = 0.9
BETA_TWO = 0.999
ADAM_EPS = 1e-08
WEIGHT_DECAY = 0.01
CLIP_NORM = 1.0
VECTOR_RATE = 1.0
MATRIX_RATE = 2.0
NEG_FILL = -1e30

BF = jnp.bfloat16
F32 = jnp.float32
AXES = ("dp", "mp")
BLK = 256
ROWS = 768
HALF = ROWS // 2
PAIRS = HEADS // 2
RB = 8
RP = D // RB
VMEM_LIMIT = 60 * 1024 * 1024

KEY_BLOCKS = np.array(
    [
        [[0, 1, 2, 3]] * 3,
        [[3, 4, 5, 0], [1, 2, 6, 7], [1, 2, 6, 7]],
        [[6, 7, 0, 1], [6, 7, 0, 1], [2, 3, 4, 5]],
        [[5, 0, 1, 2]] * 3,
    ],
    np.int32,
)
BLOCK_SEQ = np.array(
    [[0, 0, 0, 0, 0, 0, 0, 0], [0, 1, 1, 0, 0, 0, 1, 1], [1, 1, 2, 2, 2, 2, 1, 1], [2, 2, 2, 2, 2, 2, 2, 2]], np.int32
)
BLOCK_PLACE = np.array(
    [[0, 1, 2, 3, 4, 4, 4, 4], [3, 0, 1, 0, 1, 2, 2, 3], [2, 3, 0, 1, 2, 3, 0, 1], [1, 2, 3, 4, 4, 0, 4, 4]], np.int32
)


def dot_nn(left, right):
    return jnp.dot(left, right, preferred_element_type=F32)


def dot_nt(left, right):
    return lax.dot_general(left, right, (((1,), (1,)), ((), ())), preferred_element_type=F32)


def lane_ids(rows):
    return lax.broadcasted_iota(jnp.int32, (rows, 128), 1)


def assemble(tab, pieces, part, target, col):
    width = pieces[0].shape[-1]
    core, chip = tab[20], tab[21]
    for n in range(4):
        for half in range(2):
            at = ((n ^ chip) * 2 + (core ^ half)) * RP
            target[pl.ds(pl.multiple_of(at, RP), RP), col : col + width] = pieces[4 * half + n][part]


def key_extra(count):
    place = lane_ids(BLK) % HDIM
    row = lax.broadcasted_iota(jnp.int32, (BLK, 128), 0)
    mask = jnp.where(row >= count, NEG_FILL, 0.0)
    return jnp.where(place == 0, mask, jnp.where(place <= 3, 1.0, 0.0)).astype(BF)


def split_three(value):
    high = value.astype(BF)
    rest = value - high.astype(F32)
    mid = rest.astype(BF)
    low = (rest - mid.astype(F32)).astype(BF)
    return high, mid, low


def attend_kernel(
    tab, own_ref, nb_ref, mid_ref, *refs
):
    pieces = refs[:8]
    vec_ref, o_ref, qe_ref, qo_ref, k_ref, v_ref, xt_ref, w_s, ka_e, ka_o, va_s, extra_s = refs[8:]
    mine = pl.ds(pl.multiple_of(pl.program_id(0) * 128, 128), 128)

    @pl.when(pl.program_id(0) == 0)
    def _():
        for b in range(8):
            extra_s[b] = key_extra(tab[12 + b])

    for part in range(3):
        assemble(tab, pieces, part, w_s, 128 * part)
    bias_q = vec_ref[0:1, :]
    bias_v = vec_ref[1:2, :]
    low = lane_ids(BLK) < HDIM
    place = lane_ids(BLK) % HDIM
    ones = jnp.ones((BLK, 128), BF)
    for src, first, count in ((own_ref, 0, 3), (nb_ref, 3, 3), (mid_ref, 6, 2)):
        at = slice(first * BLK, (first + count) * BLK)
        xt_ref[:, at] = src[:, mine].T
        kv = dot_nn(src[...], w_s[:, 128:384])
        k_ref[at, :] = kv[:, :128].astype(BF)
        v_ref[at, :] = (kv[:, 128:] + bias_v).astype(BF)
    for b in range(8):
        at = slice(b * BLK, (b + 1) * BLK)
        k = k_ref[at, :]
        ka_e[b] = jnp.where(low, k, extra_s[b])
        ka_o[b] = jnp.where(low, extra_s[b], k)
        va_s[0, b] = jnp.where(low, v_ref[at, :], ones)
        va_s[1, b] = jnp.where(low, ones, v_ref[at, :])
    q_extra = jnp.where(place == 0, 1.0, 0.0).astype(BF)
    queries = []
    for i in range(3):
        q = (dot_nn(own_ref[i * BLK : (i + 1) * BLK, :], w_s[:, :128]) + bias_q).astype(BF) * jnp.asarray(0.125, BF)
        queries.append((jnp.where(low, q, q_extra), jnp.where(low, q_extra, q)))
    keys = (ka_e, ka_o)

    def score(unit, j):
        i, head = unit
        return dot_nt(queries[i][head], keys[head][tab[4 * i + j]])

    units = [(i, head) for i in range(3) for head in range(2)]
    now = [score(units[0], j) for j in range(4)]
    for n, (i, head) in enumerate(units):
        peak = jnp.max(jnp.maximum(jnp.maximum(now[0], now[1]), jnp.maximum(now[2], now[3])), -1, keepdims=True)
        acc = jnp.zeros((BLK, 128), F32)
        later = []
        for j in range(4):
            if n + 1 < len(units):
                later.append(score(units[n + 1], j))
            probs = jnp.exp(now[j] - peak).astype(BF)
            acc = acc + dot_nn(probs, va_s[head, tab[4 * i + j]])
        now = later
        rows = slice(i * BLK, (i + 1) * BLK)
        high, mid, small = split_three(-(peak + jnp.log(acc)))
        extra = jnp.where(place == 0, 1.0, 0.0).astype(BF)
        extra = jnp.where(place == 1, high, extra)
        extra = jnp.where(place == 2, mid, extra)
        extra = jnp.where(place == 3, small, extra)
        if head == 0:
            qe_ref[rows, :] = jnp.where(low, queries[i][0], extra)
            even = acc
        else:
            qo_ref[rows, :] = jnp.where(low, extra, queries[i][1])
            total = jnp.where(low, acc, even)
            value = jnp.where(low, even, acc)
            o_ref[rows, :] = (value / pltpu.roll(total, HDIM, 1)).astype(BF)


def attend_back_kernel(
    tab,
    qe_ref,
    qo_ref,
    k_ref,
    v_ref,
    do_ref,
    o_ref,
    xt_ref,
    dq_ref,
    dk_ref,
    dv_ref,
    keep_ref,
    give_ref,
    db_ref,
    ka_e,
    ka_o,
    vb_e,
    vb_o,
    extra_s,
    dk_s,
    dv_s,
    dkv_s,
):
    @pl.when(pl.program_id(0) == 0)
    def _():
        for b in range(8):
            extra_s[b] = key_extra(tab[12 + b])

    low = lane_ids(BLK) < HDIM
    place = lane_ids(BLK) % HDIM
    v_extra = jnp.where(place < 3, 1.0, 0.0).astype(BF)
    zero = jnp.zeros((BLK, 128), BF)
    for b in range(8):
        at = slice(b * BLK, (b + 1) * BLK)
        k = k_ref[at, :]
        v = v_ref[at, :]
        ka_e[b] = jnp.where(low, k, extra_s[b])
        ka_o[b] = jnp.where(low, extra_s[b], k)
        vb_e[b] = jnp.where(low, v, v_extra)
        vb_o[b] = jnp.where(low, v_extra, v)
    dk_s[...] = jnp.zeros(dk_s.shape, F32)
    dv_s[...] = jnp.zeros(dv_s.shape, F32)
    sides = ((ka_e, vb_e), (ka_o, vb_o))
    given = []
    for i in range(3):
        rows = slice(i * BLK, (i + 1) * BLK)
        d_out = do_ref[rows, :]
        product = d_out.astype(F32) * o_ref[rows, :].astype(F32)
        qas = (qe_ref[rows, :], qo_ref[rows, :])
        d_augs = []
        for head in range(2):
            mine = low if head == 0 else jnp.logical_not(low)
            delta = jnp.sum(jnp.where(mine, product, 0.0), -1, keepdims=True)
            high, mid, small = split_three(-delta)
            extra = jnp.where(place == 0, high, jnp.where(place == 1, mid, jnp.where(place == 2, small, zero)))
            d_augs.append(jnp.where(mine, d_out, extra))
        given.append((qas, d_augs, d_out.T, jnp.where(low, qas[0], qas[1]).T))

    def score(unit, j):
        i, head = unit
        b = tab[4 * i + j]
        qas, d_augs = given[i][:2]
        return dot_nt(qas[head], sides[head][0][b]), dot_nt(d_augs[head], sides[head][1][b])

    units = [(i, head) for i in range(3) for head in range(2)]
    now = [score(units[0], j) for j in range(4)]
    for n, (i, head) in enumerate(units):
        lanes = slice(head * HDIM, (head + 1) * HDIM)
        dot_t, qt = given[i][2:]
        dq = jnp.zeros((BLK, 128), F32)
        later = []
        for j in range(4):
            if n + 1 < len(units):
                later.append(score(units[n + 1], j))
            b = tab[4 * i + j]
            probs = jnp.exp(now[j][0])
            d_scores = (probs * now[j][1]).astype(BF)
            dv_s[b, lanes, :] += dot_nn(dot_t[lanes, :], probs.astype(BF))
            dk_s[b, lanes, :] += dot_nn(qt[lanes, :], d_scores)
            dq = dq + dot_nn(d_scores, k_ref[pl.ds(pl.multiple_of(b * BLK, BLK), BLK), :])
        now = later
        if head == 0:
            even = dq
        else:
            dq_ref[i * BLK : (i + 1) * BLK, :] = (jnp.where(low, even, dq) * 0.125).astype(BF)
    for b in range(8):
        dk = dk_s[b].T.astype(BF)
        dv = dv_s[b].T.astype(BF)
        dk_ref[b * BLK : (b + 1) * BLK, :] = dk
        dv_ref[b * BLK : (b + 1) * BLK, :] = dv
        dkv_s[b * BLK : (b + 1) * BLK, :128] = dk
        dkv_s[b * BLK : (b + 1) * BLK, 128:] = dv
    dq_all = dq_ref[...]
    db_ref[0:1, :] = jnp.sum(dq_all.astype(F32), 0, keepdims=True)
    db_ref[1:2, :] = jnp.sum(dkv_s[:, 128:].astype(F32), 0, keepdims=True)
    dw_q = dot_nn(xt_ref[:, :ROWS], dq_all).astype(BF)
    dw_kv = dot_nn(xt_ref[...], dkv_s[...]).astype(BF)
    for n, grad in enumerate((dw_q, dw_kv[:, :128], dw_kv[:, 128:])):
        grad = grad.reshape(RB // 2, 2, RP, 128)
        for pos in range(RB // 2):
            keep_ref[pos ^ tab[21], n] = jnp.where(tab[20] == 0, grad[pos, 0], grad[pos, 1])
            give_ref[pos ^ tab[21], n] = jnp.where(tab[20] == 0, grad[pos, 1], grad[pos, 0])


def gelu_both(pre):
    size = jnp.abs(pre)
    bell = jnp.exp(pre * pre * -0.5)
    t = 1.0 / (1.0 + size * (0.3275911 * math.sqrt(0.5)))
    poly = t * (
        0.5 * 0.254829592
        + t * (0.5 * -0.284496736 + t * (0.5 * 1.421413741 + t * (0.5 * -1.453152027 + t * (0.5 * 1.061405429))))
    )
    tail = poly * bell
    phi = jnp.where(pre >= 0, 1.0 - tail, tail)
    return pre * phi, phi + pre * bell * (1.0 / math.sqrt(2.0 * math.pi))


def norm_parts(summed):
    average = jnp.mean(summed, -1, keepdims=True)
    centered = summed - average
    variance = jnp.mean(centered * centered, -1, keepdims=True)
    root = lax.rsqrt(variance + LN_EPS)
    return centered * root, root


def norm_back(cot, gain, hat, root):
    gz = cot * gain
    return root * (gz - jnp.mean(gz, -1, keepdims=True) - hat * jnp.mean(gz * hat, -1, keepdims=True))


def feed_kernel(tab, o_ref, x_ref, *refs):
    pieces = refs[:8]
    vec_ref, w_ref, cot_ref, weight_ref, out_ref, dw_ref, dz1_ref, do_ref, sums_ref, db1_ref = refs[8:18]
    wo_s, h1b_s, h1t_s, hat1_s, root1_s, z2_s, u_s, gp_s, e2_s, e2t_s, ep_s = refs[18:]
    step = pl.program_id(0)
    blocks = [slice(i * HALF, (i + 1) * HALF) for i in range(2)]

    @pl.when(step == 0)
    def _():
        assemble(tab, pieces, 0, wo_s, 0)
        for rows in blocks:
            z1 = x_ref[rows, :].astype(F32) + dot_nt(o_ref[rows, :], wo_s[...]) + vec_ref[2:3, :]
            hat, root = norm_parts(z1)
            h1 = hat * vec_ref[3:4, :] + vec_ref[4:5, :]
            hat1_s[rows, :] = hat
            root1_s[rows, :] = root
            z2_s[rows, :] = h1 + vec_ref[5:6, :]
            h1b = h1.astype(BF)
            h1b_s[rows, :] = h1b
            h1t_s[:, rows] = h1b.T

    @pl.when(step < 4)
    def _():
        w1 = w_ref[:, 0, 0].reshape(D, D)
        w2t = w_ref[:, 0, 1].reshape(D, D)
        bias = vec_ref[pl.ds(8 + step, 1), :]
        now = dot_nn(h1b_s[:HALF, :], w1)
        for i, rows in enumerate(blocks):
            later = dot_nn(h1b_s[blocks[1], :], w1) if i == 0 else None
            act, slope = gelu_both(now + bias)
            act = act.astype(BF)
            u_s[step, rows, :] = act
            gp_s[step, rows, :] = slope.astype(BF)
            now = later
        z2_s[...] += dot_nt(u_s[step], w2t)

    @pl.when(step == 3)
    def _():
        sums = [jnp.zeros((1, D), F32) for _ in range(3)]
        for rows in blocks:
            hat, root = norm_parts(z2_s[rows, :])
            out_ref[rows, :] = (hat * vec_ref[6:7, :] + vec_ref[7:8, :]).astype(BF)
            cot = cot_ref[rows, :].astype(F32) * weight_ref[rows, :]
            dz2 = norm_back(cot, vec_ref[6:7, :], hat, root)
            z2_s[rows, :] = dz2
            e2 = dz2.astype(BF)
            e2_s[rows, :] = e2
            e2t_s[:, rows] = e2.T
            sums[0] += jnp.sum(dz2, 0, keepdims=True)
            sums[1] += jnp.sum(cot * hat, 0, keepdims=True)
            sums[2] += jnp.sum(cot, 0, keepdims=True)
        for n in range(3):
            sums_ref[3 + n : 4 + n, :] = sums[n]

    @pl.when(jnp.logical_and(step >= 4, step < 8))
    def _():
        m = step - 4
        w1 = w_ref[:, 0, 0].reshape(D, D)
        w2t = w_ref[:, 0, 1].reshape(D, D)
        db1 = jnp.zeros((1, D), F32)
        now = dot_nn(e2_s[:HALF, :], w2t)
        for i, rows in enumerate(blocks):
            later = dot_nn(e2_s[blocks[1], :], w2t) if i == 0 else None
            ep = (gp_s[m, rows, :].astype(F32) * now).astype(BF)
            ep_s[rows, :] = ep
            db1 += jnp.sum(ep.astype(F32), 0, keepdims=True)
            z2_s[rows, :] += dot_nt(ep, w1)
            now = later
        db1_ref[pl.ds(m, 1), :] = db1
        dw_ref[:, :RP] = dot_nn(h1t_s[...], ep_s[...]).astype(BF).reshape(RB, RP, D)
        dw_ref[:, RP:] = dot_nn(e2t_s[...], u_s[m]).astype(BF).reshape(RB, RP, D)

    @pl.when(step == 8)
    def _():
        sums = [jnp.zeros((1, D), F32) for _ in range(3)]
        for rows in blocks:
            dh = z2_s[rows, :]
            hat = hat1_s[rows, :]
            dz1 = norm_back(dh, vec_ref[3:4, :], hat, root1_s[rows, :])
            dz1_ref[rows, :] = dz1
            e1 = dz1.astype(BF)
            e2t_s[:, rows] = e1.T
            do_ref[rows, :] = dot_nn(e1, wo_s[...]).astype(BF)
            sums[0] += jnp.sum(dz1, 0, keepdims=True)
            sums[1] += jnp.sum(dh * hat, 0, keepdims=True)
            sums[2] += jnp.sum(dh, 0, keepdims=True)
        for n in range(3):
            sums_ref[n : n + 1, :] = sums[n]
        dw_ref[:, :RP] = dot_nn(e2t_s[...], o_ref[...]).astype(BF).reshape(RB, RP, D)


def pack_kernel(tab, own_ref, *rest):
    others, out_ref, line_s = rest[:-2], rest[-2], rest[-1]
    line_s[0] = own_ref[...]
    for n, ref in enumerate(others):
        line_s[n + 1] = ref[...]
    width = own_ref.shape[-1] // 4
    for m in range(4):
        shard = line_s[m ^ tab[0]]
        for n in range(4):
            out_ref[n, :, m * width : (m + 1) * width] = shard[:, n * width : (n + 1) * width]


def input_rest_kernel(tab, dk_ref, dv_ref, *refs):
    pieces, (nb_ref, mid_ref, w_s) = refs[:8], refs[8:]
    step = pl.program_id(0)

    @pl.when(step == 0)
    def _():
        for part in range(2):
            assemble(tab, pieces, part + 1, w_s, D * part)

    back = (dot_nt(dk_ref[...], w_s[:, :D]) + dot_nt(dv_ref[...], w_s[:, D:])).astype(BF)

    @pl.when(step < 3)
    def _():
        nb_ref[...] = back

    @pl.when(step >= 3)
    def _():
        mid_ref[...] = back


def input_own_kernel(tab, dq_ref, dk_ref, dv_ref, *refs):
    pieces, (dz1_ref, own_ref, w_s) = refs[:8], refs[8:]

    @pl.when(pl.program_id(0) == 0)
    def _():
        for part in range(3):
            assemble(tab, pieces, part, w_s, D * part)

    back = dot_nt(dk_ref[...], w_s[:, D : 2 * D]) + dot_nt(dv_ref[...], w_s[:, 2 * D :])
    own_ref[...] = back + dot_nt(dq_ref[...], w_s[:, :D]) + dz1_ref[...]


def head_line_kernel(z_ref, own_ref, *refs):
    others, outs = refs[:-4], refs[-4:]
    total = own_ref[...].astype(F32)
    for ref in others:
        total = total + ref[...].astype(F32)
    total = total.astype(BF)
    width = D // 4
    for m in range(4):
        at = slice(m * width, (m + 1) * width)
        mine = jnp.concatenate([total[kind, :, at] for kind in range(3)], 1)
        for n, ref in enumerate(outs):

            @pl.when((m ^ z_ref[0]) == n)
            def _():
                ref[...] = mine


def feed_line_kernel(z_ref, feed_ref, *outs):
    width = D // 4
    rows = outs[0].shape[0]
    for m in range(4):
        for n, ref in enumerate(outs):

            @pl.when((m ^ z_ref[0]) == n)
            def _():
                ref[:, :D] = feed_ref[2 * m * rows : (2 * m + 1) * rows, :]
                ref[:, D : 2 * D] = feed_ref[(2 * m + 1) * rows : (2 * m + 2) * rows, :]
                ref[:, 2 * D :] = feed_ref[8 * rows :, m * width : (m + 1) * width]


def call(kernel, grid, in_specs, out_specs, out_shape, scratch, flops, bytes_accessed, name):
    return pl.pallas_call(
        kernel,
        grid_spec=pltpu.PrefetchScalarGridSpec(
            num_scalar_prefetch=1, grid=(grid,), in_specs=in_specs, out_specs=out_specs, scratch_shapes=scratch
        ),
        out_shape=out_shape,
        compiler_params=pltpu.CompilerParams(
            dimension_semantics=("arbitrary",), vmem_limit_bytes=VMEM_LIMIT
        ),
        cost_estimate=pl.CostEstimate(flops=flops, bytes_accessed=bytes_accessed, transcendentals=0),
        name=name,
    )


def whole(*shape):
    return pl.BlockSpec(shape, lambda s, t: (0,) * len(shape))


def columns(rows, width=128):
    return pl.BlockSpec((rows, width), lambda s, t: (0, s))


def shape_of(shape, dtype):
    return jax.ShapeDtypeStruct(shape, dtype)


def vm(shape, dtype):
    return pltpu.VMEM(shape, dtype)


def attend(tab, own, nb, mid, pieces, vectors):
    w_spec = pl.BlockSpec((3, RP, 128), lambda s, t: (0, 0, s))
    return call(
        attend_kernel,
        PAIRS,
        [whole(ROWS, D), whole(ROWS, D), whole(2 * BLK, D)] + [w_spec] * 8 + [columns(12)],
        [columns(ROWS), columns(ROWS), columns(ROWS), columns(8 * BLK), columns(8 * BLK)]
        + [pl.BlockSpec((128, 8 * BLK), lambda s, t: (s, 0))],
        [shape_of((ROWS, D), BF)] * 3 + [shape_of((8 * BLK, D), BF)] * 2 + [shape_of((D, 8 * BLK), BF)],
        [vm((D, 384), BF)] + [vm((8, BLK, 128), BF)] * 2 + [vm((2, 8, BLK, 128), BF), vm((8, BLK, 128), BF)],
        5_000_000_000,
        16_000_000,
        "attend",
    )(tab, own, nb, mid, *pieces, vectors)


def attend_back(tab, qe, qo, k, v, d_out, o, xt):
    return call(
        attend_back_kernel,
        PAIRS,
        [columns(ROWS), columns(ROWS), columns(8 * BLK), columns(8 * BLK), columns(ROWS), columns(ROWS), whole(D, 8 * BLK)],
        [
            columns(ROWS),
            columns(8 * BLK),
            columns(8 * BLK),
            pl.BlockSpec((RB // 2, 3, RP, 128), lambda s, t: (0, 0, 0, s)),
            pl.BlockSpec((RB // 2, 3, RP, 128), lambda s, t: (0, 0, 0, s)),
            columns(2),
        ],
        [
            shape_of((ROWS, D), BF),
            shape_of((8 * BLK, D), BF),
            shape_of((8 * BLK, D), BF),
            shape_of((RB // 2, 3, RP, D), BF),
            shape_of((RB // 2, 3, RP, D), BF),
            shape_of((2, D), F32),
        ],
        [vm((8, BLK, 128), BF)] * 5
        + [vm((8, 128, BLK), F32)] * 2
        + [vm((8 * BLK, BLK), BF)],
        50_000_000_000,
        24_000_000,
        "attend_back",
    )(tab, qe, qo, k, v, d_out, o, xt)


def feed(tab, o, x, pieces, vectors, w, cot, weight):
    wo_spec = pl.BlockSpec((1, RP, D), lambda s, t: (3, 0, 0))

    def group(s):
        return jnp.where(s < 4, s, jnp.minimum(s - 4, 3))

    return call(
        feed_kernel,
        9,
        [
            whole(ROWS, D),
            whole(ROWS, D),
            *[wo_spec] * 8,
            whole(12, D),
            pl.BlockSpec((RB, 1, 2, RP, D), lambda s, t: (0, group(s), 0, 0, 0)),
            whole(ROWS, D),
            whole(ROWS, 1),
        ],
        [
            whole(ROWS, D),
            pl.BlockSpec((RB, 2 * RP, D), lambda s, t: (0, jnp.maximum(s - 4, 0), 0)),
            whole(ROWS, D),
            whole(ROWS, D),
            whole(6, D),
            whole(4, D),
        ],
        [
            shape_of((ROWS, D), BF),
            shape_of((RB, 9 * RP, D), BF),
            shape_of((ROWS, D), F32),
            shape_of((ROWS, D), BF),
            shape_of((6, D), F32),
            shape_of((4, D), F32),
        ],
        [
            vm((D, D), BF),
            vm((ROWS, D), BF),
            vm((D, ROWS), BF),
            vm((ROWS, D), F32),
            vm((ROWS, 1), F32),
            vm((ROWS, D), F32),
            vm((4, ROWS, D), BF),
            vm((4, ROWS, D), BF),
            vm((ROWS, D), BF),
            vm((D, ROWS), BF),
            vm((ROWS, D), BF),
        ],
        40_000_000_000,
        48_000_000,
        "feed",
    )(tab, o, x, *pieces, vectors, w, cot, weight)


def round_kernel(qkv_ref, proj_ref, up_ref, down_ref, mine_ref, feed_ref):
    width = qkv_ref.shape[-1]
    for n in range(3):
        mine_ref[:, n * width : (n + 1) * width] = qkv_ref[n].astype(BF)
    mine_ref[:, 3 * width :] = proj_ref[...].T.astype(BF)
    feed_ref[0] = up_ref[...].astype(BF)
    feed_ref[1] = down_ref[...].astype(BF)


def round_shards(qkv, proj, up, down):
    rows = up.shape[0]
    return pl.pallas_call(
        round_kernel,
        in_specs=[pl.BlockSpec(memory_space=pltpu.VMEM)] * 4,
        out_specs=[pl.BlockSpec(memory_space=pltpu.VMEM)] * 2,
        out_shape=[shape_of((rows, D), BF), shape_of((2, rows, D), BF)],
        cost_estimate=pl.CostEstimate(flops=1_000_000, bytes_accessed=1_500_000, transcendentals=0),
        name="round_shards",
    )(qkv, proj, up, down)


def pack_line(z, own, others):
    rows, width = own.shape
    return call(
        pack_kernel,
        1,
        [whole(rows, width)] * 4,
        whole(4, rows, D),
        shape_of((4, rows, D), BF),
        [vm((4, rows, width), BF)],
        60_000_000_000,
        1_000_000,
        "pack_line",
    )(z.reshape(1).astype(jnp.int32), own, *others)


def input_rest(tab, dk, dv, pieces):
    w_spec = whole(3, RP, D)
    each = pl.BlockSpec((BLK, D), lambda s, t: (s + 3, 0))
    return call(
        input_rest_kernel,
        5,
        [each, each] + [w_spec] * 8,
        [
            pl.BlockSpec((BLK, D), lambda s, t: (jnp.minimum(s, 2), 0)),
            pl.BlockSpec((BLK, D), lambda s, t: (jnp.maximum(s - 3, 0), 0)),
        ],
        [shape_of((3 * BLK, D), BF), shape_of((2 * BLK, D), BF)],
        [vm((D, 2 * D), BF)],
        8_000_000_000,
        12_000_000,
        "input_rest",
    )(tab, dk, dv, *pieces)


def input_own(tab, dq, dk, dv, pieces, dz1):
    w_spec = whole(3, RP, D)
    each = pl.BlockSpec((BLK, D), lambda s, t: (s, 0))
    return call(
        input_own_kernel,
        3,
        [each, each, each] + [w_spec] * 8 + [each],
        each,
        shape_of((ROWS, D), F32),
        [vm((D, 3 * D), BF)],
        5_000_000_000,
        12_000_000,
        "input_own",
    )(tab, dq, dk, dv, *pieces, dz1)


def in_line(kernel, name, rows, width, z, *parts):
    return pl.pallas_call(
        kernel,
        in_specs=[pl.BlockSpec(memory_space=pltpu.SMEM)] + [pl.BlockSpec(memory_space=pltpu.VMEM)] * len(parts),
        out_specs=[pl.BlockSpec(memory_space=pltpu.VMEM)] * 4,
        out_shape=[shape_of((rows, width), BF)] * 4,
        compiler_params=pltpu.CompilerParams(vmem_limit_bytes=VMEM_LIMIT),
        cost_estimate=pl.CostEstimate(flops=2_000_000, bytes_accessed=4_000_000, transcendentals=0),
        name=name,
    )(z.reshape(1).astype(jnp.int32), *parts)


def adamw(weight, clipped, first, second, rate, decay):
    first_new = BETA_ONE * first + (1.0 - BETA_ONE) * clipped
    second_new = BETA_TWO * second + (1.0 - BETA_TWO) * clipped * clipped
    first_hat = first_new / (1.0 - BETA_ONE**STEP)
    second_hat = second_new / (1.0 - BETA_TWO**STEP)
    updated = weight * (1.0 - rate * decay) - rate * first_hat / (jnp.sqrt(second_hat) + ADAM_EPS)
    return (clipped, first_new, second_new, updated)


def update_kernel(squares_ref, head_ref, feed_ref, vec_ref, *refs):
    ins, norm_ref, outs = refs[:15], refs[15], refs[16:]
    norm = jnp.sqrt(jnp.sum(squares_ref[...], keepdims=True))
    norm_ref[...] = norm
    clip = jnp.minimum(1.0, CLIP_NORM / (norm + 1e-06))
    head = head_ref[...]
    fed = feed_ref[...]
    width = D // 4
    grads = (
        [head[:, n * width : (n + 1) * width] for n in range(3)],
        [fed[:, 2 * D :].T],
        [fed[:, :D]],
        [fed[:, D : 2 * D]],
        [vec_ref[...]],
    )
    for kind, parts in enumerate(grads):
        rate, decay = (VECTOR_RATE, 0.0) if kind == 4 else (MATRIX_RATE / math.sqrt(D), WEIGHT_DECAY)
        for n, grad in enumerate(parts):
            at = n if kind == 0 else Ellipsis
            results = adamw(ins[kind][at], grad * clip, ins[5 + kind][at], ins[10 + kind][at], rate, decay)
            for m, result in enumerate(results):
                outs[4 * kind + m][at] = result


def update(squares, sums, vec, weights, firsts, seconds):
    vmem = pl.BlockSpec(memory_space=pltpu.VMEM)
    return pl.pallas_call(
        update_kernel,
        in_specs=[vmem] * 19,
        out_specs=[vmem] * 21,
        out_shape=[shape_of((1, 1), F32)] + [shape_of(one.shape, F32) for one in weights for _ in range(4)],
        compiler_params=pltpu.CompilerParams(vmem_limit_bytes=VMEM_LIMIT),
        cost_estimate=pl.CostEstimate(flops=10_000_000, bytes_accessed=8_000_000, transcendentals=0),
        name="update",
    )(squares, *sums, vec, *weights, *firsts, *seconds)


def total_kernel(vec_ref, *refs):
    vec = jnp.sum(vec_ref[...], 0, keepdims=True)
    refs[10][...] = vec
    square = jnp.sum(vec * vec, keepdims=True)
    for n in range(2):
        sums = refs[4 * n][...].astype(F32)
        for ref in refs[4 * n + 1 : 4 * n + 4]:
            sums = sums + ref[...].astype(F32)
        refs[8 + n][...] = sums
        square = square + jnp.sum(sums * sums, keepdims=True)
    refs[11][...] = jnp.broadcast_to(square, refs[11].shape)


def total(vec, groups, devices):
    vmem = pl.BlockSpec(memory_space=pltpu.VMEM)
    *sums, vec_sum, square = pl.pallas_call(
        total_kernel,
        in_specs=[vmem] * 9,
        out_specs=[vmem] * 4,
        out_shape=[shape_of(group[0].shape, F32) for group in groups]
        + [shape_of((1, vec.shape[1]), F32), shape_of((devices, 1), F32)],
        compiler_params=pltpu.CompilerParams(vmem_limit_bytes=VMEM_LIMIT),
        cost_estimate=pl.CostEstimate(flops=2_000_000, bytes_accessed=4_000_000, transcendentals=0),
        name="total",
    )(vec, *[one for group in groups for one in group])
    return sums, vec_sum, square


def shards(
    tokens,
    out_cotangent,
    lengths,
    starts,
    ends,
    flags,
    qkv_master,
    proj_master,
    up_master,
    down_master,
    vectors,
    qkv_first,
    proj_first,
    up_first,
    down_first,
    qkv_second,
    proj_second,
    up_second,
    down_second,
    vector_first,
    vector_second,
):
    mp_count = lax.axis_size("mp")
    dp_count = lax.axis_size("dp")
    devices = mp_count * dp_count
    z = lax.axis_index("mp")
    dp_index = lax.axis_index("dp")
    core = dp_index % 2
    chips = dp_count // 2
    part = D // dp_count
    head_cols = D // mp_count

    def linear(chip, core_of, z_of):
        return (chip * 2 + core_of) * mp_count + z_of

    def permutation(move):
        return [
            (linear(chip, c, k), linear(*move(chip, c, k)))
            for chip in range(chips)
            for c in range(2)
            for k in range(mp_count)
        ]

    planes = [[linear(chip, c, k) for chip in range(chips)] for c in range(2) for k in range(mp_count)]
    swap_core = permutation(lambda chip, c, k: (chip, 1 - c, k))
    swap_z = [permutation(lambda chip, c, k, n=n: (chip, c, k ^ n)) for n in range(mp_count)]
    swap_chip = [permutation(lambda chip, c, k, n=n: (chip ^ n, c, k)) for n in range(chips)]
    middle = (0, 2, 1, 3)
    swap_mid = permutation(lambda chip, c, k: (chip, c, middle[k]))
    chip_index = dp_index // 2

    def over_plane(value):
        return lax.all_to_all(value, AXES, 0, 0, tiled=True, axis_index_groups=planes)

    def over_z(value):
        return lax.all_to_all(value, "mp", 0, 0, tiled=True)

    def absolute(same, other):
        order = jnp.arange(chips, dtype=jnp.int32) ^ chip_index
        same, other = jnp.stack(same)[order], jnp.stack(other)[order]
        both = jnp.where(core == 0, jnp.stack([same, other], 1), jnp.stack([other, same], 1))
        kinds = both.shape[2]
        both = both.transpose(2, 0, 1, 3, 4).reshape(kinds, RB // 2, 2, RP, D).transpose(1, 2, 0, 3, 4)
        return [both[n, half] for half in range(2) for n in range(RB // 2)]

    mine, feed_mine = round_shards(qkv_master, proj_master, up_master, down_master.T)
    feed_w = lax.all_gather(feed_mine, AXES, axis=0, tiled=False).reshape(dp_count, mp_count, 2, part, D)
    line = [lax.ppermute(mine, AXES, swap_z[n]) for n in range(1, mp_count)]
    tokens_late, mine, *line = lax.optimization_barrier((tokens, mine, *line))
    along_z = pack_line(z, mine, line)
    mid_at = jnp.where(z == 1, BLK, 0)
    nb = lax.ppermute(tokens_late, AXES, swap_z[1])
    mid = lax.ppermute(lax.dynamic_slice_in_dim(tokens_late, mid_at, 2 * BLK, 0), AXES, swap_mid)
    same = [along_z] + [lax.ppermute(along_z, AXES, swap_chip[n]) for n in range(1, chips)]
    first, same[1], nb = lax.optimization_barrier((along_z, same[1], nb))
    other = [lax.ppermute(one, AXES, swap_core) for one in [first] + same[1:]]
    pieces = same + other
    kernel_core, kernel_chip = core, chip_index
    if part != RP:
        pieces = absolute(same, other)
        feed_w = feed_w.transpose(1, 2, 0, 3, 4).reshape(mp_count, 2, RB, RP, D).transpose(2, 0, 1, 3, 4)
        kernel_core = kernel_chip = jnp.zeros((), jnp.int32)

    place = jnp.asarray(BLOCK_PLACE)[z]
    counts = jnp.clip(lengths[jnp.asarray(BLOCK_SEQ)[z]] - BLK * place, 0, BLK)
    tab = jnp.concatenate(
        [jnp.asarray(KEY_BLOCKS)[z].reshape(12), counts, kernel_core.reshape(1), kernel_chip.reshape(1)]
    ).astype(jnp.int32)

    positions = z * ROWS + jnp.arange(ROWS, dtype=jnp.int32)
    seq_of = positions // LEN
    within = positions % LEN
    picker = (seq_of[:, None] == jnp.arange(lengths.shape[0], dtype=jnp.int32)[None, :]).astype(jnp.int32)
    length_row = jnp.sum(picker * lengths[None, :], 1)
    start_row = jnp.sum(picker * starts[None, :], 1)
    end_row = jnp.sum(picker * ends[None, :], 1)
    flag_row = jnp.sum(picker * flags[None, :], 1).astype(F32)
    valid_row = (within < length_row).astype(F32)
    answer = (within == start_row).astype(F32) + (within == end_row).astype(F32)
    opening = (within == 0).astype(F32)
    row_weight = valid_row * (1.0 + 2.0 * (1.0 - flag_row) * answer + 4.0 * flag_row * opening)

    o, qe, qo, k, v, xt = attend(tab, tokens, nb, mid, pieces, vectors)
    block_out, feed_dw, dz1, d_o, sums_norm, bias_up_grad = feed(
        tab, o, tokens, pieces, vectors, feed_w, out_cotangent, row_weight[:, None]
    )

    def to_parts(grad):
        if part == RP:
            return grad
        lead = grad.shape[1:-2]
        moved = jnp.moveaxis(grad, 0, -3).reshape(*lead, dp_count, part, D)
        return jnp.moveaxis(moved, -3, 0)

    if part != RP:
        feed_dw = to_parts(feed_dw.reshape(RB, 9, RP, D)).reshape(dp_count, 9 * part, D)
    feed_part = lax.psum_scatter(feed_dw, "dp", scatter_dimension=0, tiled=False)

    dq, dk, dv, keep, give, sums_head = attend_back(tab, qe, qo, k, v, d_o, o, xt)
    if part != RP:
        both = jnp.stack([keep, give], 1).reshape(RB, 3, RP, D)
        both = to_parts(both).reshape(chips, 2, 3, part, D)
        order = jnp.arange(chips, dtype=jnp.int32) ^ chip_index
        keep = lax.dynamic_index_in_dim(both, core, 1, keepdims=False)[order]
        give = lax.dynamic_index_in_dim(both, 1 - core, 1, keepdims=False)[order]
    got = lax.ppermute(give, AXES, swap_core)
    chip_sum = (keep.astype(F32) + got.astype(F32)).astype(BF)
    to_nb, to_mid = input_rest(tab, dk, dv, pieces)
    chip_sum, dq, dk, dv, sums_head, to_nb, to_mid = lax.optimization_barrier(
        (chip_sum, dq, dk, dv, sums_head, to_nb, to_mid)
    )
    from_chips = [lax.ppermute(chip_sum[n], AXES, swap_chip[n]) for n in range(1, chips)]
    from_nb = lax.ppermute(to_nb, AXES, swap_z[1])
    from_mid = lax.ppermute(to_mid, AXES, swap_mid)
    dx_own = input_own(tab, dq, dk, dv, pieces, dz1)
    vector_part = jnp.concatenate([sums_head, sums_norm, bias_up_grad], 0)
    vec_columns = D // devices
    vector_part = vector_part.reshape(12, devices, vec_columns).transpose(1, 0, 2).reshape(devices, 12 * vec_columns)
    vector_parts = lax.all_to_all(vector_part, AXES, 0, 0, tiled=True)
    vector_parts, dx_own, from_nb, from_mid, *from_chips = lax.optimization_barrier(
        (vector_parts, dx_own, from_nb, from_mid, *from_chips)
    )

    def along_line(parts):
        return [parts[0]] + [lax.ppermute(parts[n], AXES, swap_z[n]) for n in range(1, mp_count)]

    head_line = along_line(in_line(head_line_kernel, "head_line", part, 3 * D // 4, z, chip_sum[0], *from_chips))
    feed_part, *head_line = lax.optimization_barrier((feed_part, *head_line))
    feed_line = along_line(in_line(feed_line_kernel, "feed_line", part, 2 * D + D // 4, z, feed_part))
    zero_block = jnp.zeros((BLK, D), BF)
    from_mid = jnp.where(
        z == 1, jnp.concatenate([zero_block, from_mid], 0), jnp.concatenate([from_mid, zero_block], 0)
    )
    input_grad = dx_own + from_nb.astype(F32) + from_mid.astype(F32)

    sums, vector_grad, square = total(vector_parts, (head_line, feed_line), devices)
    vector_grad = vector_grad.reshape(12, vec_columns)
    squares = lax.all_to_all(square, AXES, 0, 0, tiled=True)
    vec_index = dp_index * mp_count + z
    vector_shard = lax.dynamic_slice_in_dim(vectors, vec_index * vec_columns, vec_columns, 1)
    grad_norm, *results = update(
        squares,
        sums,
        vector_grad,
        (qkv_master, proj_master, up_master, down_master.T, vector_shard),
        (qkv_first, proj_first, up_first, down_first.T, vector_first),
        (qkv_second, proj_second, up_second, down_second.T, vector_second),
    )
    down_set = [one.T for one in results[12:16]]
    return (block_out, input_grad, grad_norm.reshape(()), *results[:12], *down_set, *results[16:])


def solution(mesh):
    rows = P(AXES, None)
    group = P("dp")
    qkv = P(None, "dp", "mp")
    proj = P("mp", "dp")
    up = P("dp", "mp")
    vec = P(None, AXES)
    return jax.shard_map(
        shards,
        mesh=mesh,
        in_specs=(rows, rows, group, group, group, group)
        + (qkv, proj, up, proj, P())
        + (qkv, proj, up, proj) * 2
        + (vec, vec),
        out_specs=(rows, rows, P()) + (qkv,) * 4 + (proj,) * 4 + (up,) * 4 + (proj,) * 4 + (vec,) * 4,
        check_vma=False,
    )
```

```python
from functools import partial
import math

import jax
import jax.numpy as jnp
import numpy as np
from jax import lax
from jax.experimental import pallas as pl
from jax.experimental.pallas import tpu as pltpu
from jax.sharding import PartitionSpec as P

D = 768
HEADS = 12
HDIM = 64
FF = 3072
LEN = 1024
STEP = 10

LN_EPS = 1e-06
BETA_ONE = 0.9
BETA_TWO = 0.999
ADAM_EPS = 1e-08
WEIGHT_DECAY = 0.01
CLIP_NORM = 1.0
VECTOR_RATE = 1.0
MATRIX_RATE = 2.0
NEG_FILL = -1e30

BF = jnp.bfloat16
F32 = jnp.float32
AXES = ("dp", "mp")
BLK = 256
ROWS = 768
HALF = ROWS // 2
PAIRS = HEADS // 2
RB = 8
RP = D // RB
VMEM_LIMIT = 60 * 1024 * 1024

KEY_BLOCKS = np.array(
    [
        [[0, 1, 2, 3]] * 3,
        [[3, 4, 5, 0], [1, 2, 6, 7], [1, 2, 6, 7]],
        [[6, 7, 0, 1], [6, 7, 0, 1], [2, 3, 4, 5]],
        [[5, 0, 1, 2]] * 3,
    ],
    np.int32,
)
BLOCK_SEQ = np.array(
    [[0, 0, 0, 0, 0, 0, 0, 0], [0, 1, 1, 0, 0, 0, 1, 1], [1, 1, 2, 2, 2, 2, 1, 1], [2, 2, 2, 2, 2, 2, 2, 2]], np.int32
)
BLOCK_PLACE = np.array(
    [[0, 1, 2, 3, 4, 4, 4, 4], [3, 0, 1, 0, 1, 2, 2, 3], [2, 3, 0, 1, 2, 3, 0, 1], [1, 2, 3, 4, 4, 0, 4, 4]], np.int32
)


def dot_nn(left, right):
    return jnp.dot(left, right, preferred_element_type=F32)


def dot_nt(left, right):
    return lax.dot_general(left, right, (((1,), (1,)), ((), ())), preferred_element_type=F32)


def lane_ids(rows):
    return lax.broadcasted_iota(jnp.int32, (rows, 128), 1)


def assemble(tab, pieces, part, target, col):
    width = pieces[0].shape[-1]
    core, chip = tab[20], tab[21]
    for n in range(4):
        for half in range(2):
            at = ((n ^ chip) * 2 + (core ^ half)) * RP
            target[pl.ds(pl.multiple_of(at, RP), RP), col : col + width] = pieces[4 * half + n][part]


def key_extra(count):
    place = lane_ids(BLK) % HDIM
    row = lax.broadcasted_iota(jnp.int32, (BLK, 128), 0)
    mask = jnp.where(row >= count, NEG_FILL, 0.0)
    return jnp.where(place == 0, mask, jnp.where(place <= 3, 1.0, 0.0)).astype(BF)


def split_three(value):
    high = value.astype(BF)
    rest = value - high.astype(F32)
    mid = rest.astype(BF)
    low = (rest - mid.astype(F32)).astype(BF)
    return high, mid, low


def attend_kernel(
    tab, own_ref, nb_ref, mid_ref, *refs
):
    pieces = refs[:8]
    vec_ref, o_ref, qe_ref, qo_ref, k_ref, v_ref, xt_ref, w_s, ka_e, ka_o, va_s, extra_s = refs[8:]
    mine = pl.ds(pl.multiple_of(pl.program_id(0) * 128, 128), 128)

    @pl.when(pl.program_id(0) == 0)
    def _():
        for b in range(8):
            extra_s[b] = key_extra(tab[12 + b])

    for part in range(3):
        assemble(tab, pieces, part, w_s, 128 * part)
    bias_q = vec_ref[0:1, :]
    bias_v = vec_ref[1:2, :]
    low = lane_ids(BLK) < HDIM
    place = lane_ids(BLK) % HDIM
    ones = jnp.ones((BLK, 128), BF)
    for src, first, count in ((own_ref, 0, 3), (nb_ref, 3, 3), (mid_ref, 6, 2)):
        at = slice(first * BLK, (first + count) * BLK)
        xt_ref[:, at] = src[:, mine].T
        kv = dot_nn(src[...], w_s[:, 128:384])
        k_ref[at, :] = kv[:, :128].astype(BF)
        v_ref[at, :] = (kv[:, 128:] + bias_v).astype(BF)
    for b in range(8):
        at = slice(b * BLK, (b + 1) * BLK)
        k = k_ref[at, :]
        ka_e[b] = jnp.where(low, k, extra_s[b])
        ka_o[b] = jnp.where(low, extra_s[b], k)
        va_s[0, b] = jnp.where(low, v_ref[at, :], ones)
        va_s[1, b] = jnp.where(low, ones, v_ref[at, :])
    q_extra = jnp.where(place == 0, 1.0, 0.0).astype(BF)
    queries = []
    for i in range(3):
        q = (dot_nn(own_ref[i * BLK : (i + 1) * BLK, :], w_s[:, :128]) + bias_q).astype(BF) * jnp.asarray(0.125, BF)
        queries.append((jnp.where(low, q, q_extra), jnp.where(low, q_extra, q)))
    keys = (ka_e, ka_o)

    def score(unit, j):
        i, head = unit
        return dot_nt(queries[i][head], keys[head][tab[4 * i + j]])

    units = [(i, head) for i in range(3) for head in range(2)]
    now = [score(units[0], j) for j in range(4)]
    for n, (i, head) in enumerate(units):
        peak = jnp.max(jnp.maximum(jnp.maximum(now[0], now[1]), jnp.maximum(now[2], now[3])), -1, keepdims=True)
        acc = jnp.zeros((BLK, 128), F32)
        later = []
        for j in range(4):
            if n + 1 < len(units):
                later.append(score(units[n + 1], j))
            probs = jnp.exp(now[j] - peak).astype(BF)
            acc = acc + dot_nn(probs, va_s[head, tab[4 * i + j]])
        now = later
        rows = slice(i * BLK, (i + 1) * BLK)
        high, mid, small = split_three(-(peak + jnp.log(acc)))
        extra = jnp.where(place == 0, 1.0, 0.0).astype(BF)
        extra = jnp.where(place == 1, high, extra)
        extra = jnp.where(place == 2, mid, extra)
        extra = jnp.where(place == 3, small, extra)
        if head == 0:
            qe_ref[rows, :] = jnp.where(low, queries[i][0], extra)
            even = acc
        else:
            qo_ref[rows, :] = jnp.where(low, extra, queries[i][1])
            total = jnp.where(low, acc, even)
            value = jnp.where(low, even, acc)
            o_ref[rows, :] = (value / pltpu.roll(total, HDIM, 1)).astype(BF)


def attend_back_kernel(
    tab,
    qe_ref,
    qo_ref,
    k_ref,
    v_ref,
    do_ref,
    o_ref,
    xt_ref,
    dq_ref,
    dk_ref,
    dv_ref,
    keep_ref,
    give_ref,
    db_ref,
    ka_e,
    ka_o,
    vb_e,
    vb_o,
    extra_s,
    dk_s,
    dv_s,
    dkv_s,
):
    @pl.when(pl.program_id(0) == 0)
    def _():
        for b in range(8):
            extra_s[b] = key_extra(tab[12 + b])

    low = lane_ids(BLK) < HDIM
    place = lane_ids(BLK) % HDIM
    v_extra = jnp.where(place < 3, 1.0, 0.0).astype(BF)
    zero = jnp.zeros((BLK, 128), BF)
    for b in range(8):
        at = slice(b * BLK, (b + 1) * BLK)
        k = k_ref[at, :]
        v = v_ref[at, :]
        ka_e[b] = jnp.where(low, k, extra_s[b])
        ka_o[b] = jnp.where(low, extra_s[b], k)
        vb_e[b] = jnp.where(low, v, v_extra)
        vb_o[b] = jnp.where(low, v_extra, v)
    dk_s[...] = jnp.zeros(dk_s.shape, F32)
    dv_s[...] = jnp.zeros(dv_s.shape, F32)
    sides = ((ka_e, vb_e), (ka_o, vb_o))
    given = []
    for i in range(3):
        rows = slice(i * BLK, (i + 1) * BLK)
        d_out = do_ref[rows, :]
        product = d_out.astype(F32) * o_ref[rows, :].astype(F32)
        qas = (qe_ref[rows, :], qo_ref[rows, :])
        d_augs = []
        for head in range(2):
            mine = low if head == 0 else jnp.logical_not(low)
            delta = jnp.sum(jnp.where(mine, product, 0.0), -1, keepdims=True)
            high, mid, small = split_three(-delta)
            extra = jnp.where(place == 0, high, jnp.where(place == 1, mid, jnp.where(place == 2, small, zero)))
            d_augs.append(jnp.where(mine, d_out, extra))
        given.append((qas, d_augs, d_out.T, jnp.where(low, qas[0], qas[1]).T))

    def score(unit, j):
        i, head = unit
        b = tab[4 * i + j]
        qas, d_augs = given[i][:2]
        return dot_nt(qas[head], sides[head][0][b]), dot_nt(d_augs[head], sides[head][1][b])

    units = [(i, head) for i in range(3) for head in range(2)]
    now = [score(units[0], j) for j in range(4)]
    for n, (i, head) in enumerate(units):
        lanes = slice(head * HDIM, (head + 1) * HDIM)
        dot_t, qt = given[i][2:]
        dq = jnp.zeros((BLK, 128), F32)
        later = []
        for j in range(4):
            if n + 1 < len(units):
                later.append(score(units[n + 1], j))
            b = tab[4 * i + j]
            probs = jnp.exp(now[j][0])
            d_scores = (probs * now[j][1]).astype(BF)
            dv_s[b, lanes, :] += dot_nn(dot_t[lanes, :], probs.astype(BF))
            dk_s[b, lanes, :] += dot_nn(qt[lanes, :], d_scores)
            dq = dq + dot_nn(d_scores, k_ref[pl.ds(pl.multiple_of(b * BLK, BLK), BLK), :])
        now = later
        if head == 0:
            even = dq
        else:
            dq_ref[i * BLK : (i + 1) * BLK, :] = (jnp.where(low, even, dq) * 0.125).astype(BF)
    for b in range(8):
        dk = dk_s[b].T.astype(BF)
        dv = dv_s[b].T.astype(BF)
        dk_ref[b * BLK : (b + 1) * BLK, :] = dk
        dv_ref[b * BLK : (b + 1) * BLK, :] = dv
        dkv_s[b * BLK : (b + 1) * BLK, :128] = dk
        dkv_s[b * BLK : (b + 1) * BLK, 128:] = dv
    dq_all = dq_ref[...]
    db_ref[0:1, :] = jnp.sum(dq_all.astype(F32), 0, keepdims=True)
    db_ref[1:2, :] = jnp.sum(dkv_s[:, 128:].astype(F32), 0, keepdims=True)
    dw_q = dot_nn(xt_ref[:, :ROWS], dq_all).astype(BF)
    dw_kv = dot_nn(xt_ref[...], dkv_s[...]).astype(BF)
    for n, grad in enumerate((dw_q, dw_kv[:, :128], dw_kv[:, 128:])):
        grad = grad.reshape(RB // 2, 2, RP, 128)
        for pos in range(RB // 2):
            keep_ref[pos ^ tab[21], n] = jnp.where(tab[20] == 0, grad[pos, 0], grad[pos, 1])
            give_ref[pos ^ tab[21], n] = jnp.where(tab[20] == 0, grad[pos, 1], grad[pos, 0])


def gelu_both(pre):
    size = jnp.abs(pre)
    bell = jnp.exp(pre * pre * -0.5)
    t = 1.0 / (1.0 + size * (0.3275911 * math.sqrt(0.5)))
    poly = t * (
        0.5 * 0.254829592
        + t * (0.5 * -0.284496736 + t * (0.5 * 1.421413741 + t * (0.5 * -1.453152027 + t * (0.5 * 1.061405429))))
    )
    tail = poly * bell
    phi = jnp.where(pre >= 0, 1.0 - tail, tail)
    return pre * phi, phi + pre * bell * (1.0 / math.sqrt(2.0 * math.pi))


def norm_parts(summed):
    average = jnp.mean(summed, -1, keepdims=True)
    centered = summed - average
    variance = jnp.mean(centered * centered, -1, keepdims=True)
    root = lax.rsqrt(variance + LN_EPS)
    return centered * root, root


def norm_back(cot, gain, hat, root):
    gz = cot * gain
    return root * (gz - jnp.mean(gz, -1, keepdims=True) - hat * jnp.mean(gz * hat, -1, keepdims=True))


def feed_kernel(tab, o_ref, x_ref, *refs):
    pieces = refs[:8]
    vec_ref, w_ref, cot_ref, weight_ref, out_ref, dw_ref, dz1_ref, do_ref, sums_ref, db1_ref = refs[8:18]
    wo_s, h1b_s, h1t_s, hat1_s, root1_s, z2_s, u_s, gp_s, e2_s, e2t_s, ep_s = refs[18:]
    step = pl.program_id(0)
    blocks = [slice(i * HALF, (i + 1) * HALF) for i in range(2)]

    @pl.when(step == 0)
    def _():
        assemble(tab, pieces, 0, wo_s, 0)
        for rows in blocks:
            z1 = x_ref[rows, :].astype(F32) + dot_nt(o_ref[rows, :], wo_s[...]) + vec_ref[2:3, :]
            hat, root = norm_parts(z1)
            h1 = hat * vec_ref[3:4, :] + vec_ref[4:5, :]
            hat1_s[rows, :] = hat
            root1_s[rows, :] = root
            z2_s[rows, :] = h1 + vec_ref[5:6, :]
            h1b = h1.astype(BF)
            h1b_s[rows, :] = h1b
            h1t_s[:, rows] = h1b.T

    @pl.when(step < 4)
    def _():
        w1 = w_ref[:, 0, 0].reshape(D, D)
        w2t = w_ref[:, 0, 1].reshape(D, D)
        bias = vec_ref[pl.ds(8 + step, 1), :]
        now = dot_nn(h1b_s[:HALF, :], w1)
        for i, rows in enumerate(blocks):
            later = dot_nn(h1b_s[blocks[1], :], w1) if i == 0 else None
            act, slope = gelu_both(now + bias)
            act = act.astype(BF)
            u_s[step, rows, :] = act
            gp_s[step, rows, :] = slope.astype(BF)
            now = later
        z2_s[...] += dot_nt(u_s[step], w2t)

    @pl.when(step == 3)
    def _():
        sums = [jnp.zeros((1, D), F32) for _ in range(3)]
        for rows in blocks:
            hat, root = norm_parts(z2_s[rows, :])
            out_ref[rows, :] = (hat * vec_ref[6:7, :] + vec_ref[7:8, :]).astype(BF)
            cot = cot_ref[rows, :].astype(F32) * weight_ref[rows, :]
            dz2 = norm_back(cot, vec_ref[6:7, :], hat, root)
            z2_s[rows, :] = dz2
            e2 = dz2.astype(BF)
            e2_s[rows, :] = e2
            e2t_s[:, rows] = e2.T
            sums[0] += jnp.sum(dz2, 0, keepdims=True)
            sums[1] += jnp.sum(cot * hat, 0, keepdims=True)
            sums[2] += jnp.sum(cot, 0, keepdims=True)
        for n in range(3):
            sums_ref[3 + n : 4 + n, :] = sums[n]

    @pl.when(jnp.logical_and(step >= 4, step < 8))
    def _():
        m = step - 4
        w1 = w_ref[:, 0, 0].reshape(D, D)
        w2t = w_ref[:, 0, 1].reshape(D, D)
        db1 = jnp.zeros((1, D), F32)
        now = dot_nn(e2_s[:HALF, :], w2t)
        for i, rows in enumerate(blocks):
            later = dot_nn(e2_s[blocks[1], :], w2t) if i == 0 else None
            ep = (gp_s[m, rows, :].astype(F32) * now).astype(BF)
            ep_s[rows, :] = ep
            db1 += jnp.sum(ep.astype(F32), 0, keepdims=True)
            z2_s[rows, :] += dot_nt(ep, w1)
            now = later
        db1_ref[pl.ds(m, 1), :] = db1
        dw_ref[:, :RP] = dot_nn(h1t_s[...], ep_s[...]).astype(BF).reshape(RB, RP, D)
        dw_ref[:, RP:] = dot_nn(e2t_s[...], u_s[m]).astype(BF).reshape(RB, RP, D)

    @pl.when(step == 8)
    def _():
        sums = [jnp.zeros((1, D), F32) for _ in range(3)]
        for rows in blocks:
            dh = z2_s[rows, :]
            hat = hat1_s[rows, :]
            dz1 = norm_back(dh, vec_ref[3:4, :], hat, root1_s[rows, :])
            dz1_ref[rows, :] = dz1
            e1 = dz1.astype(BF)
            e2t_s[:, rows] = e1.T
            do_ref[rows, :] = dot_nn(e1, wo_s[...]).astype(BF)
            sums[0] += jnp.sum(dz1, 0, keepdims=True)
            sums[1] += jnp.sum(dh * hat, 0, keepdims=True)
            sums[2] += jnp.sum(dh, 0, keepdims=True)
        for n in range(3):
            sums_ref[n : n + 1, :] = sums[n]
        dw_ref[:, :RP] = dot_nn(e2t_s[...], o_ref[...]).astype(BF).reshape(RB, RP, D)
        dw_ref[:, RP:] = jnp.zeros((RB, RP, D), BF)


def pack_kernel(tab, own_ref, *rest):
    others, out_ref, line_s = rest[:-2], rest[-2], rest[-1]
    line_s[0] = own_ref[...]
    for n, ref in enumerate(others):
        line_s[n + 1] = ref[...]
    width = own_ref.shape[-1] // 4
    for m in range(4):
        shard = line_s[m ^ tab[0]]
        for n in range(4):
            out_ref[n, :, m * width : (m + 1) * width] = shard[:, n * width : (n + 1) * width]


def input_rest_kernel(tab, dk_ref, dv_ref, *refs):
    pieces, (nb_ref, mid_ref, w_s) = refs[:8], refs[8:]
    step = pl.program_id(0)

    @pl.when(step == 0)
    def _():
        for part in range(2):
            assemble(tab, pieces, part + 1, w_s, D * part)

    back = (dot_nt(dk_ref[...], w_s[:, :D]) + dot_nt(dv_ref[...], w_s[:, D:])).astype(BF)

    @pl.when(step < 3)
    def _():
        nb_ref[...] = back

    @pl.when(step >= 3)
    def _():
        mid_ref[...] = back


def input_own_kernel(tab, dq_ref, dk_ref, dv_ref, *refs):
    pieces, (dz1_ref, own_ref, w_s) = refs[:8], refs[8:]

    @pl.when(pl.program_id(0) == 0)
    def _():
        for part in range(3):
            assemble(tab, pieces, part, w_s, D * part)

    back = dot_nt(dk_ref[...], w_s[:, D : 2 * D]) + dot_nt(dv_ref[...], w_s[:, 2 * D :])
    own_ref[...] = back + dot_nt(dq_ref[...], w_s[:, :D]) + dz1_ref[...]


def head_line_kernel(z_ref, own_ref, *refs):
    others, outs = refs[:-4], refs[-4:]
    total = own_ref[...].astype(F32)
    for ref in others:
        total = total + ref[...].astype(F32)
    total = total.astype(BF)
    width = D // 4
    for m in range(4):
        at = slice(m * width, (m + 1) * width)
        mine = jnp.concatenate([total[kind, :, at] for kind in range(3)], 1)
        for n, ref in enumerate(outs):

            @pl.when((m ^ z_ref[0]) == n)
            def _():
                ref[...] = mine


def feed_line_kernel(z_ref, feed_ref, *outs):
    width = D // 4
    rows = outs[0].shape[0]
    for m in range(4):
        for n, ref in enumerate(outs):

            @pl.when((m ^ z_ref[0]) == n)
            def _():
                ref[:, :D] = feed_ref[2 * m * rows : (2 * m + 1) * rows, :]
                ref[:, D : 2 * D] = feed_ref[(2 * m + 1) * rows : (2 * m + 2) * rows, :]
                ref[:, 2 * D :] = feed_ref[8 * rows : 9 * rows, m * width : (m + 1) * width]


def call(kernel, grid, in_specs, out_specs, out_shape, scratch, flops, bytes_accessed, name):
    return pl.pallas_call(
        kernel,
        grid_spec=pltpu.PrefetchScalarGridSpec(
            num_scalar_prefetch=1, grid=(grid,), in_specs=in_specs, out_specs=out_specs, scratch_shapes=scratch
        ),
        out_shape=out_shape,
        compiler_params=pltpu.CompilerParams(
            dimension_semantics=("arbitrary",), vmem_limit_bytes=VMEM_LIMIT
        ),
        cost_estimate=pl.CostEstimate(flops=flops, bytes_accessed=bytes_accessed, transcendentals=0),
        name=name,
    )


def whole(*shape):
    return pl.BlockSpec(shape, lambda s, t: (0,) * len(shape))


def columns(rows, width=128):
    return pl.BlockSpec((rows, width), lambda s, t: (0, s))


def shape_of(shape, dtype):
    return jax.ShapeDtypeStruct(shape, dtype)


def vm(shape, dtype):
    return pltpu.VMEM(shape, dtype)


def attend(tab, own, nb, mid, pieces, vectors):
    w_spec = pl.BlockSpec((3, RP, 128), lambda s, t: (0, 0, s))
    return call(
        attend_kernel,
        PAIRS,
        [whole(ROWS, D), whole(ROWS, D), whole(2 * BLK, D)] + [w_spec] * 8 + [columns(12)],
        [columns(ROWS), columns(ROWS), columns(ROWS), columns(8 * BLK), columns(8 * BLK)]
        + [pl.BlockSpec((128, 8 * BLK), lambda s, t: (s, 0))],
        [shape_of((ROWS, D), BF)] * 3 + [shape_of((8 * BLK, D), BF)] * 2 + [shape_of((D, 8 * BLK), BF)],
        [vm((D, 384), BF)] + [vm((8, BLK, 128), BF)] * 2 + [vm((2, 8, BLK, 128), BF), vm((8, BLK, 128), BF)],
        5_000_000_000,
        16_000_000,
        "attend",
    )(tab, own, nb, mid, *pieces, vectors)


def attend_back(tab, qe, qo, k, v, d_out, o, xt):
    return call(
        attend_back_kernel,
        PAIRS,
        [columns(ROWS), columns(ROWS), columns(8 * BLK), columns(8 * BLK), columns(ROWS), columns(ROWS), whole(D, 8 * BLK)],
        [
            columns(ROWS),
            columns(8 * BLK),
            columns(8 * BLK),
            pl.BlockSpec((RB // 2, 3, RP, 128), lambda s, t: (0, 0, 0, s)),
            pl.BlockSpec((RB // 2, 3, RP, 128), lambda s, t: (0, 0, 0, s)),
            columns(2),
        ],
        [
            shape_of((ROWS, D), BF),
            shape_of((8 * BLK, D), BF),
            shape_of((8 * BLK, D), BF),
            shape_of((RB // 2, 3, RP, D), BF),
            shape_of((RB // 2, 3, RP, D), BF),
            shape_of((2, D), F32),
        ],
        [vm((8, BLK, 128), BF)] * 5
        + [vm((8, 128, BLK), F32)] * 2
        + [vm((8 * BLK, BLK), BF)],
        50_000_000_000,
        24_000_000,
        "attend_back",
    )(tab, qe, qo, k, v, d_out, o, xt)


def feed(tab, o, x, pieces, vectors, w, cot, weight):
    wo_spec = pl.BlockSpec((1, RP, D), lambda s, t: (3, 0, 0))

    def group(s):
        return jnp.where(s < 4, s, jnp.minimum(s - 4, 3))

    return call(
        feed_kernel,
        9,
        [
            whole(ROWS, D),
            whole(ROWS, D),
            *[wo_spec] * 8,
            whole(12, D),
            pl.BlockSpec((RB, 1, 2, RP, D), lambda s, t: (0, group(s), 0, 0, 0)),
            whole(ROWS, D),
            whole(ROWS, 1),
        ],
        [
            whole(ROWS, D),
            pl.BlockSpec((RB, 2 * RP, D), lambda s, t: (0, jnp.maximum(s - 4, 0), 0)),
            whole(ROWS, D),
            whole(ROWS, D),
            whole(6, D),
            whole(4, D),
        ],
        [
            shape_of((ROWS, D), BF),
            shape_of((RB, 10 * RP, D), BF),
            shape_of((ROWS, D), F32),
            shape_of((ROWS, D), BF),
            shape_of((6, D), F32),
            shape_of((4, D), F32),
        ],
        [
            vm((D, D), BF),
            vm((ROWS, D), BF),
            vm((D, ROWS), BF),
            vm((ROWS, D), F32),
            vm((ROWS, 1), F32),
            vm((ROWS, D), F32),
            vm((4, ROWS, D), BF),
            vm((4, ROWS, D), BF),
            vm((ROWS, D), BF),
            vm((D, ROWS), BF),
            vm((ROWS, D), BF),
        ],
        40_000_000_000,
        48_000_000,
        "feed",
    )(tab, o, x, *pieces, vectors, w, cot, weight)


def round_kernel(qkv_ref, proj_ref, up_ref, down_ref, mine_ref, feed_ref):
    width = qkv_ref.shape[-1]
    for n in range(3):
        mine_ref[:, n * width : (n + 1) * width] = qkv_ref[n].astype(BF)
    mine_ref[:, 3 * width :] = proj_ref[...].T.astype(BF)
    feed_ref[0] = up_ref[...].astype(BF)
    feed_ref[1] = down_ref[...].astype(BF)


def round_shards(qkv, proj, up, down):
    rows = up.shape[0]
    return pl.pallas_call(
        round_kernel,
        in_specs=[pl.BlockSpec(memory_space=pltpu.VMEM)] * 4,
        out_specs=[pl.BlockSpec(memory_space=pltpu.VMEM)] * 2,
        out_shape=[shape_of((rows, D), BF), shape_of((2, rows, D), BF)],
        cost_estimate=pl.CostEstimate(flops=1_000_000, bytes_accessed=1_500_000, transcendentals=0),
        name="round_shards",
    )(qkv, proj, up, down)


def pack_line(z, own, others):
    rows, width = own.shape
    return call(
        pack_kernel,
        1,
        [whole(rows, width)] * 4,
        whole(4, rows, D),
        shape_of((4, rows, D), BF),
        [vm((4, rows, width), BF)],
        60_000_000_000,
        1_000_000,
        "pack_line",
    )(z.reshape(1).astype(jnp.int32), own, *others)


def input_rest(tab, dk, dv, pieces):
    w_spec = whole(3, RP, D)
    each = pl.BlockSpec((BLK, D), lambda s, t: (s + 3, 0))
    return call(
        input_rest_kernel,
        5,
        [each, each] + [w_spec] * 8,
        [
            pl.BlockSpec((BLK, D), lambda s, t: (jnp.minimum(s, 2), 0)),
            pl.BlockSpec((BLK, D), lambda s, t: (jnp.maximum(s - 3, 0), 0)),
        ],
        [shape_of((3 * BLK, D), BF), shape_of((2 * BLK, D), BF)],
        [vm((D, 2 * D), BF)],
        8_000_000_000,
        12_000_000,
        "input_rest",
    )(tab, dk, dv, *pieces)


def input_own(tab, dq, dk, dv, pieces, dz1):
    w_spec = whole(3, RP, D)
    each = pl.BlockSpec((BLK, D), lambda s, t: (s, 0))
    return call(
        input_own_kernel,
        3,
        [each, each, each] + [w_spec] * 8 + [each],
        each,
        shape_of((ROWS, D), F32),
        [vm((D, 3 * D), BF)],
        5_000_000_000,
        12_000_000,
        "input_own",
    )(tab, dq, dk, dv, *pieces, dz1)


def in_line(kernel, name, rows, width, z, *parts):
    return pl.pallas_call(
        kernel,
        in_specs=[pl.BlockSpec(memory_space=pltpu.SMEM)] + [pl.BlockSpec(memory_space=pltpu.VMEM)] * len(parts),
        out_specs=[pl.BlockSpec(memory_space=pltpu.VMEM)] * 4,
        out_shape=[shape_of((rows, width), BF)] * 4,
        compiler_params=pltpu.CompilerParams(vmem_limit_bytes=VMEM_LIMIT),
        cost_estimate=pl.CostEstimate(flops=2_000_000, bytes_accessed=4_000_000, transcendentals=0),
        name=name,
    )(z.reshape(1).astype(jnp.int32), *parts)


def adamw(weight, clipped, first, second, rate, decay):
    first_new = BETA_ONE * first + (1.0 - BETA_ONE) * clipped
    second_new = BETA_TWO * second + (1.0 - BETA_TWO) * clipped * clipped
    first_hat = first_new / (1.0 - BETA_ONE**STEP)
    second_hat = second_new / (1.0 - BETA_TWO**STEP)
    updated = weight * (1.0 - rate * decay) - rate * first_hat / (jnp.sqrt(second_hat) + ADAM_EPS)
    return (clipped, first_new, second_new, updated)


def update_kernel(squares_ref, head_ref, feed_ref, vec_ref, *refs):
    ins, norm_ref, outs = refs[:15], refs[15], refs[16:]
    norm = jnp.sqrt(jnp.sum(squares_ref[...], keepdims=True))
    norm_ref[...] = norm
    clip = jnp.minimum(1.0, CLIP_NORM / (norm + 1e-06))
    head = head_ref[...]
    fed = feed_ref[...]
    width = D // 4
    grads = (
        [head[:, n * width : (n + 1) * width] for n in range(3)],
        [fed[:, 2 * D :].T],
        [fed[:, :D]],
        [fed[:, D : 2 * D]],
        [vec_ref[...]],
    )
    for kind, parts in enumerate(grads):
        rate, decay = (VECTOR_RATE, 0.0) if kind == 4 else (MATRIX_RATE / math.sqrt(D), WEIGHT_DECAY)
        for n, grad in enumerate(parts):
            at = n if kind == 0 else Ellipsis
            results = adamw(ins[kind][at], grad * clip, ins[5 + kind][at], ins[10 + kind][at], rate, decay)
            for m, result in enumerate(results):
                outs[4 * kind + m][at] = result


def update(squares, sums, vec, weights, firsts, seconds):
    vmem = pl.BlockSpec(memory_space=pltpu.VMEM)
    return pl.pallas_call(
        update_kernel,
        in_specs=[vmem] * 19,
        out_specs=[vmem] * 21,
        out_shape=[shape_of((1, 1), F32)] + [shape_of(one.shape, F32) for one in weights for _ in range(4)],
        compiler_params=pltpu.CompilerParams(vmem_limit_bytes=VMEM_LIMIT),
        cost_estimate=pl.CostEstimate(flops=10_000_000, bytes_accessed=8_000_000, transcendentals=0),
        name="update",
    )(squares, *sums, vec, *weights, *firsts, *seconds)


def total_kernel(vec_ref, *refs):
    vec = jnp.sum(vec_ref[...], 0, keepdims=True)
    refs[10][...] = vec
    square = jnp.sum(vec * vec, keepdims=True)
    for n in range(2):
        sums = refs[4 * n][...].astype(F32)
        for ref in refs[4 * n + 1 : 4 * n + 4]:
            sums = sums + ref[...].astype(F32)
        refs[8 + n][...] = sums
        square = square + jnp.sum(sums * sums, keepdims=True)
    refs[11][...] = jnp.broadcast_to(square, refs[11].shape)


def total(vec, groups, devices):
    vmem = pl.BlockSpec(memory_space=pltpu.VMEM)
    *sums, vec_sum, square = pl.pallas_call(
        total_kernel,
        in_specs=[vmem] * 9,
        out_specs=[vmem] * 4,
        out_shape=[shape_of(group[0].shape, F32) for group in groups]
        + [shape_of((1, vec.shape[1]), F32), shape_of((devices, 1), F32)],
        compiler_params=pltpu.CompilerParams(vmem_limit_bytes=VMEM_LIMIT),
        cost_estimate=pl.CostEstimate(flops=2_000_000, bytes_accessed=4_000_000, transcendentals=0),
        name="total",
    )(vec, *[one for group in groups for one in group])
    return sums, vec_sum, square


def shards(
    tokens,
    out_cotangent,
    lengths,
    starts,
    ends,
    flags,
    qkv_master,
    proj_master,
    up_master,
    down_master,
    vectors,
    qkv_first,
    proj_first,
    up_first,
    down_first,
    qkv_second,
    proj_second,
    up_second,
    down_second,
    vector_first,
    vector_second,
):
    mp_count = lax.axis_size("mp")
    dp_count = lax.axis_size("dp")
    devices = mp_count * dp_count
    z = lax.axis_index("mp")
    dp_index = lax.axis_index("dp")
    core = dp_index % 2
    chips = dp_count // 2
    part = D // dp_count
    head_cols = D // mp_count

    def linear(chip, core_of, z_of):
        return (chip * 2 + core_of) * mp_count + z_of

    def permutation(move):
        return [
            (linear(chip, c, k), linear(*move(chip, c, k)))
            for chip in range(chips)
            for c in range(2)
            for k in range(mp_count)
        ]

    planes = [[linear(chip, c, k) for chip in range(chips)] for c in range(2) for k in range(mp_count)]
    swap_core = permutation(lambda chip, c, k: (chip, 1 - c, k))
    swap_z = [permutation(lambda chip, c, k, n=n: (chip, c, k ^ n)) for n in range(mp_count)]
    swap_chip = [permutation(lambda chip, c, k, n=n: (chip ^ n, c, k)) for n in range(chips)]
    middle = (0, 2, 1, 3)
    swap_mid = permutation(lambda chip, c, k: (chip, c, middle[k]))
    chip_index = dp_index // 2

    def over_plane(value):
        return lax.all_to_all(value, AXES, 0, 0, tiled=True, axis_index_groups=planes)

    def over_z(value):
        return lax.all_to_all(value, "mp", 0, 0, tiled=True)

    def absolute(same, other):
        order = jnp.arange(chips, dtype=jnp.int32) ^ chip_index
        same, other = jnp.stack(same)[order], jnp.stack(other)[order]
        both = jnp.where(core == 0, jnp.stack([same, other], 1), jnp.stack([other, same], 1))
        kinds = both.shape[2]
        both = both.transpose(2, 0, 1, 3, 4).reshape(kinds, RB // 2, 2, RP, D).transpose(1, 2, 0, 3, 4)
        return [both[n, half] for half in range(2) for n in range(RB // 2)]

    mine, feed_mine = round_shards(qkv_master, proj_master, up_master, down_master.T)
    feed_w = lax.all_gather(feed_mine, AXES, axis=0, tiled=False).reshape(dp_count, mp_count, 2, part, D)
    line = [lax.ppermute(mine, AXES, swap_z[n]) for n in range(1, mp_count)]
    tokens_late, mine, *line = lax.optimization_barrier((tokens, mine, *line))
    along_z = pack_line(z, mine, line)
    mid_at = jnp.where(z == 1, BLK, 0)
    nb = lax.ppermute(tokens_late, AXES, swap_z[1])
    mid = lax.ppermute(lax.dynamic_slice_in_dim(tokens_late, mid_at, 2 * BLK, 0), AXES, swap_mid)
    same = [along_z] + [lax.ppermute(along_z, AXES, swap_chip[n]) for n in range(1, chips)]
    first, same[1], nb = lax.optimization_barrier((along_z, same[1], nb))
    other = [lax.ppermute(one, AXES, swap_core) for one in [first] + same[1:]]
    pieces = same + other
    kernel_core, kernel_chip = core, chip_index
    if part != RP:
        pieces = absolute(same, other)
        feed_w = feed_w.transpose(1, 2, 0, 3, 4).reshape(mp_count, 2, RB, RP, D).transpose(2, 0, 1, 3, 4)
        kernel_core = kernel_chip = jnp.zeros((), jnp.int32)

    place = jnp.asarray(BLOCK_PLACE)[z]
    counts = jnp.clip(lengths[jnp.asarray(BLOCK_SEQ)[z]] - BLK * place, 0, BLK)
    tab = jnp.concatenate(
        [jnp.asarray(KEY_BLOCKS)[z].reshape(12), counts, kernel_core.reshape(1), kernel_chip.reshape(1)]
    ).astype(jnp.int32)

    positions = z * ROWS + jnp.arange(ROWS, dtype=jnp.int32)
    seq_of = positions // LEN
    within = positions % LEN
    picker = (seq_of[:, None] == jnp.arange(lengths.shape[0], dtype=jnp.int32)[None, :]).astype(jnp.int32)
    length_row = jnp.sum(picker * lengths[None, :], 1)
    start_row = jnp.sum(picker * starts[None, :], 1)
    end_row = jnp.sum(picker * ends[None, :], 1)
    flag_row = jnp.sum(picker * flags[None, :], 1).astype(F32)
    valid_row = (within < length_row).astype(F32)
    answer = (within == start_row).astype(F32) + (within == end_row).astype(F32)
    opening = (within == 0).astype(F32)
    row_weight = valid_row * (1.0 + 2.0 * (1.0 - flag_row) * answer + 4.0 * flag_row * opening)

    o, qe, qo, k, v, xt = attend(tab, tokens, nb, mid, pieces, vectors)
    block_out, feed_dw, dz1, d_o, sums_norm, bias_up_grad = feed(
        tab, o, tokens, pieces, vectors, feed_w, out_cotangent, row_weight[:, None]
    )

    def to_parts(grad):
        if part == RP:
            return grad
        lead = grad.shape[1:-2]
        moved = jnp.moveaxis(grad, 0, -3).reshape(*lead, dp_count, part, D)
        return jnp.moveaxis(moved, -3, 0)

    if part != RP:
        feed_dw = to_parts(feed_dw.reshape(RB, 10, RP, D)).reshape(dp_count, 10 * part, D)
    feed_part = lax.psum_scatter(feed_dw, "dp", scatter_dimension=0, tiled=False)

    dq, dk, dv, keep, give, sums_head = attend_back(tab, qe, qo, k, v, d_o, o, xt)
    if part != RP:
        both = jnp.stack([keep, give], 1).reshape(RB, 3, RP, D)
        both = to_parts(both).reshape(chips, 2, 3, part, D)
        order = jnp.arange(chips, dtype=jnp.int32) ^ chip_index
        keep = lax.dynamic_index_in_dim(both, core, 1, keepdims=False)[order]
        give = lax.dynamic_index_in_dim(both, 1 - core, 1, keepdims=False)[order]
    got = lax.ppermute(give, AXES, swap_core)
    chip_sum = (keep.astype(F32) + got.astype(F32)).astype(BF)
    to_nb, to_mid = input_rest(tab, dk, dv, pieces)
    chip_sum, dq, dk, dv, sums_head, to_nb, to_mid = lax.optimization_barrier(
        (chip_sum, dq, dk, dv, sums_head, to_nb, to_mid)
    )
    from_chips = [lax.ppermute(chip_sum[n], AXES, swap_chip[n]) for n in range(1, chips)]
    from_nb = lax.ppermute(to_nb, AXES, swap_z[1])
    from_mid = lax.ppermute(to_mid, AXES, swap_mid)
    dx_own = input_own(tab, dq, dk, dv, pieces, dz1)
    vector_part = jnp.concatenate([sums_head, sums_norm, bias_up_grad], 0)
    vec_columns = D // devices
    vector_part = vector_part.reshape(12, devices, vec_columns).transpose(1, 0, 2).reshape(devices, 12 * vec_columns)
    vector_parts = lax.all_to_all(vector_part, AXES, 0, 0, tiled=True)
    vector_parts, dx_own, from_nb, from_mid, *from_chips = lax.optimization_barrier(
        (vector_parts, dx_own, from_nb, from_mid, *from_chips)
    )

    def along_line(parts):
        return [parts[0]] + [lax.ppermute(parts[n], AXES, swap_z[n]) for n in range(1, mp_count)]

    head_line = along_line(in_line(head_line_kernel, "head_line", part, 3 * D // 4, z, chip_sum[0], *from_chips))
    feed_part, *head_line = lax.optimization_barrier((feed_part, *head_line))
    feed_line = along_line(in_line(feed_line_kernel, "feed_line", part, 2 * D + D // 4, z, feed_part))
    zero_block = jnp.zeros((BLK, D), BF)
    from_mid = jnp.where(
        z == 1, jnp.concatenate([zero_block, from_mid], 0), jnp.concatenate([from_mid, zero_block], 0)
    )
    input_grad = dx_own + from_nb.astype(F32) + from_mid.astype(F32)

    sums, vector_grad, square = total(vector_parts, (head_line, feed_line), devices)
    vector_grad = vector_grad.reshape(12, vec_columns)
    squares = lax.all_to_all(square, AXES, 0, 0, tiled=True)
    vec_index = dp_index * mp_count + z
    vector_shard = lax.dynamic_slice_in_dim(vectors, vec_index * vec_columns, vec_columns, 1)
    grad_norm, *results = update(
        squares,
        sums,
        vector_grad,
        (qkv_master, proj_master, up_master, down_master.T, vector_shard),
        (qkv_first, proj_first, up_first, down_first.T, vector_first),
        (qkv_second, proj_second, up_second, down_second.T, vector_second),
    )
    down_set = [one.T for one in results[12:16]]
    return (block_out, input_grad, grad_norm.reshape(()), *results[:12], *down_set, *results[16:])


def solution(mesh):
    rows = P(AXES, None)
    group = P("dp")
    qkv = P(None, "dp", "mp")
    proj = P("mp", "dp")
    up = P("dp", "mp")
    vec = P(None, AXES)
    return jax.shard_map(
        shards,
        mesh=mesh,
        in_specs=(rows, rows, group, group, group, group)
        + (qkv, proj, up, proj, P())
        + (qkv, proj, up, proj) * 2
        + (vec, vec),
        out_specs=(rows, rows, P()) + (qkv,) * 4 + (proj,) * 4 + (up,) * 4 + (proj,) * 4 + (vec,) * 4,
        check_vma=False,
    )
```
